256 devices in a mesh: tile: 64 (over z, x, y_hi), head: 4 (over y_lo, core).
Axes of the slice: x: 4, y: 4 (y_hi: 2, y_lo: 2; y = y_hi * 2 + y_lo), z: 8, core: 2. Of those that a mesh axis runs over, the one named last changes fastest.
Arguments:
- queries: bfloat16 [10240, 3072], P('tile', 'head'), as said below
- keys: bfloat16 [10240, 3072], P('tile', 'head'), as said below
- values: bfloat16 [10240, 3072], P('tile', 'head'), may hold values from -5 to 5
- w_out: bfloat16 [3072, 3072], P(None, 'head'), may hold values from -0.109375 to 0.109375
- out_grad: bfloat16 [10240, 3072], P('tile', 'head'), may hold values from -5 to 5
- tile_valid: int32 [64], replicated, may hold values 0 or 1
Outputs:
- mixed: bfloat16 [10240, 3072], P('tile', 'head')
- query_grad: bfloat16 [10240, 3072], P('tile', 'head')
- key_grad: bfloat16 [10240, 3072], P('tile', 'head')
- value_grad: bfloat16 [10240, 3072], P('tile', 'head')
The draws below stay inside these ranges and needn't reach their ends.
Inputs may be any that keep to these rules, and one draw needn't show every extreme that they name: `queries`: entries lie within -5 to 5. `keys`: entries lie within -5 to 5.
All inputs are finite; a program needn't handle non-finite values.
Results may differ from the reference program's by a relative error of at most 0.012.
Values may be sent and summed in bfloat16 or wider, within the bound.
A program may use at most 64 MiB of HBM per device.

```python
import jax
import jax.numpy as jnp
from jax import lax

D = 3072
HEADS = 24
HD = 128
GT = 4
TF = 2
TH = 1
W = 80
TOKENS = 10240
FEAT = 3072
N_TILE = 64


def draw_queries(key, part):
    key = jax.random.fold_in(key, 1)
    normal_part = jnp.clip(jax.random.normal(key, (TOKENS, HEADS * HD), jnp.float32), -5.0, 5.0)
    return normal_part.astype(jnp.bfloat16)


def draw_keys(key, part):
    key = jax.random.fold_in(key, 2)
    normal_part = jnp.clip(jax.random.normal(key, (TOKENS, HEADS * HD), jnp.float32), -5.0, 5.0)
    return normal_part.astype(jnp.bfloat16)


def touch_ends(result, stream_key, low, high):
    extent = result.shape
    spot = [jax.random.randint(jax.random.fold_in(stream_key, axis), (), 0, extent[axis]) for axis in range(len(extent))]
    result = result.at[tuple(spot)].set(low)
    longest = extent.index(max(extent))
    spot[longest] = (spot[longest] + 1) % extent[longest]
    return result.at[tuple(spot)].set(high)


def steps_of(stream_key, dims, pieces, least, high):
    level, own = 1.0, jax.random.fold_in(stream_key, 6)
    for dim, parts in pieces:
        draws = jnp.exp(jax.random.uniform(jax.random.fold_in(own, dim), (parts,), jnp.float32, least / len(pieces), high / len(pieces)))
        level = level * jnp.repeat(draws, dims[dim] // parts).reshape([-1 if axis == dim else 1 for axis in range(len(dims))])
    return level


def scatter_about(key, extent, deviation, limit, pieces=(), kind=jnp.bfloat16):
    entries = jax.random.normal(key, extent, jnp.float32) * deviation
    if len(pieces) > 0:
        entries = steps_of(key, extent, pieces, -0.22, 0.18) * entries
    return jnp.clip(entries, min=-limit, max=limit).astype(kind)


def setup_inputs(seed: int = 0) -> dict:
    key_of = jax.random.split(jax.random.key(seed), 7)
    queries = draw_queries(jax.random.fold_in(key_of[6], 71), 0)
    keys = draw_keys(jax.random.fold_in(key_of[6], 71), 0)
    values = scatter_about(key_of[2], (TOKENS, FEAT), 1.0, 5.0, ((0, 64), (1, 4)))
    w_out = scatter_about(key_of[3], (D, FEAT), FEAT ** -0.5, 0.109375, ((1, 4),))
    out_grad = scatter_about(key_of[4], (TOKENS, D), 1.0, 5.0, ((0, 64), (1, 4)))
    tile_valid = touch_ends((jax.random.randint(key_of[5], (N_TILE,), 0, 2) < 1).astype(jnp.int32), jax.random.fold_in(key_of[5], 1), 0, 1)
    return {"queries": queries, "keys": keys, "values": values, "w_out": w_out, "out_grad": out_grad, "tile_valid": tile_valid}


def window_mask(tile_time, tile_height, grid_height, tile_valid):
    tile_tokens = TF * TH * W
    blocks = []
    for step_time in (-1, 0, 1):
        for step_row in (-1, 0, 1):
            near_time = tile_time + step_time
            near_height = tile_height + step_row
            inside = (near_time >= 0) & (near_time < GT) & (near_height >= 0) & (near_height < grid_height)
            tile_id = jnp.clip(near_time * grid_height + near_height, 0, GT * grid_height - 1).astype(jnp.int32)
            usable = inside & ((tile_valid[tile_id] > 0) | (step_time == 0 and step_row == 0))
            blocks.append(jnp.broadcast_to(usable, (tile_tokens, tile_tokens)))
    return jnp.concatenate(blocks, axis=1)


def tile_attention(query_tile, near_keys, near_values, grad_tile, allowed):
    query_count = query_tile.shape[0]
    key_count = near_keys.shape[0]
    head_count = query_tile.shape[1] // HD
    score_scale = HD ** -0.5
    query_heads = query_tile.reshape(query_count, head_count, HD).astype(jnp.float32)
    key_heads = near_keys.reshape(key_count, head_count, HD).astype(jnp.float32)
    value_heads = near_values.reshape(key_count, head_count, HD).astype(jnp.float32)
    grad_heads = grad_tile.reshape(query_count, head_count, HD).astype(jnp.float32)
    scores = jnp.einsum('qhd,khd->hqk', query_heads, key_heads) * score_scale
    scores = jnp.where(allowed[None], scores, -jnp.inf)
    largest = jnp.max(scores, axis=2, keepdims=True)
    exponent = jnp.exp(scores - largest)
    weights = (exponent / jnp.sum(exponent, axis=2, keepdims=True)).astype(jnp.bfloat16)
    weights_wide = weights.astype(jnp.float32)
    attended = jnp.einsum('hqk,khd->qhd', weights_wide, value_heads).astype(jnp.bfloat16)
    row_dot = jnp.sum(grad_heads * attended.astype(jnp.float32), axis=2)
    weight_grad = jnp.einsum('qhd,khd->hqk', grad_heads, value_heads)
    score_grad = (weights_wide * (weight_grad - row_dot.T[:, :, None]) * score_scale).astype(jnp.bfloat16)
    score_wide = score_grad.astype(jnp.float32)
    query_part = jnp.einsum('hqk,khd->qhd', score_wide, key_heads).astype(jnp.bfloat16)
    key_part = jnp.einsum('hqk,qhd->khd', score_wide, query_heads)
    value_part = jnp.einsum('hqk,qhd->khd', weights_wide, grad_heads)
    return (attended.reshape(query_count, head_count * HD), query_part.reshape(query_count, head_count * HD),
            key_part.reshape(key_count, head_count * HD), value_part.reshape(key_count, head_count * HD))


def reference(queries, keys, values, w_out, out_grad, tile_valid):
    grid_height = N_TILE // GT
    tile_tokens = TF * TH * W
    feature_count = HEADS * HD
    attn_grad = jnp.dot(out_grad, w_out, preferred_element_type=jnp.float32).astype(jnp.bfloat16)
    grid_shape = (GT, grid_height, tile_tokens, feature_count)
    padding = ((1, 1), (1, 1), (0, 0), (0, 0))
    key_grid = jnp.pad(keys.reshape(grid_shape), padding)
    value_grid = jnp.pad(values.reshape(grid_shape), padding)
    query_tiles = queries.reshape(N_TILE, tile_tokens, feature_count)
    grad_tiles = attn_grad.reshape(N_TILE, tile_tokens, feature_count)
    zero_index = jnp.zeros((), jnp.int32)
    window_shape = (3, 3, tile_tokens, feature_count)

    def visit(carry, tile_index):
        key_total, value_total = carry
        tile_time = (tile_index // grid_height).astype(jnp.int32)
        tile_height = (tile_index % grid_height).astype(jnp.int32)
        corner = (tile_time, tile_height, zero_index, zero_index)
        near_keys = lax.dynamic_slice(key_grid, corner, window_shape).reshape(9 * tile_tokens, feature_count)
        near_values = lax.dynamic_slice(value_grid, corner, window_shape).reshape(9 * tile_tokens, feature_count)
        allowed = window_mask(tile_time, tile_height, grid_height, tile_valid)
        attended, query_part, key_part, value_part = tile_attention(
            query_tiles[tile_index], near_keys, near_values, grad_tiles[tile_index], allowed)
        key_total = lax.dynamic_update_slice(
            key_total, lax.dynamic_slice(key_total, corner, window_shape) + key_part.reshape(window_shape), corner)
        value_total = lax.dynamic_update_slice(
            value_total, lax.dynamic_slice(value_total, corner, window_shape) + value_part.reshape(window_shape), corner)
        return (key_total, value_total), (attended, query_part)

    empty_grid = jnp.zeros((GT + 2, grid_height + 2, tile_tokens, feature_count), jnp.float32)
    (key_total, value_total), (attended, query_grad) = lax.scan(
        visit, (empty_grid, empty_grid), jnp.arange(N_TILE, dtype=jnp.int32))
    key_grad = key_total[1:-1, 1:-1].reshape(N_TILE * tile_tokens, feature_count).astype(jnp.bfloat16)
    value_grad = value_total[1:-1, 1:-1].reshape(N_TILE * tile_tokens, feature_count).astype(jnp.bfloat16)
    attended = attended.reshape(N_TILE * tile_tokens, feature_count)
    mixed = jnp.dot(attended, w_out.T, preferred_element_type=jnp.float32).astype(jnp.bfloat16)
    return mixed, query_grad.reshape(N_TILE * tile_tokens, feature_count), key_grad, value_grad
```

```python
import jax
import jax.numpy as jnp
from jax import lax
from jax.experimental import pallas as pl
from jax.experimental.pallas import tpu as pltpu
from jax.sharding import PartitionSpec as P

HD = 128
GT = 4
GH = 16
T = 160
NH = 3
HALF = NH * HD
FULL = 2 * HALF
WIN = 9 * T
SIDE = 3 * T
MESH = pl.DeviceIdType.MESH
BF = jnp.bfloat16
F32 = jnp.float32


def nt(a, b):
    return lax.dot_general(a, b, (((1,), (1,)), ((), ())), preferred_element_type=F32)


def nn(a, b):
    return lax.dot_general(a, b, (((1,), (0,)), ((), ())), preferred_element_type=F32)


def tn(a, b):
    return lax.dot_general(a, b, (((0,), (0,)), ((), ())), preferred_element_type=F32)


def kernel(
    q_in, k_in, v_in, w_in, g_in, valid,
    mixed, dq_out, dk_out, dv_out,
    kv, kvo, qo, qb, dob, dop, gall, wm, wo, att, attr, dqb, pb, bias,
    xs, rx, acc, zs, rz, ys, ms, mr, ms2, mr2, mo, rb, rb2, rc,
    lsem, hsem, fs, fr, bxs, bxr, bzs, bzr, bys, byr, gs, gr, qs, qr, dqs, dqr, ats, atr, mss, msr, rls, rlr, bcs, bcr,
):
    i = lax.axis_index("tile")
    j = lax.axis_index("head")
    t = i // GH
    g = i % GH
    p = g % 2
    u = g // 2
    d = 2 * p - 1
    e = (u == 3).astype(jnp.int32) - (u == 4).astype(jnp.int32)
    near = (t * GH + (g + 2 * d + GH) % GH, j)
    far = (t * GH + (g - 2 * d + GH) % GH, j)
    up = (((t + 1) % GT) * GH + g, j)
    down = (((t + GT - 1) % GT) * GH + g, j)
    relay = (t * GH + (g + GH // 2) % GH, j)
    relay_to = (t * GH + (g + 6 + 4 * (u == 7).astype(jnp.int32)) % GH, j)
    back = (((t - e + GT) % GT) * GH + (g + 2 * e), j)
    j1 = j + 1 - 2 * (j % 2)
    j2 = (j + 2) % 4
    partner = (i + 1 - 2 * p, j2)
    j3 = (j1 + 2) % 4
    sibling = (i, j1)
    across = (i, j2)
    has_up = t < GT - 1
    has_down = t > 0
    has_near = (u + d >= 0) & (u + d < GH // 2)
    has_far = (u - d >= 0) & (u - d < GH // 2)
    near_cross = e == d
    far_cross = e == -d
    is_cross = e != 0
    is_relay = (u == 0) | (u == 7)
    has_back = (t - e >= 0) & (t - e < GT)
    has_ahead = (t + e >= 0) & (t + e < GT)
    mine = pl.multiple_of(p * HALF, 128)
    theirs = pl.multiple_of((1 - p) * HALF, 128)
    scale = HD ** (-0.5)

    @pl.when(jnp.logical_not(has_down))
    def _():
        for s in (0, 3, 6, 9):
            kv[:, pl.ds(s * T, T), :] = jnp.zeros((NH, T, 2 * HD), BF)
        rz[:, 1] = jnp.zeros((NH, 2 * T, 2 * HD), BF)

    @pl.when(jnp.logical_not(has_up))
    def _():
        for s in (2, 5, 8, 11):
            kv[:, pl.ds(s * T, T), :] = jnp.zeros((NH, T, 2 * HD), BF)
        rz[:, 0] = jnp.zeros((NH, 2 * T, 2 * HD), BF)

    for n, side, there, crossing in ((0, 0, has_near, near_cross), (1, 3, has_far, far_cross)):
        @pl.when(jnp.logical_not(there))
        def _():
            kv[:, pl.ds(side * SIDE, SIDE), :] = jnp.zeros((NH, SIDE, 2 * HD), BF)

        @pl.when(jnp.logical_not(there) | crossing)
        def _():
            rx[:, n] = jnp.zeros((NH, SIDE, 2 * HD), BF)

    barrier = pltpu.get_barrier_semaphore()
    greeted = 0
    for peer, cond in (
        (partner, None), (sibling, None), (across, None), (near, has_near), (far, has_far), (up, has_up),
        (down, has_down), (relay, is_cross | is_relay), (relay_to, is_relay),
        ((t * GH + (g + GH - 6 * e) % GH, j), is_cross), (back, is_cross & has_back),
    ):
        if cond is None:
            pl.semaphore_signal(barrier, inc=1, device_id=peer, device_id_type=MESH)
            greeted += 1
        else:
            @pl.when(cond)
            def _():
                pl.semaphore_signal(barrier, inc=1, device_id=peer, device_id_type=MESH)
            greeted += cond.astype(jnp.int32)

    START, WAIT = 0, 1

    def when(cond, action):
        if cond is None:
            action()
        else:
            @pl.when(cond)
            def _():
                action()

    def remote(act, src, dst, send, recv, device, cond=None):
        copy = pltpu.make_async_remote_copy(
            src_ref=src, dst_ref=dst, send_sem=send, recv_sem=recv, device_id=device, device_id_type=MESH
        )
        when(cond, copy.start if act == START else copy.wait_send)

    def arrived(dst, recv, cond=None):
        copy = pltpu.make_async_remote_copy(
            src_ref=dst, dst_ref=dst, send_sem=lsem.at[0], recv_sem=recv, device_id=partner, device_id_type=MESH
        )
        when(cond, copy.wait_recv)

    def slot(h, s):
        return kv.at[h, pl.ds(s * T, T), :]

    def cols(h):
        return pl.ds(pl.multiple_of(h * HD, HD), HD)

    def mine_cols(h):
        return pl.ds(pl.multiple_of(mine + h * HD, HD), HD)

    def their_cols(h):
        return pl.ds(pl.multiple_of(theirs + h * HD, HD), HD)

    def local(src, dst, sem):
        copy = pltpu.make_async_copy(src, dst, sem)
        copy.start()
        return copy

    staged = [
        [
            local(source.at[:, columns(h)], kvo.at[h, n, :, pl.ds(part * HD, HD)], hsem.at[h, 2 * n + part])
            for n, columns in enumerate((mine_cols, their_cols))
            for part, source in enumerate((k_in, v_in))
        ]
        for h in range(NH)
    ]
    g_copy = local(g_in, gall.at[0], lsem.at[0])
    q_copies = [
        local(q_in.at[:, pl.ds(mine, HALF)], qo.at[0], lsem.at[1]),
        local(q_in.at[:, pl.ds(theirs, HALF)], qo.at[1], lsem.at[2]),
    ]
    w_copies = [
        local(w_in.at[:, pl.ds(theirs, HALF)], wo, lsem.at[3]),
        local(w_in.at[:, pl.ds(mine, HALF)], wm, lsem.at[4]),
    ]

    lanes = lax.broadcasted_iota(jnp.int32, (1, WIN), 1)
    for a in range(2):
        row = jnp.zeros((1, WIN), F32)
        for n in range(9):
            g_slot, t_slot = a + n // 3, n % 3
            t_abs = t + t_slot - 1
            g_abs = g + (g_slot - 1) * (1 - 2 * p)
            if t_slot == 1 and g_slot == a + 1:
                value = jnp.float32(0.0)
            else:
                flag = valid[((t_abs + GT) % GT) * GH + (g_abs + GH) % GH]
                inside = (t_abs >= 0) & (t_abs < GT) & (g_abs >= 0) & (g_abs < GH)
                value = jnp.where(inside & (flag > 0), 0.0, -jnp.inf).astype(F32)
            row = jnp.where((lanes >= n * T) & (lanes < (n + 1) * T), value, row)
        bias[a] = row

    pl.semaphore_wait(barrier, greeted)

    def send_side(act, h, s, target, n, device, there, crossing):
        tile = slot(h, s)
        remote(act, tile, slot(h, target), fs.at[h, n], fr.at[h, target], device, there & jnp.logical_not(crossing))
        remote(act, tile, rb.at[h], rls.at[h, 0], rlr.at[h, 0], relay, crossing)
        remote(
            act, tile, slot(h, target + e), fs.at[h, n + 1], fr.at[h, target + e], back, crossing & has_back
        )

    def send_swap(act, h):
        remote(act, kvo.at[h, 0], slot(h, 4), fs.at[h, 12], fr.at[h, 4], across)
        remote(act, kvo.at[h, 1], slot(h, 7), fs.at[h, 13], fr.at[h, 7], partner)

    def send_z(act, h, s):
        remote(act, slot(h, s), slot(h, s - 1), fs.at[h, 0 if s == 4 else 2], fr.at[h, s - 1], up, has_up)
        remote(act, slot(h, s), slot(h, s + 1), fs.at[h, 1 if s == 4 else 3], fr.at[h, s + 1], down, has_down)

    def send_own_x(act, h):
        send_side(act, h, 4, 10, 4, near, has_near, near_cross)

    def send_other_x(act, h):
        send_side(act, h, 7, 1, 6, far, has_far, far_cross)

    def pass_on(act, h):
        target = jnp.where((u == 7) == (p == 1), 10, 1)
        remote(act, rb.at[h], slot(h, target), rls.at[h, 1], fr.at[h, target], relay_to, is_relay)

    def forward(act, h, n):
        target, device, there, crossing = ((9, near, has_near, near_cross), (0, far, has_far, far_cross))[n]
        for k, exists, way in ((0, has_down, 1), (2, has_up, -1)):
            source = slot(h, 3 + 3 * n + k)
            if act == START:
                arrived(source, fr.at[h, 3 + 3 * n + k], exists)
            remote(
                act, source, slot(h, target + k), fs.at[h, 8 + 2 * n + k // 2], fr.at[h, target + k], device,
                exists & there & (jnp.logical_not(crossing) | (e == way)),
            )

    def send_back(act, h, n):
        device, there, crossing = ((far, has_far, far_cross), (near, has_near, near_cross))[n]
        remote(
            act, xs.at[h, n], rx.at[h, n], bxs.at[h, n, 0], bxr.at[h, n, 0], device,
            there & jnp.logical_not(crossing),
        )
        remote(act, xs.at[h, n, pl.ds(T, T)], rb2.at[h], rls.at[h, 2], rlr.at[h, 1], relay, crossing)
        rows = pl.ds((1 + e) * T, T)
        remote(
            act, xs.at[h, n, rows], rx.at[h, n, rows], bxs.at[h, n, 1], bxr.at[h, n, 2], device, crossing & has_ahead
        )
        remote(
            act, xs.at[h, n, pl.ds((1 - e) * T, T)], rc.at[h], bcs.at[h, n], bcr.at[h], back, crossing & has_back
        )

    def pass_back(act, h):
        n = jnp.where(u == 7, p, 1 - p)
        remote(act, rb2.at[h], rx.at[h, n, pl.ds(T, T)], rls.at[h, 3], bxr.at[h, n, 1], relay_to, is_relay)

    def send_attended(act, h):
        for n, device in enumerate((across, partner)):
            remote(act, att.at[n, :, cols(h)], attr.at[n, :, cols(h)], ats.at[h, n], atr.at[h, n], device)

    def send_query_grad(act, h):
        for n, device in enumerate((across, partner)):
            remote(act, dqb.at[n, :, cols(h)], dq_out.at[:, mine_cols(h)], dqs.at[h, n], dqr.at[h, n], device)

    def send_reduced(act, h):
        remote(act, zs.at[h, 0], rz.at[h, 0], bzs.at[h, 0], bzr.at[h, 0], down, has_down)
        remote(act, zs.at[h, 1], rz.at[h, 1], bzs.at[h, 1], bzr.at[h, 1], up, has_up)

    def send_total(act, h):
        for n, device in enumerate((across, partner)):
            for part, out in enumerate((dk_out, dv_out)):
                remote(
                    act, ys.at[h, n, :, pl.ds(part * HD, HD)], out.at[:, mine_cols(h)], bys.at[h, n, part],
                    byr.at[h, n, part], device,
                )

    def attend(h):
        for s, there in ((9, has_far & has_down), (10, has_far), (11, has_far & has_up),
                         (0, has_near & has_down), (1, has_near), (2, has_near & has_up)):
            arrived(slot(h, s), fr.at[h, s], there)
        for a in range(2):
            window = pl.ds(a * SIDE, WIN)
            s = nt(qb[a, :, cols(h)], kv[h, window, pl.ds(0, HD)]) * scale + bias[a]
            x = jnp.exp(s - jnp.max(s, axis=1, keepdims=True))
            weights = (x * (1.0 / jnp.sum(x, axis=1, keepdims=True))).astype(BF)
            pb[a] = weights
            att[a, :, cols(h)] = nn(weights, kv[h, window, pl.ds(HD, HD)]).astype(BF)
        send_attended(START, h)

    def differentiate(h, a):
        q = qb[a, :, cols(h)]
        do = dob[a, :, cols(h)]
        window = pl.ds(a * SIDE, WIN)
        k = kv[h, window, pl.ds(0, HD)]
        weights = pb[a]
        row_dot = jnp.sum(do.astype(F32) * att[a, :, cols(h)].astype(F32), axis=1, keepdims=True)
        weight_grad = nt(do, kv[h, window, pl.ds(HD, HD)])
        score_grad = (weights.astype(F32) * (weight_grad - row_dot) * scale).astype(BF)
        dqb[a, :, cols(h)] = nn(score_grad, k).astype(BF)
        for part, lhs, rhs in ((0, score_grad, q), (1, weights, do)):
            grad = tn(lhs, rhs)
            lane = pl.ds(part * HD, HD)
            if a == 0:
                xs[h, 1, :, lane] = grad[:SIDE].astype(BF)
                acc[h, :, lane] = grad[SIDE:]
            else:
                acc[h, :, lane] += grad[:2 * SIDE]
                xs[h, 0, :, lane] = grad[2 * SIDE:].astype(BF)
        send_back(START, h, 1 - a)
        if a == 1:
            send_query_grad(START, h)

    def reduce_x(h):
        for n, there, crossing in ((0, has_near, near_cross), (1, has_far, far_cross)):
            arrived(rx.at[h, n], bxr.at[h, n, 0], there & jnp.logical_not(crossing))
            arrived(rx.at[h, n, pl.ds(T, T)], bxr.at[h, n, 1], crossing)
            arrived(rx.at[h, n, pl.ds((1 - e) * T, T)], bxr.at[h, n, 2], crossing & has_back)
        for n in range(2):
            for part, row in ((0, 0), (1, 2 * T)):
                zs[h, part, pl.ds(n * T, T), :] = (
                    acc[h, pl.ds(n * SIDE + row, T), :] + rx[h, n, pl.ds(row, T), :].astype(F32)
                ).astype(BF)
            acc[h, pl.ds(n * SIDE + T, T), :] += rx[h, n, pl.ds(T, T), :].astype(F32)
        send_reduced(START, h)

    def reduce_z(h):
        arrived(rz.at[h, 0], bzr.at[h, 0], has_up)
        arrived(rz.at[h, 1], bzr.at[h, 1], has_down)
        arrived(rc.at[h], bcr.at[h], is_cross & has_back)
        for n, crossing in ((0, near_cross), (1, far_cross)):
            @pl.when(crossing & has_back)
            def _():
                acc[h, pl.ds(n * SIDE + T, T), :] += rc[h].astype(F32)

        for n in range(2):
            rows = pl.ds(n * T, T)
            ys[h, n] = (
                acc[h, pl.ds(n * SIDE + T, T), :] + rz[h, 0, rows, :].astype(F32) + rz[h, 1, rows, :].astype(F32)
            ).astype(BF)
        send_total(START, h)

    blocks = (j, j1, j2, j3)
    rows = [pl.ds(pl.multiple_of(block * FULL, FULL), FULL) for block in blocks]

    def attn_grad(weights_ref):
        total = nn(gall[0], weights_ref[rows[0], :])
        for n in range(1, 4):
            total = total + nn(gall[n], weights_ref[rows[n], :])
        return total.astype(BF)

    blocks = (j, j1, j2, j3)
    rows = [pl.ds(pl.multiple_of(block * FULL, FULL), FULL) for block in blocks]

    def send_gathered(act, n):
        source, target, device, k = ((0, 2, across, 1), (0, 1, sibling, 0), (2, 3, sibling, 2))[n]
        remote(act, gall.at[source], gall.at[target], gs.at[k], gr.at[k], device)

    def send_queries(act):
        for n, device in enumerate((across, partner)):
            remote(act, qo.at[n], qb.at[n], qs.at[n], qr.at[n], device)

    def send_attn_grad(n):
        weights_ref = (wm, wo)[n]
        total = nn(gall[0], weights_ref[rows[0], :])
        for k in range(1, 4):
            total = total + nn(gall[k], weights_ref[rows[k], :])
        dop[n] = total.astype(BF)
        remote(START, dop.at[n], dob.at[n], qs.at[2 + n], qr.at[2 + n], (across, partner)[n])

    def project(n):
        return nt(attr[0], wm[rows[n], :]) + nt(attr[1], wo[rows[n], :])

    for copy in staged[0]:
        copy.wait()
    send_swap(START, 0)
    g_copy.wait()
    send_gathered(START, 1)
    arrived(slot(0, 7), fr.at[0, 7])
    send_z(START, 0, 7)
    arrived(slot(0, 4), fr.at[0, 4])
    send_z(START, 0, 4)
    for copy in staged[1]:
        copy.wait()
    send_swap(START, 1)
    send_own_x(START, 0)
    send_gathered(START, 0)
    send_other_x(START, 0)
    arrived(gall.at[2], gr.at[1])
    send_gathered(START, 2)
    arrived(slot(1, 7), fr.at[1, 7])
    send_z(START, 1, 7)
    for copy in q_copies:
        copy.wait()
    send_queries(START)
    for copy in staged[2]:
        copy.wait()
    send_swap(START, 2)
    forward(START, 0, 1)
    arrived(rb.at[0], rlr.at[0, 0], is_relay)
    pass_on(START, 0)
    forward(START, 0, 0)
    send_other_x(START, 1)
    send_z(WAIT, 0, 4)
    for copy in w_copies:
        copy.wait()
    arrived(gall.at[1], gr.at[0])
    arrived(gall.at[3], gr.at[2])
    send_attn_grad(1)
    send_attn_grad(0)
    arrived(slot(1, 4), fr.at[1, 4])
    send_z(START, 1, 4)
    send_z(WAIT, 0, 7)
    send_own_x(START, 1)
    for n in range(2):
        arrived(qb.at[n], qr.at[n])
    attend(0)
    for n in range(2):
        arrived(dob.at[n], qr.at[2 + n])
    differentiate(0, 0)
    differentiate(0, 1)
    forward(START, 1, 0)
    forward(START, 1, 1)
    arrived(slot(2, 4), fr.at[2, 4])
    send_z(START, 2, 4)
    arrived(rb2.at[0], rlr.at[0, 1], is_relay)
    pass_back(START, 0)
    arrived(slot(2, 7), fr.at[2, 7])
    send_z(START, 2, 7)
    arrived(rb.at[1], rlr.at[1, 0], is_relay)
    pass_on(START, 1)
    send_own_x(START, 2)
    attend(1)
    send_other_x(START, 2)
    send_z(WAIT, 1, 7)
    forward(START, 2, 0)
    reduce_x(0)
    forward(START, 2, 1)
    send_z(WAIT, 2, 7)
    differentiate(1, 0)
    send_z(WAIT, 2, 4)
    send_z(WAIT, 1, 4)
    differentiate(1, 1)
    arrived(rb.at[2], rlr.at[2, 0], is_relay)
    pass_on(START, 2)
    attend(2)
    differentiate(2, 0)
    arrived(rb2.at[1], rlr.at[1, 1], is_relay)
    pass_back(START, 1)
    reduce_x(1)
    differentiate(2, 1)
    arrived(rb2.at[2], rlr.at[2, 1], is_relay)
    pass_back(START, 2)
    reduce_z(0)
    reduce_x(2)
    for h in range(NH):
        for n in range(2):
            arrived(attr.at[n, :, cols(h)], atr.at[h, n])
    ms[0] = project(3).astype(BF)
    ms[1] = project(1).astype(BF)
    remote(START, ms, mr, mss.at[0], msr.at[0], sibling)
    reduce_z(1)
    crossing_sum = project(2)
    arrived(mr, msr.at[0])
    ms2[...] = (crossing_sum + mr[0].astype(F32)).astype(BF)
    remote(START, ms2, mr2, mss.at[1], msr.at[1], across)
    kept = project(0) + mr[1].astype(F32)
    reduce_z(2)
    arrived(mr2, msr.at[1])
    mo[...] = (kept + mr2[...].astype(F32)).astype(BF)
    mixed_copy = local(mo, mixed, lsem.at[5])

    for n in range(3):
        send_gathered(WAIT, n)
    send_queries(WAIT)
    for n, device in enumerate((across, partner)):
        remote(WAIT, dop.at[n], dob.at[n], qs.at[2 + n], qr.at[2 + n], device)
    remote(WAIT, ms, mr, mss.at[0], msr.at[0], sibling)
    remote(WAIT, ms2, mr2, mss.at[1], msr.at[1], across)
    for h in range(NH):
        for send in (
            send_swap, send_own_x, send_other_x, pass_on, pass_back, send_attended, send_query_grad, send_reduced,
            send_total,
        ):
            send(WAIT, h)
        for n, columns in enumerate((mine_cols, their_cols)):
            forward(WAIT, h, n)
            send_back(WAIT, h, n)
            arrived(dq_out.at[:, columns(h)], dqr.at[h, n])
            arrived(dk_out.at[:, columns(h)], byr.at[h, n, 0])
            arrived(dv_out.at[:, columns(h)], byr.at[h, n, 1])
    mixed_copy.wait()

def hand_over(*refs):
    for n in range(4):
        refs[4 + n][...] = refs[n][...]


def on_device(queries, keys, values, w_out, out_grad, tile_valid):
    dma = pltpu.SemaphoreType.DMA
    any_space = pl.BlockSpec(memory_space=pl.ANY)
    block = jax.ShapeDtypeStruct(queries.shape, BF)
    results = pl.pallas_call(
        kernel,
        out_shape=(block, block, block, block),
        in_specs=[any_space] * 5 + [pl.BlockSpec(memory_space=pltpu.SMEM)],
        out_specs=(any_space, any_space, any_space, any_space),
        scratch_shapes=[
            pltpu.VMEM((NH, 12 * T, 2 * HD), BF),
            pltpu.VMEM((NH, 2, T, 2 * HD), BF),
            pltpu.VMEM((2, T, HALF), BF),
            pltpu.VMEM((2, T, HALF), BF),
            pltpu.VMEM((2, T, HALF), BF),
            pltpu.VMEM((2, T, HALF), BF),
            pltpu.VMEM((4, T, FULL), BF),
            pltpu.VMEM((4 * FULL, HALF), BF),
            pltpu.VMEM((4 * FULL, HALF), BF),
            pltpu.VMEM((2, T, HALF), BF),
            pltpu.VMEM((2, T, HALF), BF),
            pltpu.VMEM((2, T, HALF), BF),
            pltpu.VMEM((2, T, WIN), BF),
            pltpu.VMEM((2, 1, WIN), F32),
            pltpu.VMEM((NH, 2, SIDE, 2 * HD), BF),
            pltpu.VMEM((NH, 2, SIDE, 2 * HD), BF),
            pltpu.VMEM((NH, 2 * SIDE, 2 * HD), F32),
            pltpu.VMEM((NH, 2, 2 * T, 2 * HD), BF),
            pltpu.VMEM((NH, 2, 2 * T, 2 * HD), BF),
            pltpu.VMEM((NH, 2, T, 2 * HD), BF),
            pltpu.VMEM((2, T, FULL), BF),
            pltpu.VMEM((2, T, FULL), BF),
            pltpu.VMEM((T, FULL), BF),
            pltpu.VMEM((T, FULL), BF),
            pltpu.VMEM((T, FULL), BF),
            pltpu.VMEM((NH, T, 2 * HD), BF),
            pltpu.VMEM((NH, T, 2 * HD), BF),
            pltpu.VMEM((NH, T, 2 * HD), BF),
            dma((6,)),
            dma((NH, 4)),
            dma((NH, 14)),
            dma((NH, 12)),
            dma((NH, 2, 2)),
            dma((NH, 2, 3)),
            dma((NH, 2)),
            dma((NH, 2)),
            dma((NH, 2, 2)),
            dma((NH, 2, 2)),
            dma((3,)),
            dma((3,)),
            dma((4,)),
            dma((4,)),
            dma((NH, 2)),
            dma((NH, 2)),
            dma((NH, 2)),
            dma((NH, 2)),
            dma((2,)),
            dma((2,)),
            dma((NH, 4)),
            dma((NH, 2)),
            dma((NH, 2)),
            dma((NH,)),
        ],
        compiler_params=pltpu.CompilerParams(
            collective_id=0, has_side_effects=True, vmem_limit_bytes=56 * 1024 * 1024
        ),
    )(queries, keys, values, w_out, out_grad, tile_valid)
    whole = pl.BlockSpec(memory_space=pltpu.VMEM)
    return pl.pallas_call(
        hand_over,
        out_shape=(block, block, block, block),
        in_specs=[whole] * 4,
        out_specs=(whole, whole, whole, whole),
    )(*results)


def solution(mesh):
    return jax.shard_map(
        on_device,
        mesh=mesh,
        in_specs=(
            P("tile", "head"),
            P("tile", "head"),
            P("tile", "head"),
            P(None, "head"),
            P("tile", "head"),
            P(),
        ),
        out_specs=(P("tile", "head"), P("tile", "head"), P("tile", "head"), P("tile", "head")),
        check_vma=False,
    )
```

```python
import jax
import jax.numpy as jnp
from jax import lax
from jax.experimental import pallas as pl
from jax.experimental.pallas import tpu as pltpu
from jax.sharding import PartitionSpec as P

HD = 128
GT = 4
GH = 16
T = 160
NH = 3
HALF = NH * HD
FULL = 2 * HALF
WIN = 9 * T
SIDE = 3 * T
MESH = pl.DeviceIdType.MESH
BF = jnp.bfloat16
F32 = jnp.float32


def nt(a, b):
    return lax.dot_general(a, b, (((1,), (1,)), ((), ())), preferred_element_type=F32)


def nn(a, b):
    return lax.dot_general(a, b, (((1,), (0,)), ((), ())), preferred_element_type=F32)


def tn(a, b):
    return lax.dot_general(a, b, (((0,), (0,)), ((), ())), preferred_element_type=F32)


def kernel(
    q_in, k_in, v_in, w_in, g_in, valid,
    mixed, dq_out, dk_out, dv_out,
    kv, kvo, qo, qb, dob, dop, gall, wm, wo, att, attr, dqb, pb, bias,
    xs, rx, acc, zs, rz, ys, ms, mr, ms2, mr2, mo, rb, rb2, rc,
    lsem, hsem, fs, fr, bxs, bxr, bzs, bzr, bys, byr, gs, gr, qs, qr, dqs, dqr, ats, atr, mss, msr, rls, rlr, bcs, bcr,
):
    i = lax.axis_index("tile")
    j = lax.axis_index("head")
    t = i // GH
    g = i % GH
    p = g % 2
    u = g // 2
    d = 2 * p - 1
    e = (u == 3).astype(jnp.int32) - (u == 4).astype(jnp.int32)
    near = (t * GH + (g + 2 * d + GH) % GH, j)
    far = (t * GH + (g - 2 * d + GH) % GH, j)
    up = (((t + 1) % GT) * GH + g, j)
    down = (((t + GT - 1) % GT) * GH + g, j)
    relay = (t * GH + (g + GH // 2) % GH, j)
    relay_to = (t * GH + (g + 6 + 4 * (u == 7).astype(jnp.int32)) % GH, j)
    back = (((t - e + GT) % GT) * GH + (g + 2 * e), j)
    j1 = j + 1 - 2 * (j % 2)
    j2 = (j + 2) % 4
    partner = (i + 1 - 2 * p, j2)
    j3 = (j1 + 2) % 4
    sibling = (i, j1)
    across = (i, j2)
    has_up = t < GT - 1
    has_down = t > 0
    has_near = (u + d >= 0) & (u + d < GH // 2)
    has_far = (u - d >= 0) & (u - d < GH // 2)
    near_cross = e == d
    far_cross = e == -d
    is_cross = e != 0
    is_relay = (u == 0) | (u == 7)
    has_back = (t - e >= 0) & (t - e < GT)
    has_ahead = (t + e >= 0) & (t + e < GT)
    mine = pl.multiple_of(p * HALF, 128)
    theirs = pl.multiple_of((1 - p) * HALF, 128)
    scale = HD ** (-0.5)

    @pl.when(jnp.logical_not(has_down))
    def _():
        for s in (0, 3, 6, 9):
            kv[:, pl.ds(s * T, T), :] = jnp.zeros((NH, T, 2 * HD), BF)
        rz[:, 1] = jnp.zeros((NH, 2 * T, 2 * HD), BF)

    @pl.when(jnp.logical_not(has_up))
    def _():
        for s in (2, 5, 8, 11):
            kv[:, pl.ds(s * T, T), :] = jnp.zeros((NH, T, 2 * HD), BF)
        rz[:, 0] = jnp.zeros((NH, 2 * T, 2 * HD), BF)

    for n, side, there, crossing in ((0, 0, has_near, near_cross), (1, 3, has_far, far_cross)):
        @pl.when(jnp.logical_not(there))
        def _():
            kv[:, pl.ds(side * SIDE, SIDE), :] = jnp.zeros((NH, SIDE, 2 * HD), BF)

        @pl.when(jnp.logical_not(there) | crossing)
        def _():
            rx[:, n] = jnp.zeros((NH, SIDE, 2 * HD), BF)

    barrier = pltpu.get_barrier_semaphore()
    greeted = 0
    for peer, cond in (
        (partner, None), (sibling, None), (across, None), (near, has_near), (far, has_far), (up, has_up),
        (down, has_down), (relay, is_cross | is_relay), (relay_to, is_relay),
        ((t * GH + (g + GH - 6 * e) % GH, j), is_cross), (back, is_cross & has_back),
    ):
        if cond is None:
            pl.semaphore_signal(barrier, inc=1, device_id=peer, device_id_type=MESH)
            greeted += 1
        else:
            @pl.when(cond)
            def _():
                pl.semaphore_signal(barrier, inc=1, device_id=peer, device_id_type=MESH)
            greeted += cond.astype(jnp.int32)

    START, WAIT = 0, 1

    def when(cond, action):
        if cond is None:
            action()
        else:
            @pl.when(cond)
            def _():
                action()

    def remote(act, src, dst, send, recv, device, cond=None):
        copy = pltpu.make_async_remote_copy(
            src_ref=src, dst_ref=dst, send_sem=send, recv_sem=recv, device_id=device, device_id_type=MESH
        )
        when(cond, copy.start if act == START else copy.wait_send)

    def arrived(dst, recv, cond=None):
        copy = pltpu.make_async_remote_copy(
            src_ref=dst, dst_ref=dst, send_sem=lsem.at[0], recv_sem=recv, device_id=partner, device_id_type=MESH
        )
        when(cond, copy.wait_recv)

    def slot(h, s):
        return kv.at[h, pl.ds(s * T, T), :]

    def cols(h):
        return pl.ds(pl.multiple_of(h * HD, HD), HD)

    def mine_cols(h):
        return pl.ds(pl.multiple_of(mine + h * HD, HD), HD)

    def their_cols(h):
        return pl.ds(pl.multiple_of(theirs + h * HD, HD), HD)

    def local(src, dst, sem):
        copy = pltpu.make_async_copy(src, dst, sem)
        copy.start()
        return copy

    staged = [
        [
            local(source.at[:, columns(h)], kvo.at[h, n, :, pl.ds(part * HD, HD)], hsem.at[h, 2 * n + part])
            for n, columns in enumerate((mine_cols, their_cols))
            for part, source in enumerate((k_in, v_in))
        ]
        for h in range(NH)
    ]
    g_copy = local(g_in, gall.at[0], lsem.at[0])
    q_copies = [
        local(q_in.at[:, pl.ds(mine, HALF)], qo.at[0], lsem.at[1]),
        local(q_in.at[:, pl.ds(theirs, HALF)], qo.at[1], lsem.at[2]),
    ]
    w_copies = [
        local(w_in.at[:, pl.ds(theirs, HALF)], wo, lsem.at[3]),
        local(w_in.at[:, pl.ds(mine, HALF)], wm, lsem.at[4]),
    ]

    lanes = lax.broadcasted_iota(jnp.int32, (1, WIN), 1)
    for a in range(2):
        row = jnp.zeros((1, WIN), F32)
        for n in range(9):
            g_slot, t_slot = a + n // 3, n % 3
            t_abs = t + t_slot - 1
            g_abs = g + (g_slot - 1) * (1 - 2 * p)
            if t_slot == 1 and g_slot == a + 1:
                value = jnp.float32(0.0)
            else:
                flag = valid[((t_abs + GT) % GT) * GH + (g_abs + GH) % GH]
                inside = (t_abs >= 0) & (t_abs < GT) & (g_abs >= 0) & (g_abs < GH)
                value = jnp.where(inside & (flag > 0), 0.0, -jnp.inf).astype(F32)
            row = jnp.where((lanes >= n * T) & (lanes < (n + 1) * T), value, row)
        bias[a] = row

    pl.semaphore_wait(barrier, greeted)

    def send_side(act, h, s, target, n, device, there, crossing):
        tile = slot(h, s)
        remote(act, tile, slot(h, target), fs.at[h, n], fr.at[h, target], device, there & jnp.logical_not(crossing))
        remote(act, tile, rb.at[h], rls.at[h, 0], rlr.at[h, 0], relay, crossing)
        remote(
            act, tile, slot(h, target + e), fs.at[h, n + 1], fr.at[h, target + e], back, crossing & has_back
        )

    def send_swap(act, h):
        remote(act, kvo.at[h, 0], slot(h, 4), fs.at[h, 12], fr.at[h, 4], across)
        remote(act, kvo.at[h, 1], slot(h, 7), fs.at[h, 13], fr.at[h, 7], partner)

    def send_z(act, h, s):
        remote(act, slot(h, s), slot(h, s - 1), fs.at[h, 0 if s == 4 else 2], fr.at[h, s - 1], up, has_up)
        remote(act, slot(h, s), slot(h, s + 1), fs.at[h, 1 if s == 4 else 3], fr.at[h, s + 1], down, has_down)

    def send_own_x(act, h):
        send_side(act, h, 4, 10, 4, near, has_near, near_cross)

    def send_other_x(act, h):
        send_side(act, h, 7, 1, 6, far, has_far, far_cross)

    def pass_on(act, h):
        target = jnp.where((u == 7) == (p == 1), 10, 1)
        remote(act, rb.at[h], slot(h, target), rls.at[h, 1], fr.at[h, target], relay_to, is_relay)

    def forward(act, h, n):
        target, device, there, crossing = ((9, near, has_near, near_cross), (0, far, has_far, far_cross))[n]
        for k, exists, way in ((0, has_down, 1), (2, has_up, -1)):
            source = slot(h, 3 + 3 * n + k)
            if act == START:
                arrived(source, fr.at[h, 3 + 3 * n + k], exists)
            remote(
                act, source, slot(h, target + k), fs.at[h, 8 + 2 * n + k // 2], fr.at[h, target + k], device,
                exists & there & (jnp.logical_not(crossing) | (e == way)),
            )

    def send_back(act, h, n):
        device, there, crossing = ((far, has_far, far_cross), (near, has_near, near_cross))[n]
        remote(
            act, xs.at[h, n], rx.at[h, n], bxs.at[h, n, 0], bxr.at[h, n, 0], device,
            there & jnp.logical_not(crossing),
        )
        remote(act, xs.at[h, n, pl.ds(T, T)], rb2.at[h], rls.at[h, 2], rlr.at[h, 1], relay, crossing)
        rows = pl.ds((1 + e) * T, T)
        remote(
            act, xs.at[h, n, rows], rx.at[h, n, rows], bxs.at[h, n, 1], bxr.at[h, n, 2], device, crossing & has_ahead
        )
        remote(
            act, xs.at[h, n, pl.ds((1 - e) * T, T)], rc.at[h], bcs.at[h, n], bcr.at[h], back, crossing & has_back
        )

    def pass_back(act, h):
        n = jnp.where(u == 7, p, 1 - p)
        remote(act, rb2.at[h], rx.at[h, n, pl.ds(T, T)], rls.at[h, 3], bxr.at[h, n, 1], relay_to, is_relay)

    def send_attended(act, h):
        for n, device in enumerate((across, partner)):
            remote(act, att.at[n, :, cols(h)], attr.at[n, :, cols(h)], ats.at[h, n], atr.at[h, n], device)

    def send_query_grad(act, h):
        for n, device in enumerate((across, partner)):
            remote(act, dqb.at[n, :, cols(h)], dq_out.at[:, mine_cols(h)], dqs.at[h, n], dqr.at[h, n], device)

    def send_reduced(act, h):
        remote(act, zs.at[h, 0], rz.at[h, 0], bzs.at[h, 0], bzr.at[h, 0], down, has_down)
        remote(act, zs.at[h, 1], rz.at[h, 1], bzs.at[h, 1], bzr.at[h, 1], up, has_up)

    def send_total(act, h):
        for n, device in enumerate((across, partner)):
            for part, out in enumerate((dk_out, dv_out)):
                remote(
                    act, ys.at[h, n, :, pl.ds(part * HD, HD)], out.at[:, mine_cols(h)], bys.at[h, n, part],
                    byr.at[h, n, part], device,
                )

    def attend(h):
        for s, there in ((9, has_far & has_down), (10, has_far), (11, has_far & has_up),
                         (0, has_near & has_down), (1, has_near), (2, has_near & has_up)):
            arrived(slot(h, s), fr.at[h, s], there)
        for a in range(2):
            window = pl.ds(a * SIDE, WIN)
            s = nt(qb[a, :, cols(h)], kv[h, window, pl.ds(0, HD)]) * scale + bias[a]
            x = jnp.exp(s - jnp.max(s, axis=1, keepdims=True))
            weights = (x * (1.0 / jnp.sum(x, axis=1, keepdims=True))).astype(BF)
            pb[a] = weights
            att[a, :, cols(h)] = nn(weights, kv[h, window, pl.ds(HD, HD)]).astype(BF)
        send_attended(START, h)

    def differentiate(h, a):
        q = qb[a, :, cols(h)]
        do = dob[a, :, cols(h)]
        window = pl.ds(a * SIDE, WIN)
        k = kv[h, window, pl.ds(0, HD)]
        weights = pb[a]
        row_dot = jnp.sum(do.astype(F32) * att[a, :, cols(h)].astype(F32), axis=1, keepdims=True)
        weight_grad = nt(do, kv[h, window, pl.ds(HD, HD)])
        score_grad = (weights.astype(F32) * (weight_grad - row_dot) * scale).astype(BF)
        dqb[a, :, cols(h)] = nn(score_grad, k).astype(BF)
        for part, lhs, rhs in ((0, score_grad, q), (1, weights, do)):
            grad = tn(lhs, rhs)
            lane = pl.ds(part * HD, HD)
            if a == 0:
                xs[h, 1, :, lane] = grad[:SIDE].astype(BF)
                acc[h, :, lane] = grad[SIDE:]
            else:
                acc[h, :, lane] += grad[:2 * SIDE]
                xs[h, 0, :, lane] = grad[2 * SIDE:].astype(BF)
        send_back(START, h, 1 - a)
        if a == 1:
            send_query_grad(START, h)

    def reduce_x(h):
        for n, there, crossing in ((0, has_near, near_cross), (1, has_far, far_cross)):
            arrived(rx.at[h, n], bxr.at[h, n, 0], there & jnp.logical_not(crossing))
            arrived(rx.at[h, n, pl.ds(T, T)], bxr.at[h, n, 1], crossing)
            arrived(rx.at[h, n, pl.ds((1 - e) * T, T)], bxr.at[h, n, 2], crossing & has_back)
        for n in range(2):
            for part, row in ((0, 0), (1, 2 * T)):
                zs[h, part, pl.ds(n * T, T), :] = (
                    acc[h, pl.ds(n * SIDE + row, T), :] + rx[h, n, pl.ds(row, T), :].astype(F32)
                ).astype(BF)
            acc[h, pl.ds(n * SIDE + T, T), :] += rx[h, n, pl.ds(T, T), :].astype(F32)
        send_reduced(START, h)

    def reduce_z(h):
        arrived(rz.at[h, 0], bzr.at[h, 0], has_up)
        arrived(rz.at[h, 1], bzr.at[h, 1], has_down)
        arrived(rc.at[h], bcr.at[h], is_cross & has_back)
        for n, crossing in ((0, near_cross), (1, far_cross)):
            @pl.when(crossing & has_back)
            def _():
                acc[h, pl.ds(n * SIDE + T, T), :] += rc[h].astype(F32)

        for n in range(2):
            rows = pl.ds(n * T, T)
            ys[h, n] = (
                acc[h, pl.ds(n * SIDE + T, T), :] + rz[h, 0, rows, :].astype(F32) + rz[h, 1, rows, :].astype(F32)
            ).astype(BF)
        send_total(START, h)

    blocks = (j, j1, j2, j3)
    rows = [pl.ds(pl.multiple_of(block * FULL, FULL), FULL) for block in blocks]

    def attn_grad(weights_ref):
        total = nn(gall[0], weights_ref[rows[0], :])
        for n in range(1, 4):
            total = total + nn(gall[n], weights_ref[rows[n], :])
        return total.astype(BF)

    blocks = (j, j1, j2, j3)
    rows = [pl.ds(pl.multiple_of(block * FULL, FULL), FULL) for block in blocks]

    def send_gathered(act, n):
        source, target, device, k = ((0, 2, across, 1), (0, 1, sibling, 0), (2, 3, sibling, 2))[n]
        remote(act, gall.at[source], gall.at[target], gs.at[k], gr.at[k], device)

    def send_queries(act):
        for n, device in enumerate((across, partner)):
            remote(act, qo.at[n], qb.at[n], qs.at[n], qr.at[n], device)

    def send_attn_grad(n):
        weights_ref = (wm, wo)[n]
        total = nn(gall[0], weights_ref[rows[0], :])
        for k in range(1, 4):
            total = total + nn(gall[k], weights_ref[rows[k], :])
        dop[n] = total.astype(BF)
        remote(START, dop.at[n], dob.at[n], qs.at[2 + n], qr.at[2 + n], (across, partner)[n])

    def project(n):
        return nt(attr[0], wm[rows[n], :]) + nt(attr[1], wo[rows[n], :])

    g_copy.wait()
    send_gathered(START, 0)
    send_gathered(START, 1)
    for copy in staged[0]:
        copy.wait()
    send_swap(START, 0)
    for copy in staged[1]:
        copy.wait()
    send_swap(START, 1)
    for copy in staged[2]:
        copy.wait()
    send_swap(START, 2)
    arrived(slot(0, 4), fr.at[0, 4])
    send_z(START, 0, 4)
    send_own_x(START, 0)
    arrived(slot(0, 7), fr.at[0, 7])
    send_z(START, 0, 7)
    send_other_x(START, 0)
    arrived(slot(1, 4), fr.at[1, 4])
    send_z(START, 1, 4)
    send_own_x(START, 1)
    for copy in q_copies:
        copy.wait()
    send_queries(START)
    arrived(gall.at[2], gr.at[1])
    send_gathered(START, 2)
    arrived(slot(1, 7), fr.at[1, 7])
    send_z(START, 1, 7)
    send_other_x(START, 1)
    arrived(slot(2, 4), fr.at[2, 4])
    send_z(START, 2, 4)
    send_own_x(START, 2)
    arrived(rb.at[0], rlr.at[0, 0], is_relay)
    pass_on(START, 0)
    for copy in w_copies:
        copy.wait()
    arrived(gall.at[1], gr.at[0])
    arrived(gall.at[3], gr.at[2])
    send_attn_grad(1)
    send_attn_grad(0)
    arrived(slot(2, 7), fr.at[2, 7])
    send_z(START, 2, 7)
    send_other_x(START, 2)
    arrived(rb.at[1], rlr.at[1, 0], is_relay)
    pass_on(START, 1)
    forward(START, 0, 0)
    forward(START, 0, 1)
    arrived(rb.at[2], rlr.at[2, 0], is_relay)
    pass_on(START, 2)
    forward(START, 1, 0)
    forward(START, 1, 1)
    for n in range(2):
        arrived(qb.at[n], qr.at[n])
    attend(0)
    for n in range(2):
        arrived(dob.at[n], qr.at[2 + n])
    differentiate(0, 0)
    differentiate(0, 1)
    forward(START, 2, 0)
    forward(START, 2, 1)
    attend(1)
    differentiate(1, 0)
    differentiate(1, 1)
    arrived(rb2.at[0], rlr.at[0, 1], is_relay)
    pass_back(START, 0)
    reduce_x(0)
    attend(2)
    differentiate(2, 0)
    differentiate(2, 1)
    arrived(rb2.at[1], rlr.at[1, 1], is_relay)
    pass_back(START, 1)
    reduce_x(1)
    reduce_z(0)
    for h in range(NH):
        for n in range(2):
            arrived(attr.at[n, :, cols(h)], atr.at[h, n])
    ms[0] = project(3).astype(BF)
    ms[1] = project(1).astype(BF)
    remote(START, ms, mr, mss.at[0], msr.at[0], sibling)
    arrived(rb2.at[2], rlr.at[2, 1], is_relay)
    pass_back(START, 2)
    reduce_x(2)
    crossing_sum = project(2)
    arrived(mr, msr.at[0])
    ms2[...] = (crossing_sum + mr[0].astype(F32)).astype(BF)
    remote(START, ms2, mr2, mss.at[1], msr.at[1], across)
    kept = project(0) + mr[1].astype(F32)
    reduce_z(1)
    arrived(mr2, msr.at[1])
    mo[...] = (kept + mr2[...].astype(F32)).astype(BF)
    mixed_copy = local(mo, mixed, lsem.at[5])
    reduce_z(2)
    send_z(WAIT, 0, 4)
    send_z(WAIT, 0, 7)
    send_z(WAIT, 1, 4)
    send_z(WAIT, 1, 7)
    send_z(WAIT, 2, 4)
    send_z(WAIT, 2, 7)

    for n in range(3):
        send_gathered(WAIT, n)
    send_queries(WAIT)
    for n, device in enumerate((across, partner)):
        remote(WAIT, dop.at[n], dob.at[n], qs.at[2 + n], qr.at[2 + n], device)
    remote(WAIT, ms, mr, mss.at[0], msr.at[0], sibling)
    remote(WAIT, ms2, mr2, mss.at[1], msr.at[1], across)
    for h in range(NH):
        for send in (
            send_swap, send_own_x, send_other_x, pass_on, pass_back, send_attended, send_query_grad, send_reduced,
            send_total,
        ):
            send(WAIT, h)
        for n, columns in enumerate((mine_cols, their_cols)):
            forward(WAIT, h, n)
            send_back(WAIT, h, n)
            arrived(dq_out.at[:, columns(h)], dqr.at[h, n])
            arrived(dk_out.at[:, columns(h)], byr.at[h, n, 0])
            arrived(dv_out.at[:, columns(h)], byr.at[h, n, 1])
    mixed_copy.wait()

def hand_over(*refs):
    for n in range(4):
        refs[4 + n][...] = refs[n][...]


def on_device(queries, keys, values, w_out, out_grad, tile_valid):
    dma = pltpu.SemaphoreType.DMA
    any_space = pl.BlockSpec(memory_space=pl.ANY)
    block = jax.ShapeDtypeStruct(queries.shape, BF)
    results = pl.pallas_call(
        kernel,
        out_shape=(block, block, block, block),
        in_specs=[any_space] * 5 + [pl.BlockSpec(memory_space=pltpu.SMEM)],
        out_specs=(any_space, any_space, any_space, any_space),
        scratch_shapes=[
            pltpu.VMEM((NH, 12 * T, 2 * HD), BF),
            pltpu.VMEM((NH, 2, T, 2 * HD), BF),
            pltpu.VMEM((2, T, HALF), BF),
            pltpu.VMEM((2, T, HALF), BF),
            pltpu.VMEM((2, T, HALF), BF),
            pltpu.VMEM((2, T, HALF), BF),
            pltpu.VMEM((4, T, FULL), BF),
            pltpu.VMEM((4 * FULL, HALF), BF),
            pltpu.VMEM((4 * FULL, HALF), BF),
            pltpu.VMEM((2, T, HALF), BF),
            pltpu.VMEM((2, T, HALF), BF),
            pltpu.VMEM((2, T, HALF), BF),
            pltpu.VMEM((2, T, WIN), BF),
            pltpu.VMEM((2, 1, WIN), F32),
            pltpu.VMEM((NH, 2, SIDE, 2 * HD), BF),
            pltpu.VMEM((NH, 2, SIDE, 2 * HD), BF),
            pltpu.VMEM((NH, 2 * SIDE, 2 * HD), F32),
            pltpu.VMEM((NH, 2, 2 * T, 2 * HD), BF),
            pltpu.VMEM((NH, 2, 2 * T, 2 * HD), BF),
            pltpu.VMEM((NH, 2, T, 2 * HD), BF),
            pltpu.VMEM((2, T, FULL), BF),
            pltpu.VMEM((2, T, FULL), BF),
            pltpu.VMEM((T, FULL), BF),
            pltpu.VMEM((T, FULL), BF),
            pltpu.VMEM((T, FULL), BF),
            pltpu.VMEM((NH, T, 2 * HD), BF),
            pltpu.VMEM((NH, T, 2 * HD), BF),
            pltpu.VMEM((NH, T, 2 * HD), BF),
            dma((6,)),
            dma((NH, 4)),
            dma((NH, 14)),
            dma((NH, 12)),
            dma((NH, 2, 2)),
            dma((NH, 2, 3)),
            dma((NH, 2)),
            dma((NH, 2)),
            dma((NH, 2, 2)),
            dma((NH, 2, 2)),
            dma((3,)),
            dma((3,)),
            dma((4,)),
            dma((4,)),
            dma((NH, 2)),
            dma((NH, 2)),
            dma((NH, 2)),
            dma((NH, 2)),
            dma((2,)),
            dma((2,)),
            dma((NH, 4)),
            dma((NH, 2)),
            dma((NH, 2)),
            dma((NH,)),
        ],
        compiler_params=pltpu.CompilerParams(
            collective_id=0, has_side_effects=True, vmem_limit_bytes=56 * 1024 * 1024
        ),
    )(queries, keys, values, w_out, out_grad, tile_valid)
    whole = pl.BlockSpec(memory_space=pltpu.VMEM)
    return pl.pallas_call(
        hand_over,
        out_shape=(block, block, block, block),
        in_specs=[whole] * 4,
        out_specs=(whole, whole, whole, whole),
    )(*results)


def solution(mesh):
    return jax.shard_map(
        on_device,
        mesh=mesh,
        in_specs=(
            P("tile", "head"),
            P("tile", "head"),
            P("tile", "head"),
            P(None, "head"),
            P("tile", "head"),
            P(),
        ),
        out_specs=(P("tile", "head"), P("tile", "head"), P("tile", "head"), P("tile", "head")),
        check_vma=False,
    )
```

```python
import jax
import jax.numpy as jnp
from jax import lax
from jax.experimental import pallas as pl
from jax.experimental.pallas import tpu as pltpu
from jax.sharding import PartitionSpec as P

HD = 128
GT = 4
GH = 16
T = 160
NH = 3
HALF = NH * HD
FULL = 2 * HALF
WIN = 9 * T
SIDE = 3 * T
MESH = pl.DeviceIdType.MESH
BF = jnp.bfloat16
F32 = jnp.float32


def nt(a, b):
    return lax.dot_general(a, b, (((1,), (1,)), ((), ())), preferred_element_type=F32)


def nn(a, b):
    return lax.dot_general(a, b, (((1,), (0,)), ((), ())), preferred_element_type=F32)


def tn(a, b):
    return lax.dot_general(a, b, (((0,), (0,)), ((), ())), preferred_element_type=F32)


def kernel(
    q_in, k_in, v_in, w_in, g_in, valid,
    mixed, dq_out, dk_out, dv_out,
    kv, kvo, qb, dob, dop, gall, wm, wo, att, attr, dqb, bias,
    xs, rx, acc, zs, rz, yo, ys, ms, mr, ms2, mr2, mo, rb, rb2, rc, pb, qo,
    lsem, fs, fr, bxs, bxr, bzs, bzr, bys, byr, gs, gr, qs, qr, ats, atr, mss, msr, rls, rlr, bcs, bcr,
):
    i = lax.axis_index("tile")
    j = lax.axis_index("head")
    t = i // GH
    g = i % GH
    p = g % 2
    u = g // 2
    d = 2 * p - 1
    e = (u == 3).astype(jnp.int32) - (u == 4).astype(jnp.int32)
    partner = (i + 1 - 2 * p, j)
    near = (t * GH + (g + 2 * d + GH) % GH, j)
    far = (t * GH + (g - 2 * d + GH) % GH, j)
    up = (((t + 1) % GT) * GH + g, j)
    down = (((t + GT - 1) % GT) * GH + g, j)
    eight_off = (t * GH + (g + GH // 2) % GH, j)
    six_off = (t * GH + (g + 6 + 4 * (u == 7).astype(jnp.int32)) % GH, j)
    relay = (t * GH + (g + GH - 6 * e) % GH, j)
    relay_to = eight_off
    back = (((t - e + GT) % GT) * GH + (g + 2 * e), j)
    j1 = j + 1 - 2 * (j % 2)
    j2 = (j + 2) % 4
    j3 = (j1 + 2) % 4
    sibling = (i, j1)
    across = (i, j2)
    has_up = t < GT - 1
    has_down = t > 0
    has_near = (u + d >= 0) & (u + d < GH // 2)
    has_far = (u - d >= 0) & (u - d < GH // 2)
    near_cross = e == d
    far_cross = e == -d
    is_cross = e != 0
    is_relay = (u == 0) | (u == 7)
    has_back = (t - e >= 0) & (t - e < GT)
    has_ahead = (t + e >= 0) & (t + e < GT)
    mine = pl.multiple_of(p * HALF, 128)
    theirs = pl.multiple_of((1 - p) * HALF, 128)
    scale = HD ** (-0.5)

    @pl.when(jnp.logical_not(has_down))
    def _():
        for s in (0, 3, 6, 9):
            kv[:, pl.ds(s * T, T), :] = jnp.zeros((NH, T, 2 * HD), BF)
        rz[:, 1] = jnp.zeros((NH, 2 * T, 2 * HD), BF)

    @pl.when(jnp.logical_not(has_up))
    def _():
        for s in (2, 5, 8, 11):
            kv[:, pl.ds(s * T, T), :] = jnp.zeros((NH, T, 2 * HD), BF)
        rz[:, 0] = jnp.zeros((NH, 2 * T, 2 * HD), BF)

    for n, side, there, crossing in ((0, 0, has_near, near_cross), (1, 3, has_far, far_cross)):
        @pl.when(jnp.logical_not(there))
        def _():
            kv[:, pl.ds(side * SIDE, SIDE), :] = jnp.zeros((NH, SIDE, 2 * HD), BF)

        @pl.when(jnp.logical_not(there) | crossing)
        def _():
            rx[:, n] = jnp.zeros((NH, SIDE, 2 * HD), BF)

    barrier = pltpu.get_barrier_semaphore()
    greeted = 0
    for peer, cond in (
        (partner, None), (sibling, None), (across, None), (near, has_near), (far, has_far), (up, has_up),
        (down, has_down), (eight_off, is_cross | is_relay), (six_off, is_relay),
        (relay, is_cross), (back, is_cross & has_back),
    ):
        if cond is None:
            pl.semaphore_signal(barrier, inc=1, device_id=peer, device_id_type=MESH)
            greeted += 1
        else:
            @pl.when(cond)
            def _():
                pl.semaphore_signal(barrier, inc=1, device_id=peer, device_id_type=MESH)
            greeted += cond.astype(jnp.int32)

    pending = []

    def when(cond, action):
        if cond is None:
            action()
        else:
            @pl.when(cond)
            def _():
                action()

    def local(src, dst, n):
        copy = pltpu.make_async_copy(src, dst, lsem.at[n])
        copy.start()
        return copy

    def remote(src, dst, send, recv, device, cond=None):
        copy = pltpu.make_async_remote_copy(
            src_ref=src, dst_ref=dst, send_sem=send, recv_sem=recv, device_id=device, device_id_type=MESH
        )
        when(cond, copy.start)
        pending.append((cond, copy))

    def arrived(dst, recv, cond=None):
        copy = pltpu.make_async_remote_copy(
            src_ref=dst, dst_ref=dst, send_sem=lsem.at[0], recv_sem=recv, device_id=partner, device_id_type=MESH
        )
        when(cond, copy.wait_recv)

    def slot(h, s):
        return kv.at[h, pl.ds(s * T, T), :]

    g_copy = local(g_in, gall.at[0], 13)
    out_copies = []
    own_copies = []
    for h in range(NH):
        there = pl.multiple_of(theirs + h * HD, 128)
        here = pl.multiple_of(mine + h * HD, 128)
        out_copies.append((
            local(k_in.at[:, pl.ds(there, HD)], kvo.at[h, :, pl.ds(0, HD)], 4 * h),
            local(v_in.at[:, pl.ds(there, HD)], kvo.at[h, :, pl.ds(HD, HD)], 4 * h + 1),
        ))
        own_copies.append((
            local(k_in.at[:, pl.ds(here, HD)], kv.at[h, pl.ds(4 * T, T), pl.ds(0, HD)], 4 * h + 2),
            local(v_in.at[:, pl.ds(here, HD)], kv.at[h, pl.ds(4 * T, T), pl.ds(HD, HD)], 4 * h + 3),
        ))
    q_copy = local(q_in.at[:, pl.ds(mine, HALF)], qb.at[0], 12)
    qo_copy = local(q_in.at[:, pl.ds(theirs, HALF)], qo, 16)
    wo_copy = local(w_in.at[:, pl.ds(theirs, HALF)], wo, 14)
    wm_copy = local(w_in.at[:, pl.ds(mine, HALF)], wm, 15)

    lanes = lax.broadcasted_iota(jnp.int32, (1, WIN), 1)
    for a in range(2):
        row = jnp.zeros((1, WIN), F32)
        for n in range(9):
            g_slot, t_slot = a + n // 3, n % 3
            t_abs = t + t_slot - 1
            g_abs = g + (g_slot - 1) * (1 - 2 * p)
            if t_slot == 1 and g_slot == a + 1:
                value = jnp.float32(0.0)
            else:
                flag = valid[((t_abs + GT) % GT) * GH + (g_abs + GH) % GH]
                inside = (t_abs >= 0) & (t_abs < GT) & (g_abs >= 0) & (g_abs < GH)
                value = jnp.where(inside & (flag > 0), 0.0, -jnp.inf).astype(F32)
            row = jnp.where((lanes >= n * T) & (lanes < (n + 1) * T), value, row)
        bias[a] = row

    pl.semaphore_wait(barrier, greeted)

    def send_side(h, s, target, n, device, there, crossing):
        tile = slot(h, s)
        remote(tile, slot(h, target), fs.at[h, n], fr.at[h, target], device, there & jnp.logical_not(crossing))
        remote(tile, rb.at[h], rls.at[h, 0], rlr.at[h, 0], relay, crossing)
        remote(
            tile, slot(h, target + e), fs.at[h, n + 1], fr.at[h, target + e], back, crossing & has_back
        )

    def send_own(h):
        for copy in own_copies[h]:
            copy.wait()
        own = slot(h, 4)
        remote(own, slot(h, 3), fs.at[h, 0], fr.at[h, 3], up, has_up)
        remote(own, slot(h, 5), fs.at[h, 1], fr.at[h, 5], down, has_down)
        send_side(h, 4, 10, 2, near, has_near, near_cross)

    def send_other(h):
        arrived(slot(h, 7), fr.at[h, 7])
        other = slot(h, 7)
        remote(other, slot(h, 6), fs.at[h, 4], fr.at[h, 6], up, has_up)
        remote(other, slot(h, 8), fs.at[h, 5], fr.at[h, 8], down, has_down)
        send_side(h, 7, 1, 6, far, has_far, far_cross)

    def pass_on(h):
        arrived(rb.at[h], rlr.at[h, 0], is_relay)
        target = jnp.where((u == 0) == (p == 1), 10, 1)
        remote(rb.at[h], slot(h, target), rls.at[h, 1], fr.at[h, target], relay_to, is_relay)

    def forward(h):
        for n, (s, target, device, there, crossing, exists, way) in enumerate((
            (3, 9, near, has_near, near_cross, has_down, 1),
            (5, 11, near, has_near, near_cross, has_up, -1),
            (6, 0, far, has_far, far_cross, has_down, 1),
            (8, 2, far, has_far, far_cross, has_up, -1),
        )):
            arrived(slot(h, s), fr.at[h, s], exists)
            remote(
                slot(h, s), slot(h, target), fs.at[h, 8 + n], fr.at[h, target], device,
                exists & there & (jnp.logical_not(crossing) | (e == way)),
            )

    def cols(h):
        return pl.ds(h * HD, HD)

    def send_back(h, n, device, there, crossing):
        remote(
            xs.at[h, n], rx.at[h, n], bxs.at[h, n, 0], bxr.at[h, n, 0], device, there & jnp.logical_not(crossing)
        )
        remote(xs.at[h, n, pl.ds(T, T)], rb2.at[h], rls.at[h, 2], rlr.at[h, 1], relay, crossing)
        rows = pl.ds((1 + e) * T, T)
        remote(
            xs.at[h, n, rows], rx.at[h, n, rows], bxs.at[h, n, 1], bxr.at[h, n, 2], device, crossing & has_ahead
        )
        remote(xs.at[h, n, pl.ds((1 - e) * T, T)], rc.at[h], bcs.at[h, n], bcr.at[h], back, crossing & has_back)

    def pass_back(h):
        arrived(rb2.at[h], rlr.at[h, 1], is_relay)
        n = jnp.where(u == 0, p, 1 - p)
        remote(rb2.at[h], rx.at[h, n, pl.ds(T, T)], rls.at[h, 3], bxr.at[h, n, 1], relay_to, is_relay)

    def attend(h):
        for s, there in ((9, has_far & has_down), (10, has_far), (11, has_far & has_up),
                         (0, has_near & has_down), (1, has_near), (2, has_near & has_up)):
            arrived(slot(h, s), fr.at[h, s], there)
        for a in range(2):
            window = pl.ds(a * SIDE, WIN)
            s = nt(qb[a, :, cols(h)], kv[h, window, pl.ds(0, HD)]) * scale + bias[a]
            x = jnp.exp(s - jnp.max(s, axis=1, keepdims=True))
            weights = (x * (1.0 / jnp.sum(x, axis=1, keepdims=True))).astype(BF)
            pb[a] = weights
            att[a, :, cols(h)] = nn(weights, kv[h, window, pl.ds(HD, HD)]).astype(BF)
        remote(att.at[1, :, cols(h)], attr.at[:, cols(h)], ats.at[h], atr.at[h], partner)

    def differentiate(h):
        for a in range(2):
            q = qb[a, :, cols(h)]
            do = dob[a, :, cols(h)]
            window = pl.ds(a * SIDE, WIN)
            k = kv[h, window, pl.ds(0, HD)]
            weights = pb[a]
            row_dot = jnp.sum(do.astype(F32) * att[a, :, cols(h)].astype(F32), axis=1, keepdims=True)
            weight_grad = nt(do, kv[h, window, pl.ds(HD, HD)])
            score_grad = (weights.astype(F32) * (weight_grad - row_dot) * scale).astype(BF)
            dqb[a, :, cols(h)] = nn(score_grad, k).astype(BF)
            for part, lhs, rhs in ((0, score_grad, q), (1, weights, do)):
                grad = tn(lhs, rhs)
                lane = pl.ds(part * HD, HD)
                if a == 0:
                    xs[h, 1, :, lane] = grad[:SIDE].astype(BF)
                    acc[h, :, lane] = grad[SIDE:]
                else:
                    acc[h, :, lane] += grad[:2 * SIDE]
                    xs[h, 0, :, lane] = grad[2 * SIDE:].astype(BF)
            if a == 0:
                send_back(h, 1, near, has_near, near_cross)
            else:
                send_back(h, 0, far, has_far, far_cross)
        here = pl.multiple_of(mine + h * HD, 128)
        remote(dqb.at[1, :, cols(h)], dq_out.at[:, pl.ds(here, HD)], qs.at[1 + h], qr.at[1 + h], partner)

    def reduce_x(h):
        pass_back(h)
        for n, there, crossing in ((0, has_near, near_cross), (1, has_far, far_cross)):
            arrived(rx.at[h, n], bxr.at[h, n, 0], there & jnp.logical_not(crossing))
            arrived(rx.at[h, n, pl.ds(T, T)], bxr.at[h, n, 1], crossing)
            arrived(rx.at[h, n, pl.ds((1 - e) * T, T)], bxr.at[h, n, 2], crossing & has_back)
            for part, row in ((0, 0), (1, 2 * T)):
                zs[h, part, pl.ds(n * T, T), :] = (
                    acc[h, pl.ds(n * SIDE + row, T), :] + rx[h, n, pl.ds(row, T), :].astype(F32)
                ).astype(BF)
            acc[h, pl.ds(n * SIDE + T, T), :] += rx[h, n, pl.ds(T, T), :].astype(F32)
        remote(zs.at[h, 0], rz.at[h, 0], bzs.at[h, 0], bzr.at[h, 0], down, has_down)
        remote(zs.at[h, 1], rz.at[h, 1], bzs.at[h, 1], bzr.at[h, 1], up, has_up)

    def reduce_z(h):
        arrived(rz.at[h, 0], bzr.at[h, 0], has_up)
        arrived(rz.at[h, 1], bzr.at[h, 1], has_down)
        arrived(rc.at[h], bcr.at[h], is_cross & has_back)
        for n, crossing in ((0, near_cross), (1, far_cross)):
            @pl.when(crossing & has_back)
            def _():
                acc[h, pl.ds(n * SIDE + T, T), :] += rc[h].astype(F32)

        for n, out in ((1, ys), (0, yo)):
            rows = pl.ds(n * T, T)
            out[h] = (
                acc[h, pl.ds(n * SIDE + T, T), :] + rz[h, 0, rows, :].astype(F32) + rz[h, 1, rows, :].astype(F32)
            ).astype(BF)
        here = pl.ds(pl.multiple_of(mine + h * HD, 128), HD)
        for part, out in ((0, dk_out), (1, dv_out)):
            lane = pl.ds(part * HD, HD)
            remote(ys.at[h, :, lane], out.at[:, here], bys.at[h, part], byr.at[h, part], partner)
            finals.append(local(yo.at[h, :, lane], out.at[:, here], 20 + 2 * h + part))

    finals = []

    g_copy.wait()
    remote(gall.at[0], gall.at[2], gs.at[1], gr.at[1], across)
    remote(gall.at[0], gall.at[1], gs.at[0], gr.at[0], sibling)
    for h in range(NH):
        for copy in out_copies[h]:
            copy.wait()
        remote(kvo.at[h], slot(h, 7), fs.at[h, 12], fr.at[h, 7], partner)
        if h < 2:
            send_own(h)
    qo_copy.wait()
    remote(qo, qb.at[1], qs.at[0], qr.at[0], partner)
    arrived(gall.at[2], gr.at[1])
    remote(gall.at[2], gall.at[3], gs.at[2], gr.at[2], sibling)
    send_other(0)
    send_own(2)
    pass_on(0)

    wo_copy.wait()
    wm_copy.wait()
    arrived(gall.at[1], gr.at[0])
    arrived(gall.at[3], gr.at[2])
    blocks = (j, j1, j2, j3)
    rows = [pl.ds(pl.multiple_of(block * FULL, FULL), FULL) for block in blocks]
    total = nn(gall[0], wo[rows[0], :])
    for n in range(1, 4):
        total = total + nn(gall[n], wo[rows[n], :])
    dop[...] = total.astype(BF)
    remote(dop, dob.at[1], qs.at[4], qr.at[4], partner)
    send_other(1)
    pass_on(1)
    total = nn(gall[0], wm[rows[0], :])
    for n in range(1, 4):
        total = total + nn(gall[n], wm[rows[n], :])
    dob[0] = total.astype(BF)
    forward(0)
    send_other(2)
    pass_on(2)
    q_copy.wait()
    arrived(qb.at[1], qr.at[0])

    forward(1)
    attend(0)
    arrived(dob.at[1], qr.at[4])
    differentiate(0)
    forward(2)
    attend(1)
    differentiate(1)
    reduce_x(0)
    attend(2)
    differentiate(2)
    finals.append(local(dqb.at[0], dq_out.at[:, pl.ds(mine, HALF)], 26))
    reduce_x(1)
    reduce_z(0)

    for h in range(NH):
        arrived(attr.at[:, cols(h)], atr.at[h])

    def project(n):
        return nt(att[0], wm[rows[n], :]) + nt(attr[...], wo[rows[n], :])

    ms[0] = project(3).astype(BF)
    ms[1] = project(1).astype(BF)
    remote(ms, mr, mss.at[0], msr.at[0], sibling)
    reduce_x(2)
    crossing = project(2)
    arrived(mr, msr.at[0])
    ms2[...] = (crossing + mr[0].astype(F32)).astype(BF)
    remote(ms2, mr2, mss.at[1], msr.at[1], across)
    kept = project(0) + mr[1].astype(F32)
    reduce_z(1)
    arrived(mr2, msr.at[1])
    mo[...] = (kept + mr2[...].astype(F32)).astype(BF)
    finals.append(local(mo, mixed, 27))
    reduce_z(2)

    for h in range(NH):
        there = pl.ds(pl.multiple_of(theirs + h * HD, 128), HD)
        arrived(dq_out.at[:, there], qr.at[1 + h])
        arrived(dk_out.at[:, there], byr.at[h, 0])
        arrived(dv_out.at[:, there], byr.at[h, 1])
    for copy in finals:
        copy.wait()
    for cond, copy in pending:
        when(cond, copy.wait_send)


def hand_over(*refs):
    for n in range(4):
        refs[4 + n][...] = refs[n][...]


def on_device(queries, keys, values, w_out, out_grad, tile_valid):
    dma = pltpu.SemaphoreType.DMA
    any_space = pl.BlockSpec(memory_space=pl.ANY)
    block = jax.ShapeDtypeStruct(queries.shape, BF)
    results = pl.pallas_call(
        kernel,
        out_shape=(block, block, block, block),
        in_specs=[any_space] * 5 + [pl.BlockSpec(memory_space=pltpu.SMEM)],
        out_specs=(any_space, any_space, any_space, any_space),
        scratch_shapes=[
            pltpu.VMEM((NH, 12 * T, 2 * HD), BF),
            pltpu.VMEM((NH, T, 2 * HD), BF),
            pltpu.VMEM((2, T, HALF), BF),
            pltpu.VMEM((2, T, HALF), BF),
            pltpu.VMEM((T, HALF), BF),
            pltpu.VMEM((4, T, FULL), BF),
            pltpu.VMEM((4 * FULL, HALF), BF),
            pltpu.VMEM((4 * FULL, HALF), BF),
            pltpu.VMEM((2, T, HALF), BF),
            pltpu.VMEM((T, HALF), BF),
            pltpu.VMEM((2, T, HALF), BF),
            pltpu.VMEM((2, 1, WIN), F32),
            pltpu.VMEM((NH, 2, SIDE, 2 * HD), BF),
            pltpu.VMEM((NH, 2, SIDE, 2 * HD), BF),
            pltpu.VMEM((NH, 2 * SIDE, 2 * HD), F32),
            pltpu.VMEM((NH, 2, 2 * T, 2 * HD), BF),
            pltpu.VMEM((NH, 2, 2 * T, 2 * HD), BF),
            pltpu.VMEM((NH, T, 2 * HD), BF),
            pltpu.VMEM((NH, T, 2 * HD), BF),
            pltpu.VMEM((2, T, FULL), BF),
            pltpu.VMEM((2, T, FULL), BF),
            pltpu.VMEM((T, FULL), BF),
            pltpu.VMEM((T, FULL), BF),
            pltpu.VMEM((T, FULL), BF),
            pltpu.VMEM((NH, T, 2 * HD), BF),
            pltpu.VMEM((NH, T, 2 * HD), BF),
            pltpu.VMEM((NH, T, 2 * HD), BF),
            pltpu.VMEM((2, T, WIN), BF),
            pltpu.VMEM((T, HALF), BF),
            dma((28,)),
            dma((NH, 13)),
            dma((NH, 12)),
            dma((NH, 2, 2)),
            dma((NH, 2, 3)),
            dma((NH, 2)),
            dma((NH, 2)),
            dma((NH, 2)),
            dma((NH, 2)),
            dma((3,)),
            dma((3,)),
            dma((5,)),
            dma((5,)),
            dma((NH,)),
            dma((NH,)),
            dma((2,)),
            dma((2,)),
            dma((NH, 4)),
            dma((NH, 2)),
            dma((NH, 2)),
            dma((NH,)),
        ],
        compiler_params=pltpu.CompilerParams(
            collective_id=0, has_side_effects=True, vmem_limit_bytes=56 * 1024 * 1024
        ),
    )(queries, keys, values, w_out, out_grad, tile_valid)
    whole = pl.BlockSpec(memory_space=pltpu.VMEM)
    return pl.pallas_call(
        hand_over,
        out_shape=(block, block, block, block),
        in_specs=[whole] * 4,
        out_specs=(whole, whole, whole, whole),
    )(*results)


def solution(mesh):
    return jax.shard_map(
        on_device,
        mesh=mesh,
        in_specs=(
            P("tile", "head"),
            P("tile", "head"),
            P("tile", "head"),
            P(None, "head"),
            P("tile", "head"),
            P(),
        ),
        out_specs=(P("tile", "head"), P("tile", "head"), P("tile", "head"), P("tile", "head")),
        check_vma=False,
    )
```

```python
import jax
import jax.numpy as jnp
from jax import lax
from jax.experimental import pallas as pl
from jax.experimental.pallas import tpu as pltpu
from jax.sharding import PartitionSpec as P

HD = 128
GT = 4
GH = 16
T = 160
NH = 3
HALF = NH * HD
FULL = 2 * HALF
WIN = 9 * T
SIDE = 3 * T
MESH = pl.DeviceIdType.MESH
BF = jnp.bfloat16
F32 = jnp.float32


def nt(a, b):
    return lax.dot_general(a, b, (((1,), (1,)), ((), ())), preferred_element_type=F32)


def nn(a, b):
    return lax.dot_general(a, b, (((1,), (0,)), ((), ())), preferred_element_type=F32)


def tn(a, b):
    return lax.dot_general(a, b, (((0,), (0,)), ((), ())), preferred_element_type=F32)


def kernel(
    q_in, k_in, v_in, w_in, g_in, valid,
    mixed, dq_out, dk_out, dv_out,
    kv, kvo, qo, qb, dob, dop, gall, wm, wo, att, attr, dqb, pb, bias,
    xs, rx, acc, zs, rz, ys, ms, mr, ms2, mr2, mo, rb, rb2, rc,
    lsem, hsem, fs, fr, bxs, bxr, bzs, bzr, bys, byr, gs, gr, qs, qr, dqs, dqr, ats, atr, mss, msr, rls, rlr, bcs, bcr,
):
    i = lax.axis_index("tile")
    j = lax.axis_index("head")
    t = i // GH
    g = i % GH
    p = g % 2
    u = g // 2
    d = 2 * p - 1
    e = (u == 3).astype(jnp.int32) - (u == 4).astype(jnp.int32)
    partner = (i + 1 - 2 * p, j)
    near = (t * GH + (g + 2 * d + GH) % GH, j)
    far = (t * GH + (g - 2 * d + GH) % GH, j)
    up = (((t + 1) % GT) * GH + g, j)
    down = (((t + GT - 1) % GT) * GH + g, j)
    eight_off = (t * GH + (g + GH // 2) % GH, j)
    six_off = (t * GH + (g + 6 + 4 * (u == 7).astype(jnp.int32)) % GH, j)
    relay = (t * GH + (g + GH - 6 * e) % GH, j)
    relay_to = eight_off
    back = (((t - e + GT) % GT) * GH + (g + 2 * e), j)
    j1 = j + 1 - 2 * (j % 2)
    j2 = (j + 2) % 4
    j3 = (j1 + 2) % 4
    sibling = (i, j1)
    across = (i, j2)
    has_up = t < GT - 1
    has_down = t > 0
    has_near = (u + d >= 0) & (u + d < GH // 2)
    has_far = (u - d >= 0) & (u - d < GH // 2)
    near_cross = e == d
    far_cross = e == -d
    is_cross = e != 0
    is_relay = (u == 0) | (u == 7)
    has_back = (t - e >= 0) & (t - e < GT)
    has_ahead = (t + e >= 0) & (t + e < GT)
    mine = pl.multiple_of(p * HALF, 128)
    theirs = pl.multiple_of((1 - p) * HALF, 128)
    scale = HD ** (-0.5)

    @pl.when(jnp.logical_not(has_down))
    def _():
        for s in (0, 3, 6, 9):
            kv[:, pl.ds(s * T, T), :] = jnp.zeros((NH, T, 2 * HD), BF)
        rz[:, 1] = jnp.zeros((NH, 2 * T, 2 * HD), BF)

    @pl.when(jnp.logical_not(has_up))
    def _():
        for s in (2, 5, 8, 11):
            kv[:, pl.ds(s * T, T), :] = jnp.zeros((NH, T, 2 * HD), BF)
        rz[:, 0] = jnp.zeros((NH, 2 * T, 2 * HD), BF)

    for n, side, there, crossing in ((0, 0, has_near, near_cross), (1, 3, has_far, far_cross)):
        @pl.when(jnp.logical_not(there))
        def _():
            kv[:, pl.ds(side * SIDE, SIDE), :] = jnp.zeros((NH, SIDE, 2 * HD), BF)

        @pl.when(jnp.logical_not(there) | crossing)
        def _():
            rx[:, n] = jnp.zeros((NH, SIDE, 2 * HD), BF)

    barrier = pltpu.get_barrier_semaphore()
    greeted = 0
    for peer, cond in (
        (partner, None), (sibling, None), (across, None), (near, has_near), (far, has_far), (up, has_up),
        (down, has_down), (eight_off, is_cross | is_relay), (six_off, is_relay),
        (relay, is_cross), (back, is_cross & has_back),
    ):
        if cond is None:
            pl.semaphore_signal(barrier, inc=1, device_id=peer, device_id_type=MESH)
            greeted += 1
        else:
            @pl.when(cond)
            def _():
                pl.semaphore_signal(barrier, inc=1, device_id=peer, device_id_type=MESH)
            greeted += cond.astype(jnp.int32)

    START, WAIT = 0, 1

    def when(cond, action):
        if cond is None:
            action()
        else:
            @pl.when(cond)
            def _():
                action()

    def remote(act, src, dst, send, recv, device, cond=None):
        copy = pltpu.make_async_remote_copy(
            src_ref=src, dst_ref=dst, send_sem=send, recv_sem=recv, device_id=device, device_id_type=MESH
        )
        when(cond, copy.start if act == START else copy.wait_send)

    def arrived(dst, recv, cond=None):
        copy = pltpu.make_async_remote_copy(
            src_ref=dst, dst_ref=dst, send_sem=lsem.at[0], recv_sem=recv, device_id=partner, device_id_type=MESH
        )
        when(cond, copy.wait_recv)

    def slot(h, s):
        return kv.at[h, pl.ds(s * T, T), :]

    def cols(h):
        return pl.ds(pl.multiple_of(h * HD, HD), HD)

    def mine_cols(h):
        return pl.ds(pl.multiple_of(mine + h * HD, HD), HD)

    def their_cols(h):
        return pl.ds(pl.multiple_of(theirs + h * HD, HD), HD)

    def local(src, dst, sem):
        copy = pltpu.make_async_copy(src, dst, sem)
        copy.start()
        return copy

    staged = [
        [
            local(k_in.at[:, their_cols(h)], kvo.at[h, :, pl.ds(0, HD)], hsem.at[h, 0]),
            local(v_in.at[:, their_cols(h)], kvo.at[h, :, pl.ds(HD, HD)], hsem.at[h, 1]),
        ]
        for h in range(NH)
    ]
    kept_tiles = [
        [
            local(k_in.at[:, mine_cols(h)], slot(h, 4).at[:, pl.ds(0, HD)], hsem.at[h, 2]),
            local(v_in.at[:, mine_cols(h)], slot(h, 4).at[:, pl.ds(HD, HD)], hsem.at[h, 3]),
        ]
        for h in range(NH)
    ]
    g_copy = local(g_in, gall.at[0], lsem.at[0])
    q_copy = local(q_in.at[:, pl.ds(mine, HALF)], qb.at[0], lsem.at[1])
    qo_copy = local(q_in.at[:, pl.ds(theirs, HALF)], qo, lsem.at[2])
    w_copies = [
        local(w_in.at[:, pl.ds(theirs, HALF)], wo, lsem.at[3]),
        local(w_in.at[:, pl.ds(mine, HALF)], wm, lsem.at[4]),
    ]

    lanes = lax.broadcasted_iota(jnp.int32, (1, WIN), 1)
    for a in range(2):
        row = jnp.zeros((1, WIN), F32)
        for n in range(9):
            g_slot, t_slot = a + n // 3, n % 3
            t_abs = t + t_slot - 1
            g_abs = g + (g_slot - 1) * (1 - 2 * p)
            if t_slot == 1 and g_slot == a + 1:
                value = jnp.float32(0.0)
            else:
                flag = valid[((t_abs + GT) % GT) * GH + (g_abs + GH) % GH]
                inside = (t_abs >= 0) & (t_abs < GT) & (g_abs >= 0) & (g_abs < GH)
                value = jnp.where(inside & (flag > 0), 0.0, -jnp.inf).astype(F32)
            row = jnp.where((lanes >= n * T) & (lanes < (n + 1) * T), value, row)
        bias[a] = row

    pl.semaphore_wait(barrier, greeted)

    def send_side(act, h, s, target, n, device, there, crossing):
        tile = slot(h, s)
        remote(act, tile, slot(h, target), fs.at[h, n], fr.at[h, target], device, there & jnp.logical_not(crossing))
        remote(act, tile, rb.at[h], rls.at[h, 0], rlr.at[h, 0], relay, crossing)
        remote(
            act, tile, slot(h, target + e), fs.at[h, n + 1], fr.at[h, target + e], back, crossing & has_back
        )

    def send_swap(act, h):
        remote(act, kvo.at[h], slot(h, 7), fs.at[h, 12], fr.at[h, 7], partner)

    def send_z(act, h, s):
        remote(act, slot(h, s), slot(h, s - 1), fs.at[h, 0 if s == 4 else 2], fr.at[h, s - 1], up, has_up)
        remote(act, slot(h, s), slot(h, s + 1), fs.at[h, 1 if s == 4 else 3], fr.at[h, s + 1], down, has_down)

    def send_own_x(act, h):
        send_side(act, h, 4, 10, 4, near, has_near, near_cross)

    def send_other_x(act, h):
        send_side(act, h, 7, 1, 6, far, has_far, far_cross)

    def pass_on(act, h):
        target = jnp.where((u == 0) == (p == 1), 10, 1)
        remote(act, rb.at[h], slot(h, target), rls.at[h, 1], fr.at[h, target], relay_to, is_relay)

    def forward(act, h, n, k):
        target, device, there, crossing = ((9, near, has_near, near_cross), (0, far, has_far, far_cross))[n]
        exists, way = ((has_down, 1), (has_up, -1))[k]
        source = slot(h, 3 + 3 * n + 2 * k)
        if act == START:
            arrived(source, fr.at[h, 3 + 3 * n + 2 * k], exists)
        remote(
            act, source, slot(h, target + 2 * k), fs.at[h, 8 + 2 * n + k], fr.at[h, target + 2 * k], device,
            exists & there & (jnp.logical_not(crossing) | (e == way)),
        )

    def send_back(act, h, n):
        device, there, crossing = ((far, has_far, far_cross), (near, has_near, near_cross))[n]
        remote(
            act, xs.at[h, n], rx.at[h, n], bxs.at[h, n, 0], bxr.at[h, n, 0], device,
            there & jnp.logical_not(crossing),
        )
        remote(act, xs.at[h, n, pl.ds(T, T)], rb2.at[h], rls.at[h, 2], rlr.at[h, 1], relay, crossing)
        rows = pl.ds((1 + e) * T, T)
        remote(
            act, xs.at[h, n, rows], rx.at[h, n, rows], bxs.at[h, n, 1], bxr.at[h, n, 2], device, crossing & has_ahead
        )
        remote(
            act, xs.at[h, n, pl.ds((1 - e) * T, T)], rc.at[h], bcs.at[h, n], bcr.at[h], back, crossing & has_back
        )

    def pass_back(act, h):
        n = jnp.where(u == 0, p, 1 - p)
        remote(act, rb2.at[h], rx.at[h, n, pl.ds(T, T)], rls.at[h, 3], bxr.at[h, n, 1], relay_to, is_relay)

    def send_attended(act, h):
        remote(act, att.at[1, :, cols(h)], attr.at[:, cols(h)], ats.at[h], atr.at[h], partner)

    def send_query_grad(act, h):
        remote(act, dqb.at[1, :, cols(h)], dq_out.at[:, mine_cols(h)], dqs.at[h], dqr.at[h], partner)
        copy = pltpu.make_async_copy(dqb.at[0, :, cols(h)], dq_out.at[:, mine_cols(h)], hsem.at[h, 2])
        if act == START:
            copy.start()
        else:
            copy.wait()

    def send_reduced(act, h):
        remote(act, zs.at[h, 0], rz.at[h, 0], bzs.at[h, 0], bzr.at[h, 0], down, has_down)
        remote(act, zs.at[h, 1], rz.at[h, 1], bzs.at[h, 1], bzr.at[h, 1], up, has_up)

    def send_total(act, h):
        for part, out in enumerate((dk_out, dv_out)):
            lane = pl.ds(part * HD, HD)
            remote(act, ys.at[h, 1, :, lane], out.at[:, mine_cols(h)], bys.at[h, part], byr.at[h, part], partner)
            copy = pltpu.make_async_copy(ys.at[h, 0, :, lane], out.at[:, mine_cols(h)], hsem.at[h, part])
            if act == START:
                copy.start()
            else:
                copy.wait()

    def attend(h):
        for s, there in ((9, has_far & has_down), (10, has_far), (11, has_far & has_up),
                         (0, has_near & has_down), (1, has_near), (2, has_near & has_up)):
            arrived(slot(h, s), fr.at[h, s], there)
        for a in range(2):
            window = pl.ds(a * SIDE, WIN)
            s = nt(qb[a, :, cols(h)], kv[h, window, pl.ds(0, HD)]) * scale + bias[a]
            x = jnp.exp(s - jnp.max(s, axis=1, keepdims=True))
            weights = (x * (1.0 / jnp.sum(x, axis=1, keepdims=True))).astype(BF)
            pb[a] = weights
            att[a, :, cols(h)] = nn(weights, kv[h, window, pl.ds(HD, HD)]).astype(BF)
        send_attended(START, h)

    def differentiate(h, a):
        q = qb[a, :, cols(h)]
        do = dob[a, :, cols(h)]
        window = pl.ds(a * SIDE, WIN)
        k = kv[h, window, pl.ds(0, HD)]
        weights = pb[a]
        row_dot = jnp.sum(do.astype(F32) * att[a, :, cols(h)].astype(F32), axis=1, keepdims=True)
        weight_grad = nt(do, kv[h, window, pl.ds(HD, HD)])
        score_grad = (weights.astype(F32) * (weight_grad - row_dot) * scale).astype(BF)
        dqb[a, :, cols(h)] = nn(score_grad, k).astype(BF)
        for part, lhs, rhs in ((0, score_grad, q), (1, weights, do)):
            grad = tn(lhs, rhs)
            lane = pl.ds(part * HD, HD)
            if a == 0:
                xs[h, 1, :, lane] = grad[:SIDE].astype(BF)
                acc[h, :, lane] = grad[SIDE:]
            else:
                acc[h, :, lane] += grad[:2 * SIDE]
                xs[h, 0, :, lane] = grad[2 * SIDE:].astype(BF)
        send_back(START, h, 1 - a)
        if a == 1:
            send_query_grad(START, h)

    def reduce_x(h):
        for n, there, crossing in ((0, has_near, near_cross), (1, has_far, far_cross)):
            arrived(rx.at[h, n], bxr.at[h, n, 0], there & jnp.logical_not(crossing))
            arrived(rx.at[h, n, pl.ds(T, T)], bxr.at[h, n, 1], crossing)
            arrived(rx.at[h, n, pl.ds((1 - e) * T, T)], bxr.at[h, n, 2], crossing & has_back)
        for n in range(2):
            for part, row in ((0, 0), (1, 2 * T)):
                zs[h, part, pl.ds(n * T, T), :] = (
                    acc[h, pl.ds(n * SIDE + row, T), :] + rx[h, n, pl.ds(row, T), :].astype(F32)
                ).astype(BF)
            acc[h, pl.ds(n * SIDE + T, T), :] += rx[h, n, pl.ds(T, T), :].astype(F32)
        send_reduced(START, h)

    def reduce_z(h):
        arrived(rz.at[h, 0], bzr.at[h, 0], has_up)
        arrived(rz.at[h, 1], bzr.at[h, 1], has_down)
        arrived(rc.at[h], bcr.at[h], is_cross & has_back)
        for n, crossing in ((0, near_cross), (1, far_cross)):
            @pl.when(crossing & has_back)
            def _():
                acc[h, pl.ds(n * SIDE + T, T), :] += rc[h].astype(F32)

        for n in range(2):
            rows = pl.ds(n * T, T)
            ys[h, n] = (
                acc[h, pl.ds(n * SIDE + T, T), :] + rz[h, 0, rows, :].astype(F32) + rz[h, 1, rows, :].astype(F32)
            ).astype(BF)
        send_total(START, h)

    blocks = (j, j1, j2, j3)
    rows = [pl.ds(pl.multiple_of(block * FULL, FULL), FULL) for block in blocks]

    def attn_grad(weights_ref):
        total = nn(gall[0], weights_ref[rows[0], :])
        for n in range(1, 4):
            total = total + nn(gall[n], weights_ref[rows[n], :])
        return total.astype(BF)

    blocks = (j, j1, j2, j3)
    rows = [pl.ds(pl.multiple_of(block * FULL, FULL), FULL) for block in blocks]

    def send_gathered(act, n):
        source, target, device, k = ((0, 2, across, 1), (0, 1, sibling, 0), (2, 3, sibling, 2))[n]
        remote(act, gall.at[source], gall.at[target], gs.at[k], gr.at[k], device)

    def send_queries(act):
        remote(act, qo, qb.at[1], qs.at[0], qr.at[0], partner)

    def attn_grad(weights_ref):
        total = nn(gall[0], weights_ref[rows[0], :])
        for k in range(1, 4):
            total = total + nn(gall[k], weights_ref[rows[k], :])
        return total.astype(BF)

    def send_attn_grad(act):
        remote(act, dop, dob.at[1], qs.at[1], qr.at[1], partner)

    def project(n):
        return nt(att[0], wm[rows[n], :]) + nt(attr[...], wo[rows[n], :])

    for copy in staged[0]:
        copy.wait()
    send_swap(START, 0)
    for copy in kept_tiles[0]:
        copy.wait()
    send_z(START, 0, 4)
    for copy in staged[1]:
        copy.wait()
    send_swap(START, 1)
    arrived(slot(0, 7), fr.at[0, 7])
    send_z(START, 0, 7)
    for copy in kept_tiles[1]:
        copy.wait()
    send_z(START, 1, 4)
    g_copy.wait()
    send_gathered(START, 0)
    send_own_x(START, 0)
    arrived(gall.at[2], gr.at[1])
    send_gathered(START, 2)
    arrived(slot(1, 7), fr.at[1, 7])
    send_z(START, 1, 7)
    forward(START, 0, 1, 0)
    for copy in staged[2]:
        copy.wait()
    send_swap(START, 2)
    forward(START, 0, 0, 0)
    send_gathered(START, 1)
    arrived(rb.at[0], rlr.at[0, 0], is_relay)
    pass_on(START, 0)
    forward(START, 0, 0, 1)
    send_other_x(START, 0)
    qo_copy.wait()
    send_queries(START)
    forward(START, 0, 1, 1)
    send_own_x(START, 1)
    forward(START, 1, 0, 0)
    for copy in w_copies:
        copy.wait()
    arrived(gall.at[1], gr.at[0])
    arrived(gall.at[3], gr.at[2])
    dop[...] = attn_grad(wo)
    send_attn_grad(START)
    dob[0] = attn_grad(wm)
    arrived(slot(2, 7), fr.at[2, 7])
    send_z(START, 2, 7)
    for copy in kept_tiles[2]:
        copy.wait()
    send_z(START, 2, 4)
    arrived(rb.at[1], rlr.at[1, 0], is_relay)
    pass_on(START, 1)
    send_other_x(START, 1)
    send_own_x(START, 2)
    forward(START, 1, 0, 1)
    send_other_x(START, 2)
    q_copy.wait()
    arrived(qb.at[1], qr.at[0])
    attend(0)
    forward(START, 1, 1, 1)
    forward(START, 1, 1, 0)
    arrived(dob.at[1], qr.at[1])
    differentiate(0, 0)
    differentiate(0, 1)
    forward(START, 2, 0, 0)
    arrived(rb2.at[0], rlr.at[0, 1], is_relay)
    pass_back(START, 0)
    forward(START, 2, 1, 0)
    attend(1)
    arrived(rb.at[2], rlr.at[2, 0], is_relay)
    pass_on(START, 2)
    forward(START, 2, 0, 1)
    forward(START, 2, 1, 1)
    differentiate(1, 0)
    differentiate(1, 1)
    reduce_x(0)
    arrived(rb2.at[1], rlr.at[1, 1], is_relay)
    pass_back(START, 1)
    attend(2)
    differentiate(2, 0)
    differentiate(2, 1)
    reduce_x(1)
    arrived(rb2.at[2], rlr.at[2, 1], is_relay)
    pass_back(START, 2)
    for h in range(NH):
        arrived(attr.at[:, cols(h)], atr.at[h])
    ms[0] = project(3).astype(BF)
    ms[1] = project(1).astype(BF)
    remote(START, ms, mr, mss.at[0], msr.at[0], sibling)
    crossing_sum = project(2)
    arrived(mr, msr.at[0])
    ms2[...] = (crossing_sum + mr[0].astype(F32)).astype(BF)
    remote(START, ms2, mr2, mss.at[1], msr.at[1], across)
    kept = project(0) + mr[1].astype(F32)
    reduce_x(2)
    reduce_z(0)
    reduce_z(1)
    reduce_z(2)
    arrived(mr2, msr.at[1])
    mo[...] = (kept + mr2[...].astype(F32)).astype(BF)
    mixed_copy = local(mo, mixed, lsem.at[5])
    send_z(WAIT, 0, 4)
    send_z(WAIT, 0, 7)
    send_z(WAIT, 1, 4)
    send_z(WAIT, 1, 7)
    send_z(WAIT, 2, 4)
    send_z(WAIT, 2, 7)

    for n in range(3):
        send_gathered(WAIT, n)
    send_queries(WAIT)
    send_attn_grad(WAIT)
    remote(WAIT, ms, mr, mss.at[0], msr.at[0], sibling)
    remote(WAIT, ms2, mr2, mss.at[1], msr.at[1], across)
    for h in range(NH):
        for send in (
            send_swap, send_own_x, send_other_x, pass_on, pass_back, send_attended, send_query_grad, send_reduced,
            send_total,
        ):
            send(WAIT, h)
        for n in range(2):
            forward(WAIT, h, n, 0)
            forward(WAIT, h, n, 1)
            send_back(WAIT, h, n)
        arrived(dq_out.at[:, their_cols(h)], dqr.at[h])
        arrived(dk_out.at[:, their_cols(h)], byr.at[h, 0])
        arrived(dv_out.at[:, their_cols(h)], byr.at[h, 1])
    mixed_copy.wait()

def hand_over(*refs):
    for n in range(4):
        refs[4 + n][...] = refs[n][...]


def on_device(queries, keys, values, w_out, out_grad, tile_valid):
    dma = pltpu.SemaphoreType.DMA
    any_space = pl.BlockSpec(memory_space=pl.ANY)
    block = jax.ShapeDtypeStruct(queries.shape, BF)
    results = pl.pallas_call(
        kernel,
        out_shape=(block, block, block, block),
        in_specs=[any_space] * 5 + [pl.BlockSpec(memory_space=pltpu.SMEM)],
        out_specs=(any_space, any_space, any_space, any_space),
        scratch_shapes=[
            pltpu.VMEM((NH, 12 * T, 2 * HD), BF),
            pltpu.VMEM((NH, T, 2 * HD), BF),
            pltpu.VMEM((T, HALF), BF),
            pltpu.VMEM((2, T, HALF), BF),
            pltpu.VMEM((2, T, HALF), BF),
            pltpu.VMEM((T, HALF), BF),
            pltpu.VMEM((4, T, FULL), BF),
            pltpu.VMEM((4 * FULL, HALF), BF),
            pltpu.VMEM((4 * FULL, HALF), BF),
            pltpu.VMEM((2, T, HALF), BF),
            pltpu.VMEM((T, HALF), BF),
            pltpu.VMEM((2, T, HALF), BF),
            pltpu.VMEM((2, T, WIN), BF),
            pltpu.VMEM((2, 1, WIN), F32),
            pltpu.VMEM((NH, 2, SIDE, 2 * HD), BF),
            pltpu.VMEM((NH, 2, SIDE, 2 * HD), BF),
            pltpu.VMEM((NH, 2 * SIDE, 2 * HD), F32),
            pltpu.VMEM((NH, 2, 2 * T, 2 * HD), BF),
            pltpu.VMEM((NH, 2, 2 * T, 2 * HD), BF),
            pltpu.VMEM((NH, 2, T, 2 * HD), BF),
            pltpu.VMEM((2, T, FULL), BF),
            pltpu.VMEM((2, T, FULL), BF),
            pltpu.VMEM((T, FULL), BF),
            pltpu.VMEM((T, FULL), BF),
            pltpu.VMEM((T, FULL), BF),
            pltpu.VMEM((NH, T, 2 * HD), BF),
            pltpu.VMEM((NH, T, 2 * HD), BF),
            pltpu.VMEM((NH, T, 2 * HD), BF),
            dma((6,)),
            dma((NH, 4)),
            dma((NH, 14)),
            dma((NH, 12)),
            dma((NH, 2, 2)),
            dma((NH, 2, 3)),
            dma((NH, 2)),
            dma((NH, 2)),
            dma((NH, 2)),
            dma((NH, 2)),
            dma((3,)),
            dma((3,)),
            dma((2,)),
            dma((2,)),
            dma((NH,)),
            dma((NH,)),
            dma((NH,)),
            dma((NH,)),
            dma((2,)),
            dma((2,)),
            dma((NH, 4)),
            dma((NH, 2)),
            dma((NH, 2)),
            dma((NH,)),
        ],
        compiler_params=pltpu.CompilerParams(
            collective_id=0, has_side_effects=True, vmem_limit_bytes=56 * 1024 * 1024
        ),
    )(queries, keys, values, w_out, out_grad, tile_valid)
    whole = pl.BlockSpec(memory_space=pltpu.VMEM)
    return pl.pallas_call(
        hand_over,
        out_shape=(block, block, block, block),
        in_specs=[whole] * 4,
        out_specs=(whole, whole, whole, whole),
    )(*results)


def solution(mesh):
    return jax.shard_map(
        on_device,
        mesh=mesh,
        in_specs=(
            P("tile", "head"),
            P("tile", "head"),
            P("tile", "head"),
            P(None, "head"),
            P("tile", "head"),
            P(),
        ),
        out_specs=(P("tile", "head"), P("tile", "head"), P("tile", "head"), P("tile", "head")),
        check_vma=False,
    )
```

```python
import jax
import jax.numpy as jnp
from jax import lax
from jax.experimental import pallas as pl
from jax.experimental.pallas import tpu as pltpu
from jax.sharding import PartitionSpec as P

HD = 128
GT = 4
GH = 16
T = 160
NH = 3
HALF = NH * HD
FULL = 2 * HALF
WIN = 9 * T
SIDE = 3 * T
LOG2E = 1.4426950408889634
MESH = pl.DeviceIdType.MESH
BF = jnp.bfloat16
F32 = jnp.float32


def nt(a, b):
    return lax.dot_general(a, b, (((1,), (1,)), ((), ())), preferred_element_type=F32)


def nn(a, b):
    return lax.dot_general(a, b, (((1,), (0,)), ((), ())), preferred_element_type=F32)


def tn(a, b):
    return lax.dot_general(a, b, (((0,), (0,)), ((), ())), preferred_element_type=F32)


def kernel(
    q_in, k_in, v_in, w_in, g_in, valid,
    mixed, dq_out, dk_out, dv_out,
    kv, kvo, qo, qb, dob, dop, gall, wm, wo, att, attr, dqb, pb, rb_sum, bias,
    xs, rx, acc, zs, rz, ys, ms, mr, ms2, mr2, mo, rb, rb2, rc,
    lsem, hsem, fs, fr, bxs, bxr, bzs, bzr, bys, byr, gs, gr, qs, qr, dqs, dqr, ats, atr, mss, msr, rls, rlr, bcs, bcr,
):
    i = lax.axis_index("tile")
    j = lax.axis_index("head")
    t = i // GH
    g = i % GH
    p = g % 2
    u = g // 2
    d = 2 * p - 1
    e = (u == 3).astype(jnp.int32) - (u == 4).astype(jnp.int32)
    partner = (i + 1 - 2 * p, j)
    near = (t * GH + (g + 2 * d + GH) % GH, j)
    far = (t * GH + (g - 2 * d + GH) % GH, j)
    up = (((t + 1) % GT) * GH + g, j)
    down = (((t + GT - 1) % GT) * GH + g, j)
    eight_off = (t * GH + (g + GH // 2) % GH, j)
    six_off = (t * GH + (g + 6 + 4 * (u == 7).astype(jnp.int32)) % GH, j)
    relay = (t * GH + (g + GH - 6 * e) % GH, j)
    relay_to = eight_off
    back = (((t - e + GT) % GT) * GH + (g + 2 * e), j)
    j1 = j + 1 - 2 * (j % 2)
    j2 = (j + 2) % 4
    j3 = (j1 + 2) % 4
    sibling = (i, j1)
    across = (i, j2)
    has_up = t < GT - 1
    has_down = t > 0
    has_near = (u + d >= 0) & (u + d < GH // 2)
    has_far = (u - d >= 0) & (u - d < GH // 2)
    near_cross = e == d
    far_cross = e == -d
    is_cross = e != 0
    is_relay = (u == 0) | (u == 7)
    has_back = (t - e >= 0) & (t - e < GT)
    has_ahead = (t + e >= 0) & (t + e < GT)
    mine = pl.multiple_of(p * HALF, 128)
    theirs = pl.multiple_of((1 - p) * HALF, 128)
    scale = HD ** (-0.5)

    @pl.when(jnp.logical_not(has_down))
    def _():
        for s in (0, 3, 6, 9):
            kv[:, pl.ds(s * T, T), :] = jnp.zeros((NH, T, 2 * HD), BF)
        rz[:, 1] = jnp.zeros((NH, 2 * T, 2 * HD), BF)

    @pl.when(jnp.logical_not(has_up))
    def _():
        for s in (2, 5, 8, 11):
            kv[:, pl.ds(s * T, T), :] = jnp.zeros((NH, T, 2 * HD), BF)
        rz[:, 0] = jnp.zeros((NH, 2 * T, 2 * HD), BF)

    for n, side, there, crossing in ((0, 0, has_near, near_cross), (1, 3, has_far, far_cross)):
        @pl.when(jnp.logical_not(there))
        def _():
            kv[:, pl.ds(side * SIDE, SIDE), :] = jnp.zeros((NH, SIDE, 2 * HD), BF)

        @pl.when(jnp.logical_not(there) | crossing)
        def _():
            rx[:, n] = jnp.zeros((NH, SIDE, 2 * HD), BF)

    barrier = pltpu.get_barrier_semaphore()
    greeted = 0
    for peer, cond in (
        (partner, None), (sibling, None), (across, None), (near, has_near), (far, has_far), (up, has_up),
        (down, has_down), (eight_off, is_cross | is_relay), (six_off, is_relay),
        (relay, is_cross), (back, is_cross & has_back),
    ):
        if cond is None:
            pl.semaphore_signal(barrier, inc=1, device_id=peer, device_id_type=MESH)
            greeted += 1
        else:
            @pl.when(cond)
            def _():
                pl.semaphore_signal(barrier, inc=1, device_id=peer, device_id_type=MESH)
            greeted += cond.astype(jnp.int32)

    START, WAIT = 0, 1

    def when(cond, action):
        if cond is None:
            action()
        else:
            @pl.when(cond)
            def _():
                action()

    def remote(act, src, dst, send, recv, device, cond=None):
        copy = pltpu.make_async_remote_copy(
            src_ref=src, dst_ref=dst, send_sem=send, recv_sem=recv, device_id=device, device_id_type=MESH
        )
        when(cond, copy.start if act == START else copy.wait_send)

    def arrived(dst, recv, cond=None):
        copy = pltpu.make_async_remote_copy(
            src_ref=dst, dst_ref=dst, send_sem=lsem.at[0], recv_sem=recv, device_id=partner, device_id_type=MESH
        )
        when(cond, copy.wait_recv)

    def slot(h, s):
        return kv.at[h, pl.ds(s * T, T), :]

    def cols(h):
        return pl.ds(pl.multiple_of(h * HD, HD), HD)

    def mine_cols(h):
        return pl.ds(pl.multiple_of(mine + h * HD, HD), HD)

    def their_cols(h):
        return pl.ds(pl.multiple_of(theirs + h * HD, HD), HD)

    def local(src, dst, sem):
        copy = pltpu.make_async_copy(src, dst, sem)
        copy.start()
        return copy

    staged = [
        [
            local(k_in.at[:, their_cols(h)], kvo.at[h, :, pl.ds(0, HD)], hsem.at[h, 0]),
            local(v_in.at[:, their_cols(h)], kvo.at[h, :, pl.ds(HD, HD)], hsem.at[h, 1]),
        ]
        for h in range(NH)
    ]
    kept_tiles = [
        [
            local(k_in.at[:, mine_cols(h)], slot(h, 4).at[:, pl.ds(0, HD)], hsem.at[h, 2]),
            local(v_in.at[:, mine_cols(h)], slot(h, 4).at[:, pl.ds(HD, HD)], hsem.at[h, 3]),
        ]
        for h in range(NH)
    ]
    g_copy = local(g_in, gall.at[0], lsem.at[0])
    q_copy = local(q_in.at[:, pl.ds(mine, HALF)], qb.at[0], lsem.at[1])
    qo_copy = local(q_in.at[:, pl.ds(theirs, HALF)], qo, lsem.at[2])
    w_copies = [
        local(w_in.at[:, pl.ds(theirs, HALF)], wo, lsem.at[3]),
        local(w_in.at[:, pl.ds(mine, HALF)], wm, lsem.at[4]),
    ]

    lanes = lax.broadcasted_iota(jnp.int32, (1, WIN), 1)
    ones = jnp.ones((WIN, HD), BF)
    for a in range(2):
        row = jnp.zeros((1, WIN), F32)
        for n in range(9):
            g_slot, t_slot = a + n // 3, n % 3
            t_abs = t + t_slot - 1
            g_abs = g + (g_slot - 1) * (1 - 2 * p)
            if t_slot == 1 and g_slot == a + 1:
                value = jnp.float32(0.0)
            else:
                flag = valid[((t_abs + GT) % GT) * GH + (g_abs + GH) % GH]
                inside = (t_abs >= 0) & (t_abs < GT) & (g_abs >= 0) & (g_abs < GH)
                value = jnp.where(inside & (flag > 0), 0.0, -jnp.inf).astype(F32)
            row = jnp.where((lanes >= n * T) & (lanes < (n + 1) * T), value, row)
        bias[a] = row

    pl.semaphore_wait(barrier, greeted)

    def send_side(act, h, s, target, n, device, there, crossing):
        tile = slot(h, s)
        remote(act, tile, slot(h, target), fs.at[h, n], fr.at[h, target], device, there & jnp.logical_not(crossing))
        remote(act, tile, rb.at[h], rls.at[h, 0], rlr.at[h, 0], relay, crossing)
        remote(
            act, tile, slot(h, target + e), fs.at[h, n + 1], fr.at[h, target + e], back, crossing & has_back
        )

    def send_swap(act, h):
        remote(act, kvo.at[h], slot(h, 7), fs.at[h, 12], fr.at[h, 7], partner)

    def send_z(act, h, s):
        remote(act, slot(h, s), slot(h, s - 1), fs.at[h, 0 if s == 4 else 2], fr.at[h, s - 1], up, has_up)
        remote(act, slot(h, s), slot(h, s + 1), fs.at[h, 1 if s == 4 else 3], fr.at[h, s + 1], down, has_down)

    def send_own_x(act, h):
        send_side(act, h, 4, 10, 4, near, has_near, near_cross)

    def send_other_x(act, h):
        send_side(act, h, 7, 1, 6, far, has_far, far_cross)

    def pass_on(act, h):
        target = jnp.where((u == 0) == (p == 1), 10, 1)
        remote(act, rb.at[h], slot(h, target), rls.at[h, 1], fr.at[h, target], relay_to, is_relay)

    def forward(act, h, n, k):
        target, device, there, crossing = ((9, near, has_near, near_cross), (0, far, has_far, far_cross))[n]
        exists, way = ((has_down, 1), (has_up, -1))[k]
        source = slot(h, 3 + 3 * n + 2 * k)
        if act == START:
            arrived(source, fr.at[h, 3 + 3 * n + 2 * k], exists)
        remote(
            act, source, slot(h, target + 2 * k), fs.at[h, 8 + 2 * n + k], fr.at[h, target + 2 * k], device,
            exists & there & (jnp.logical_not(crossing) | (e == way)),
        )

    def send_back(act, h, n):
        device, there, crossing = ((far, has_far, far_cross), (near, has_near, near_cross))[n]
        remote(
            act, xs.at[h, n], rx.at[h, n], bxs.at[h, n, 0], bxr.at[h, n, 0], device,
            there & jnp.logical_not(crossing),
        )
        remote(act, xs.at[h, n, pl.ds(T, T)], rb2.at[h], rls.at[h, 2], rlr.at[h, 1], relay, crossing)
        rows = pl.ds((1 + e) * T, T)
        remote(
            act, xs.at[h, n, rows], rx.at[h, n, rows], bxs.at[h, n, 1], bxr.at[h, n, 2], device, crossing & has_ahead
        )
        remote(
            act, xs.at[h, n, pl.ds((1 - e) * T, T)], rc.at[h], bcs.at[h, n], bcr.at[h], back, crossing & has_back
        )

    def pass_back(act, h):
        n = jnp.where(u == 0, p, 1 - p)
        remote(act, rb2.at[h], rx.at[h, n, pl.ds(T, T)], rls.at[h, 3], bxr.at[h, n, 1], relay_to, is_relay)

    def send_attended(act, h):
        remote(act, att.at[1, :, cols(h)], attr.at[:, cols(h)], ats.at[h], atr.at[h], partner)

    def send_query_grad(act, h):
        remote(act, dqb.at[1, :, cols(h)], dq_out.at[:, mine_cols(h)], dqs.at[h], dqr.at[h], partner)
        copy = pltpu.make_async_copy(dqb.at[0, :, cols(h)], dq_out.at[:, mine_cols(h)], hsem.at[h, 2])
        if act == START:
            copy.start()
        else:
            copy.wait()

    def send_reduced(act, h):
        remote(act, zs.at[h, 0], rz.at[h, 0], bzs.at[h, 0], bzr.at[h, 0], down, has_down)
        remote(act, zs.at[h, 1], rz.at[h, 1], bzs.at[h, 1], bzr.at[h, 1], up, has_up)

    def send_total(act, h):
        for part, out in enumerate((dk_out, dv_out)):
            lane = pl.ds(part * HD, HD)
            remote(act, ys.at[h, 1, :, lane], out.at[:, mine_cols(h)], bys.at[h, part], byr.at[h, part], partner)
            copy = pltpu.make_async_copy(ys.at[h, 0, :, lane], out.at[:, mine_cols(h)], hsem.at[h, part])
            if act == START:
                copy.start()
            else:
                copy.wait()

    def attend(h):
        for s, there in ((9, has_far & has_down), (10, has_far), (11, has_far & has_up),
                         (0, has_near & has_down), (1, has_near), (2, has_near & has_up)):
            arrived(slot(h, s), fr.at[h, s], there)
        for a in range(2):
            window = pl.ds(a * SIDE, WIN)
            s = nt(qb[a, :, cols(h)], kv[h, window, pl.ds(0, HD)]) * (scale * LOG2E) + bias[a]
            x = jnp.exp2(s - jnp.max(s, axis=1, keepdims=True)).astype(BF)
            pb[a] = x
            total = nn(x, jnp.concatenate([kv[h, window, pl.ds(HD, HD)], ones], axis=1))
            inverse = 1.0 / total[:, HD:]
            rb_sum[a] = inverse
            att[a, :, cols(h)] = (total[:, :HD] * inverse).astype(BF)
        send_attended(START, h)

    def differentiate(h, a):
        q = qb[a, :, cols(h)]
        do = dob[a, :, cols(h)].astype(F32)
        window = pl.ds(a * SIDE, WIN)
        k = kv[h, window, pl.ds(0, HD)]
        weights = pb[a]
        inverse = rb_sum[a]
        row_dot = jnp.sum(do * att[a, :, cols(h)].astype(F32) * (inverse * scale), axis=1, keepdims=True)
        do_sum = (do * inverse).astype(BF)
        weight_grad = nt((do * (inverse * scale)).astype(BF), kv[h, window, pl.ds(HD, HD)])
        score_grad = weights * (weight_grad - row_dot).astype(BF)
        dqb[a, :, cols(h)] = nn(score_grad, k).astype(BF)
        for part, lhs, rhs in ((0, score_grad, q), (1, weights, do_sum)):
            grad = tn(lhs, rhs)
            lane = pl.ds(part * HD, HD)
            if a == 0:
                xs[h, 1, :, lane] = grad[:SIDE].astype(BF)
                acc[h, :, lane] = grad[SIDE:]
            else:
                acc[h, :, lane] += grad[:2 * SIDE]
                xs[h, 0, :, lane] = grad[2 * SIDE:].astype(BF)
        send_back(START, h, 1 - a)
        if a == 1:
            send_query_grad(START, h)

    def reduce_x(h):
        for n, there, crossing in ((0, has_near, near_cross), (1, has_far, far_cross)):
            arrived(rx.at[h, n], bxr.at[h, n, 0], there & jnp.logical_not(crossing))
            arrived(rx.at[h, n, pl.ds(T, T)], bxr.at[h, n, 1], crossing)
            arrived(rx.at[h, n, pl.ds((1 - e) * T, T)], bxr.at[h, n, 2], crossing & has_back)
        for n in range(2):
            for part, row in ((0, 0), (1, 2 * T)):
                zs[h, part, pl.ds(n * T, T), :] = (
                    acc[h, pl.ds(n * SIDE + row, T), :] + rx[h, n, pl.ds(row, T), :].astype(F32)
                ).astype(BF)
            acc[h, pl.ds(n * SIDE + T, T), :] += rx[h, n, pl.ds(T, T), :].astype(F32)
        send_reduced(START, h)

    def reduce_z(h):
        arrived(rz.at[h, 0], bzr.at[h, 0], has_up)
        arrived(rz.at[h, 1], bzr.at[h, 1], has_down)
        arrived(rc.at[h], bcr.at[h], is_cross & has_back)
        for n, crossing in ((0, near_cross), (1, far_cross)):
            @pl.when(crossing & has_back)
            def _():
                acc[h, pl.ds(n * SIDE + T, T), :] += rc[h].astype(F32)

        for n in range(2):
            rows = pl.ds(n * T, T)
            ys[h, n] = (
                acc[h, pl.ds(n * SIDE + T, T), :] + rz[h, 0, rows, :].astype(F32) + rz[h, 1, rows, :].astype(F32)
            ).astype(BF)
        send_total(START, h)

    blocks = (j, j1, j2, j3)
    rows = [pl.ds(pl.multiple_of(block * FULL, FULL), FULL) for block in blocks]

    def attn_grad(weights_ref):
        total = nn(gall[0], weights_ref[rows[0], :])
        for n in range(1, 4):
            total = total + nn(gall[n], weights_ref[rows[n], :])
        return total.astype(BF)

    blocks = (j, j1, j2, j3)
    rows = [pl.ds(pl.multiple_of(block * FULL, FULL), FULL) for block in blocks]

    def send_gathered(act, n):
        source, target, device, k = ((0, 2, across, 1), (0, 1, sibling, 0), (2, 3, sibling, 2))[n]
        remote(act, gall.at[source], gall.at[target], gs.at[k], gr.at[k], device)

    def send_queries(act):
        remote(act, qo, qb.at[1], qs.at[0], qr.at[0], partner)

    def attn_grad(weights_ref):
        total = nn(gall[0], weights_ref[rows[0], :])
        for k in range(1, 4):
            total = total + nn(gall[k], weights_ref[rows[k], :])
        return total.astype(BF)

    def send_attn_grad(act):
        remote(act, dop, dob.at[1], qs.at[1], qr.at[1], partner)

    def project(n):
        return nt(att[0], wm[rows[n], :]) + nt(attr[...], wo[rows[n], :])

    for copy in staged[0]:
        copy.wait()
    send_swap(START, 0)
    for copy in kept_tiles[0]:
        copy.wait()
    send_z(START, 0, 4)
    for copy in staged[1]:
        copy.wait()
    send_swap(START, 1)
    arrived(slot(0, 7), fr.at[0, 7])
    send_z(START, 0, 7)
    g_copy.wait()
    send_gathered(START, 0)
    send_own_x(START, 0)
    for copy in kept_tiles[1]:
        copy.wait()
    send_z(START, 1, 4)
    for copy in staged[2]:
        copy.wait()
    send_swap(START, 2)
    arrived(slot(1, 7), fr.at[1, 7])
    send_z(START, 1, 7)
    forward(START, 0, 0, 0)
    send_other_x(START, 0)
    forward(START, 0, 0, 1)
    forward(START, 0, 1, 0)
    qo_copy.wait()
    send_queries(START)
    send_other_x(START, 1)
    send_own_x(START, 1)
    arrived(gall.at[2], gr.at[1])
    send_gathered(START, 2)
    send_gathered(START, 1)
    forward(START, 0, 1, 1)
    arrived(rb.at[0], rlr.at[0, 0], is_relay)
    pass_on(START, 0)
    arrived(slot(2, 7), fr.at[2, 7])
    send_z(START, 2, 7)
    forward(START, 1, 0, 0)
    for copy in w_copies:
        copy.wait()
    arrived(gall.at[1], gr.at[0])
    arrived(gall.at[3], gr.at[2])
    dop[...] = attn_grad(wo)
    send_attn_grad(START)
    dob[0] = attn_grad(wm)
    for copy in kept_tiles[2]:
        copy.wait()
    send_z(START, 2, 4)
    forward(START, 1, 1, 1)
    send_other_x(START, 2)
    send_own_x(START, 2)
    arrived(rb.at[1], rlr.at[1, 0], is_relay)
    pass_on(START, 1)
    forward(START, 1, 0, 1)
    q_copy.wait()
    arrived(qb.at[1], qr.at[0])
    attend(0)
    forward(START, 1, 1, 0)
    arrived(dob.at[1], qr.at[1])
    differentiate(0, 0)
    differentiate(0, 1)
    forward(START, 2, 1, 1)
    forward(START, 2, 1, 0)
    forward(START, 2, 0, 0)
    attend(1)
    forward(START, 2, 0, 1)
    arrived(rb2.at[0], rlr.at[0, 1], is_relay)
    pass_back(START, 0)
    arrived(rb.at[2], rlr.at[2, 0], is_relay)
    pass_on(START, 2)
    differentiate(1, 0)
    differentiate(1, 1)
    reduce_x(0)
    attend(2)
    arrived(rb2.at[1], rlr.at[1, 1], is_relay)
    pass_back(START, 1)
    differentiate(2, 0)
    differentiate(2, 1)
    reduce_x(1)
    for h in range(NH):
        arrived(attr.at[:, cols(h)], atr.at[h])
    ms[0] = project(3).astype(BF)
    ms[1] = project(1).astype(BF)
    remote(START, ms, mr, mss.at[0], msr.at[0], sibling)
    arrived(rb2.at[2], rlr.at[2, 1], is_relay)
    pass_back(START, 2)
    crossing_sum = project(2)
    arrived(mr, msr.at[0])
    ms2[...] = (crossing_sum + mr[0].astype(F32)).astype(BF)
    remote(START, ms2, mr2, mss.at[1], msr.at[1], across)
    kept = project(0) + mr[1].astype(F32)
    reduce_x(2)
    reduce_z(0)
    reduce_z(1)
    reduce_z(2)
    arrived(mr2, msr.at[1])
    mo[...] = (kept + mr2[...].astype(F32)).astype(BF)
    mixed_copy = local(mo, mixed, lsem.at[5])
    send_z(WAIT, 0, 4)
    send_z(WAIT, 0, 7)
    send_z(WAIT, 1, 4)
    send_z(WAIT, 1, 7)
    send_z(WAIT, 2, 4)
    send_z(WAIT, 2, 7)

    for n in range(3):
        send_gathered(WAIT, n)
    send_queries(WAIT)
    send_attn_grad(WAIT)
    remote(WAIT, ms, mr, mss.at[0], msr.at[0], sibling)
    remote(WAIT, ms2, mr2, mss.at[1], msr.at[1], across)
    for h in range(NH):
        for send in (
            send_swap, send_own_x, send_other_x, pass_on, pass_back, send_attended, send_query_grad, send_reduced,
            send_total,
        ):
            send(WAIT, h)
        for n in range(2):
            forward(WAIT, h, n, 0)
            forward(WAIT, h, n, 1)
            send_back(WAIT, h, n)
        arrived(dq_out.at[:, their_cols(h)], dqr.at[h])
        arrived(dk_out.at[:, their_cols(h)], byr.at[h, 0])
        arrived(dv_out.at[:, their_cols(h)], byr.at[h, 1])
    mixed_copy.wait()

def hand_over(*refs):
    for n in range(4):
        refs[4 + n][...] = refs[n][...]


def on_device(queries, keys, values, w_out, out_grad, tile_valid):
    dma = pltpu.SemaphoreType.DMA
    any_space = pl.BlockSpec(memory_space=pl.ANY)
    block = jax.ShapeDtypeStruct(queries.shape, BF)
    results = pl.pallas_call(
        kernel,
        out_shape=(block, block, block, block),
        in_specs=[any_space] * 5 + [pl.BlockSpec(memory_space=pltpu.SMEM)],
        out_specs=(any_space, any_space, any_space, any_space),
        scratch_shapes=[
            pltpu.VMEM((NH, 12 * T, 2 * HD), BF),
            pltpu.VMEM((NH, T, 2 * HD), BF),
            pltpu.VMEM((T, HALF), BF),
            pltpu.VMEM((2, T, HALF), BF),
            pltpu.VMEM((2, T, HALF), BF),
            pltpu.VMEM((T, HALF), BF),
            pltpu.VMEM((4, T, FULL), BF),
            pltpu.VMEM((4 * FULL, HALF), BF),
            pltpu.VMEM((4 * FULL, HALF), BF),
            pltpu.VMEM((2, T, HALF), BF),
            pltpu.VMEM((T, HALF), BF),
            pltpu.VMEM((2, T, HALF), BF),
            pltpu.VMEM((2, T, WIN), BF),
            pltpu.VMEM((2, T, HD), F32),
            pltpu.VMEM((2, 1, WIN), F32),
            pltpu.VMEM((NH, 2, SIDE, 2 * HD), BF),
            pltpu.VMEM((NH, 2, SIDE, 2 * HD), BF),
            pltpu.VMEM((NH, 2 * SIDE, 2 * HD), F32),
            pltpu.VMEM((NH, 2, 2 * T, 2 * HD), BF),
            pltpu.VMEM((NH, 2, 2 * T, 2 * HD), BF),
            pltpu.VMEM((NH, 2, T, 2 * HD), BF),
            pltpu.VMEM((2, T, FULL), BF),
            pltpu.VMEM((2, T, FULL), BF),
            pltpu.VMEM((T, FULL), BF),
            pltpu.VMEM((T, FULL), BF),
            pltpu.VMEM((T, FULL), BF),
            pltpu.VMEM((NH, T, 2 * HD), BF),
            pltpu.VMEM((NH, T, 2 * HD), BF),
            pltpu.VMEM((NH, T, 2 * HD), BF),
            dma((6,)),
            dma((NH, 4)),
            dma((NH, 14)),
            dma((NH, 12)),
            dma((NH, 2, 2)),
            dma((NH, 2, 3)),
            dma((NH, 2)),
            dma((NH, 2)),
            dma((NH, 2)),
            dma((NH, 2)),
            dma((3,)),
            dma((3,)),
            dma((2,)),
            dma((2,)),
            dma((NH,)),
            dma((NH,)),
            dma((NH,)),
            dma((NH,)),
            dma((2,)),
            dma((2,)),
            dma((NH, 4)),
            dma((NH, 2)),
            dma((NH, 2)),
            dma((NH,)),
        ],
        compiler_params=pltpu.CompilerParams(
            collective_id=0, has_side_effects=True, vmem_limit_bytes=56 * 1024 * 1024
        ),
    )(queries, keys, values, w_out, out_grad, tile_valid)
    whole = pl.BlockSpec(memory_space=pltpu.VMEM)
    return pl.pallas_call(
        hand_over,
        out_shape=(block, block, block, block),
        in_specs=[whole] * 4,
        out_specs=(whole, whole, whole, whole),
    )(*results)


def solution(mesh):
    return jax.shard_map(
        on_device,
        mesh=mesh,
        in_specs=(
            P("tile", "head"),
            P("tile", "head"),
            P("tile", "head"),
            P(None, "head"),
            P("tile", "head"),
            P(),
        ),
        out_specs=(P("tile", "head"), P("tile", "head"), P("tile", "head"), P("tile", "head")),
        check_vma=False,
    )
```

```python
import jax
import jax.numpy as jnp
from jax import lax
from jax.experimental import pallas as pl
from jax.experimental.pallas import tpu as pltpu
from jax.sharding import PartitionSpec as P

HD = 128
GT = 4
GH = 16
T = 160
NH = 3
HALF = NH * HD
FULL = 2 * HALF
WIN = 9 * T
SIDE = 3 * T
LOG2E = 1.4426950408889634
DIRECT_OUT = (0,)
DIRECT_BACK = (2,)
MESH = pl.DeviceIdType.MESH
BF = jnp.bfloat16
F32 = jnp.float32


def nt(a, b):
    return lax.dot_general(a, b, (((1,), (1,)), ((), ())), preferred_element_type=F32)


def nn(a, b):
    return lax.dot_general(a, b, (((1,), (0,)), ((), ())), preferred_element_type=F32)


def tn(a, b):
    return lax.dot_general(a, b, (((0,), (0,)), ((), ())), preferred_element_type=F32)


def kernel(
    q_in, k_in, v_in, w_in, g_in, valid,
    mixed, dq_out, dk_out, dv_out,
    kv, kvo, qo, qb, dob, dop, gall, wm, wo, att, attr, dqb, pb, rb_sum, bias,
    xs, rx, acc, zs, rz, ys, ms, mr, ms2, mr2, mo, rb, rb2, rc,
    lsem, hsem, fs, fr, bxs, bxr, bzs, bzr, bys, byr, gs, gr, qs, qr, dqs, dqr, ats, atr, mss, msr, rls, rlr, bcs, bcr,
):
    i = lax.axis_index("tile")
    j = lax.axis_index("head")
    t = i // GH
    g = i % GH
    p = g % 2
    u = g // 2
    d = 2 * p - 1
    e = (u == 3).astype(jnp.int32) - (u == 4).astype(jnp.int32)
    partner = (i + 1 - 2 * p, j)
    near = (t * GH + (g + 2 * d + GH) % GH, j)
    far = (t * GH + (g - 2 * d + GH) % GH, j)
    up = (((t + 1) % GT) * GH + g, j)
    down = (((t + GT - 1) % GT) * GH + g, j)
    eight_off = (t * GH + (g + GH // 2) % GH, j)
    six_off = (t * GH + (g + 6 + 4 * (u == 7).astype(jnp.int32)) % GH, j)
    relay = (t * GH + (g + GH - 6 * e) % GH, j)
    relay_to = eight_off
    back = (((t - e + GT) % GT) * GH + (g + 2 * e), j)
    j1 = j + 1 - 2 * (j % 2)
    j2 = (j + 2) % 4
    j3 = (j1 + 2) % 4
    sibling = (i, j1)
    across = (i, j2)
    has_up = t < GT - 1
    has_down = t > 0
    has_near = (u + d >= 0) & (u + d < GH // 2)
    has_far = (u - d >= 0) & (u - d < GH // 2)
    near_cross = e == d
    far_cross = e == -d
    is_cross = e != 0
    is_relay = (u == 0) | (u == 7)
    has_back = (t - e >= 0) & (t - e < GT)
    has_ahead = (t + e >= 0) & (t + e < GT)
    mine = pl.multiple_of(p * HALF, 128)
    theirs = pl.multiple_of((1 - p) * HALF, 128)
    scale = HD ** (-0.5)

    @pl.when(jnp.logical_not(has_down))
    def _():
        for s in (0, 3, 6, 9):
            kv[:, pl.ds(s * T, T), :] = jnp.zeros((NH, T, 2 * HD), BF)
        rz[:, 1] = jnp.zeros((NH, 2 * T, 2 * HD), BF)

    @pl.when(jnp.logical_not(has_up))
    def _():
        for s in (2, 5, 8, 11):
            kv[:, pl.ds(s * T, T), :] = jnp.zeros((NH, T, 2 * HD), BF)
        rz[:, 0] = jnp.zeros((NH, 2 * T, 2 * HD), BF)

    for n, side, there, crossing in ((0, 0, has_near, near_cross), (1, 3, has_far, far_cross)):
        @pl.when(jnp.logical_not(there))
        def _():
            kv[:, pl.ds(side * SIDE, SIDE), :] = jnp.zeros((NH, SIDE, 2 * HD), BF)

        @pl.when(jnp.logical_not(there) | crossing)
        def _():
            rx[:, n] = jnp.zeros((NH, SIDE, 2 * HD), BF)

    barrier = pltpu.get_barrier_semaphore()
    greeted = 0
    for peer, cond in (
        (partner, None), (sibling, None), (across, None), (near, has_near), (far, has_far), (up, has_up),
        (down, has_down), (eight_off, is_cross | is_relay), (six_off, is_relay),
        (relay, is_cross), (back, is_cross & has_back),
    ):
        if cond is None:
            pl.semaphore_signal(barrier, inc=1, device_id=peer, device_id_type=MESH)
            greeted += 1
        else:
            @pl.when(cond)
            def _():
                pl.semaphore_signal(barrier, inc=1, device_id=peer, device_id_type=MESH)
            greeted += cond.astype(jnp.int32)

    START, WAIT = 0, 1

    def when(cond, action):
        if cond is None:
            action()
        else:
            @pl.when(cond)
            def _():
                action()

    def remote(act, src, dst, send, recv, device, cond=None):
        copy = pltpu.make_async_remote_copy(
            src_ref=src, dst_ref=dst, send_sem=send, recv_sem=recv, device_id=device, device_id_type=MESH
        )
        when(cond, copy.start if act == START else copy.wait_send)

    def arrived(dst, recv, cond=None):
        copy = pltpu.make_async_remote_copy(
            src_ref=dst, dst_ref=dst, send_sem=lsem.at[0], recv_sem=recv, device_id=partner, device_id_type=MESH
        )
        when(cond, copy.wait_recv)

    def slot(h, s):
        return kv.at[h, pl.ds(s * T, T), :]

    def cols(h):
        return pl.ds(pl.multiple_of(h * HD, HD), HD)

    def mine_cols(h):
        return pl.ds(pl.multiple_of(mine + h * HD, HD), HD)

    def their_cols(h):
        return pl.ds(pl.multiple_of(theirs + h * HD, HD), HD)

    def local(src, dst, sem):
        copy = pltpu.make_async_copy(src, dst, sem)
        copy.start()
        return copy

    staged = [
        [
            local(k_in.at[:, their_cols(h)], kvo.at[h, :, pl.ds(0, HD)], hsem.at[h, 0]),
            local(v_in.at[:, their_cols(h)], kvo.at[h, :, pl.ds(HD, HD)], hsem.at[h, 1]),
        ]
        for h in range(NH)
    ]
    kept_tiles = [
        [
            local(k_in.at[:, mine_cols(h)], slot(h, 4).at[:, pl.ds(0, HD)], hsem.at[h, 2]),
            local(v_in.at[:, mine_cols(h)], slot(h, 4).at[:, pl.ds(HD, HD)], hsem.at[h, 3]),
        ]
        for h in range(NH)
    ]
    g_copy = local(g_in, gall.at[0], lsem.at[0])
    q_copy = local(q_in.at[:, pl.ds(mine, HALF)], qb.at[0], lsem.at[1])
    qo_copy = local(q_in.at[:, pl.ds(theirs, HALF)], qo, lsem.at[2])
    w_copies = [
        local(w_in.at[:, pl.ds(theirs, HALF)], wo, lsem.at[3]),
        local(w_in.at[:, pl.ds(mine, HALF)], wm, lsem.at[4]),
    ]

    lanes = lax.broadcasted_iota(jnp.int32, (1, WIN), 1)
    ones = jnp.ones((WIN, HD), BF)
    for a in range(2):
        row = jnp.zeros((1, WIN), F32)
        for n in range(9):
            g_slot, t_slot = a + n // 3, n % 3
            t_abs = t + t_slot - 1
            g_abs = g + (g_slot - 1) * (1 - 2 * p)
            if t_slot == 1 and g_slot == a + 1:
                value = jnp.float32(0.0)
            else:
                flag = valid[((t_abs + GT) % GT) * GH + (g_abs + GH) % GH]
                inside = (t_abs >= 0) & (t_abs < GT) & (g_abs >= 0) & (g_abs < GH)
                value = jnp.where(inside & (flag > 0), 0.0, -jnp.inf).astype(F32)
            row = jnp.where((lanes >= n * T) & (lanes < (n + 1) * T), value, row)
        bias[a] = row

    pl.semaphore_wait(barrier, greeted)

    def send_side(act, h, s, target, n, device, there, crossing):
        tile = slot(h, s)
        direct = there if h in DIRECT_OUT else there & jnp.logical_not(crossing)
        remote(act, tile, slot(h, target), fs.at[h, n], fr.at[h, target], device, direct)
        if h not in DIRECT_OUT:
            remote(act, tile, rb.at[h], rls.at[h, 0], rlr.at[h, 0], relay, crossing)
        remote(
            act, tile, slot(h, target + e), fs.at[h, n + 1], fr.at[h, target + e], back, crossing & has_back
        )

    def send_swap(act, h):
        remote(act, kvo.at[h], slot(h, 7), fs.at[h, 12], fr.at[h, 7], partner)

    def send_z(act, h, s):
        remote(act, slot(h, s), slot(h, s - 1), fs.at[h, 0 if s == 4 else 2], fr.at[h, s - 1], up, has_up)
        remote(act, slot(h, s), slot(h, s + 1), fs.at[h, 1 if s == 4 else 3], fr.at[h, s + 1], down, has_down)

    def send_own_x(act, h):
        send_side(act, h, 4, 10, 4, near, has_near, near_cross)

    def send_other_x(act, h):
        send_side(act, h, 7, 1, 6, far, has_far, far_cross)

    def pass_on(act, h):
        if h in DIRECT_OUT:
            return
        if act == START:
            arrived(rb.at[h], rlr.at[h, 0], is_relay)
        target = jnp.where((u == 0) == (p == 1), 10, 1)
        remote(act, rb.at[h], slot(h, target), rls.at[h, 1], fr.at[h, target], relay_to, is_relay)

    def forward(act, h, n, k):
        target, device, there, crossing = ((9, near, has_near, near_cross), (0, far, has_far, far_cross))[n]
        exists, way = ((has_down, 1), (has_up, -1))[k]
        source = slot(h, 3 + 3 * n + 2 * k)
        if act == START:
            arrived(source, fr.at[h, 3 + 3 * n + 2 * k], exists)
        remote(
            act, source, slot(h, target + 2 * k), fs.at[h, 8 + 2 * n + k], fr.at[h, target + 2 * k], device,
            exists & there & (jnp.logical_not(crossing) | (e == way)),
        )

    def send_back(act, h, n):
        device, there, crossing = ((far, has_far, far_cross), (near, has_near, near_cross))[n]
        remote(
            act, xs.at[h, n], rx.at[h, n], bxs.at[h, n, 0], bxr.at[h, n, 0], device,
            there & jnp.logical_not(crossing),
        )
        middle = xs.at[h, n, pl.ds(T, T)]
        if h in DIRECT_BACK:
            remote(act, middle, rx.at[h, n, pl.ds(T, T)], bxs.at[h, n, 2], bxr.at[h, n, 1], device, crossing)
        else:
            remote(act, middle, rb2.at[h], rls.at[h, 2], rlr.at[h, 1], relay, crossing)
        rows = pl.ds((1 + e) * T, T)
        remote(
            act, xs.at[h, n, rows], rx.at[h, n, rows], bxs.at[h, n, 1], bxr.at[h, n, 2], device, crossing & has_ahead
        )
        remote(
            act, xs.at[h, n, pl.ds((1 - e) * T, T)], rc.at[h], bcs.at[h, n], bcr.at[h], back, crossing & has_back
        )

    def pass_back(act, h):
        if h in DIRECT_BACK:
            return
        if act == START:
            arrived(rb2.at[h], rlr.at[h, 1], is_relay)
        n = jnp.where(u == 0, p, 1 - p)
        remote(act, rb2.at[h], rx.at[h, n, pl.ds(T, T)], rls.at[h, 3], bxr.at[h, n, 1], relay_to, is_relay)

    def send_attended(act, h):
        remote(act, att.at[1, :, cols(h)], attr.at[:, cols(h)], ats.at[h], atr.at[h], partner)

    def send_query_grad(act, h):
        remote(act, dqb.at[1, :, cols(h)], dq_out.at[:, mine_cols(h)], dqs.at[h], dqr.at[h], partner)
        copy = pltpu.make_async_copy(dqb.at[0, :, cols(h)], dq_out.at[:, mine_cols(h)], hsem.at[h, 2])
        if act == START:
            copy.start()
        else:
            copy.wait()

    def send_reduced(act, h):
        remote(act, zs.at[h, 0], rz.at[h, 0], bzs.at[h, 0], bzr.at[h, 0], down, has_down)
        remote(act, zs.at[h, 1], rz.at[h, 1], bzs.at[h, 1], bzr.at[h, 1], up, has_up)

    def send_total(act, h):
        for part, out in enumerate((dk_out, dv_out)):
            lane = pl.ds(part * HD, HD)
            remote(act, ys.at[h, 1, :, lane], out.at[:, mine_cols(h)], bys.at[h, part], byr.at[h, part], partner)
            copy = pltpu.make_async_copy(ys.at[h, 0, :, lane], out.at[:, mine_cols(h)], hsem.at[h, part])
            if act == START:
                copy.start()
            else:
                copy.wait()

    def attend(h):
        for s, there in ((9, has_far & has_down), (10, has_far), (11, has_far & has_up),
                         (0, has_near & has_down), (1, has_near), (2, has_near & has_up)):
            arrived(slot(h, s), fr.at[h, s], there)
        for a in range(2):
            window = pl.ds(a * SIDE, WIN)
            s = nt(qb[a, :, cols(h)], kv[h, window, pl.ds(0, HD)]) * (scale * LOG2E) + bias[a]
            x = jnp.exp2(s - jnp.max(s, axis=1, keepdims=True)).astype(BF)
            pb[a] = x
            total = nn(x, jnp.concatenate([kv[h, window, pl.ds(HD, HD)], ones], axis=1))
            inverse = 1.0 / total[:, HD:]
            rb_sum[a] = inverse
            att[a, :, cols(h)] = (total[:, :HD] * inverse).astype(BF)
        send_attended(START, h)

    def differentiate(h, a):
        q = qb[a, :, cols(h)]
        do = dob[a, :, cols(h)].astype(F32)
        window = pl.ds(a * SIDE, WIN)
        k = kv[h, window, pl.ds(0, HD)]
        weights = pb[a]
        inverse = rb_sum[a]
        row_dot = jnp.sum(do * att[a, :, cols(h)].astype(F32) * (inverse * scale), axis=1, keepdims=True)
        do_sum = (do * inverse).astype(BF)
        weight_grad = nt((do * (inverse * scale)).astype(BF), kv[h, window, pl.ds(HD, HD)])
        score_grad = weights * (weight_grad - row_dot).astype(BF)
        dqb[a, :, cols(h)] = nn(score_grad, k).astype(BF)
        for part, lhs, rhs in ((0, score_grad, q), (1, weights, do_sum)):
            grad = tn(lhs, rhs)
            lane = pl.ds(part * HD, HD)
            if a == 0:
                xs[h, 1, :, lane] = grad[:SIDE].astype(BF)
                acc[h, :, lane] = grad[SIDE:]
            else:
                acc[h, :, lane] += grad[:2 * SIDE]
                xs[h, 0, :, lane] = grad[2 * SIDE:].astype(BF)
        send_back(START, h, 1 - a)
        if a == 1:
            send_query_grad(START, h)

    def reduce_x(h):
        for n, there, crossing in ((0, has_near, near_cross), (1, has_far, far_cross)):
            arrived(rx.at[h, n], bxr.at[h, n, 0], there & jnp.logical_not(crossing))
            arrived(rx.at[h, n, pl.ds(T, T)], bxr.at[h, n, 1], crossing)
            arrived(rx.at[h, n, pl.ds((1 - e) * T, T)], bxr.at[h, n, 2], crossing & has_back)
        for n in range(2):
            for part, row in ((0, 0), (1, 2 * T)):
                zs[h, part, pl.ds(n * T, T), :] = (
                    acc[h, pl.ds(n * SIDE + row, T), :] + rx[h, n, pl.ds(row, T), :].astype(F32)
                ).astype(BF)
            acc[h, pl.ds(n * SIDE + T, T), :] += rx[h, n, pl.ds(T, T), :].astype(F32)
        send_reduced(START, h)

    def reduce_z(h):
        arrived(rz.at[h, 0], bzr.at[h, 0], has_up)
        arrived(rz.at[h, 1], bzr.at[h, 1], has_down)
        arrived(rc.at[h], bcr.at[h], is_cross & has_back)
        for n, crossing in ((0, near_cross), (1, far_cross)):
            @pl.when(crossing & has_back)
            def _():
                acc[h, pl.ds(n * SIDE + T, T), :] += rc[h].astype(F32)

        for n in range(2):
            rows = pl.ds(n * T, T)
            ys[h, n] = (
                acc[h, pl.ds(n * SIDE + T, T), :] + rz[h, 0, rows, :].astype(F32) + rz[h, 1, rows, :].astype(F32)
            ).astype(BF)
        send_total(START, h)

    blocks = (j, j1, j2, j3)
    rows = [pl.ds(pl.multiple_of(block * FULL, FULL), FULL) for block in blocks]

    def attn_grad(weights_ref):
        total = nn(gall[0], weights_ref[rows[0], :])
        for n in range(1, 4):
            total = total + nn(gall[n], weights_ref[rows[n], :])
        return total.astype(BF)

    blocks = (j, j1, j2, j3)
    rows = [pl.ds(pl.multiple_of(block * FULL, FULL), FULL) for block in blocks]

    def send_gathered(act, n):
        source, target, device, k = ((0, 2, across, 1), (0, 1, sibling, 0), (2, 3, sibling, 2))[n]
        remote(act, gall.at[source], gall.at[target], gs.at[k], gr.at[k], device)

    def send_queries(act):
        remote(act, qo, qb.at[1], qs.at[0], qr.at[0], partner)

    def attn_grad(weights_ref):
        total = nn(gall[0], weights_ref[rows[0], :])
        for k in range(1, 4):
            total = total + nn(gall[k], weights_ref[rows[k], :])
        return total.astype(BF)

    def send_attn_grad(act):
        remote(act, dop, dob.at[1], qs.at[1], qr.at[1], partner)

    def project(n):
        return nt(att[0], wm[rows[n], :]) + nt(attr[...], wo[rows[n], :])

    for copy in staged[0]:
        copy.wait()
    send_swap(START, 0)
    for copy in kept_tiles[0]:
        copy.wait()
    send_z(START, 0, 4)
    for copy in staged[1]:
        copy.wait()
    send_swap(START, 1)
    arrived(slot(0, 7), fr.at[0, 7])
    send_z(START, 0, 7)
    g_copy.wait()
    send_gathered(START, 0)
    send_own_x(START, 0)
    for copy in kept_tiles[1]:
        copy.wait()
    send_z(START, 1, 4)
    for copy in staged[2]:
        copy.wait()
    send_swap(START, 2)
    arrived(slot(1, 7), fr.at[1, 7])
    send_z(START, 1, 7)
    forward(START, 0, 0, 0)
    send_other_x(START, 0)
    forward(START, 0, 0, 1)
    forward(START, 0, 1, 0)
    qo_copy.wait()
    send_queries(START)
    send_other_x(START, 1)
    send_own_x(START, 1)
    arrived(gall.at[2], gr.at[1])
    send_gathered(START, 2)
    send_gathered(START, 1)
    forward(START, 0, 1, 1)
    pass_on(START, 0)
    arrived(slot(2, 7), fr.at[2, 7])
    send_z(START, 2, 7)
    forward(START, 1, 0, 0)
    for copy in w_copies:
        copy.wait()
    arrived(gall.at[1], gr.at[0])
    arrived(gall.at[3], gr.at[2])
    dop[...] = attn_grad(wo)
    send_attn_grad(START)
    dob[0] = attn_grad(wm)
    for copy in kept_tiles[2]:
        copy.wait()
    send_z(START, 2, 4)
    forward(START, 1, 1, 1)
    send_other_x(START, 2)
    send_own_x(START, 2)
    pass_on(START, 1)
    forward(START, 1, 0, 1)
    q_copy.wait()
    arrived(qb.at[1], qr.at[0])
    attend(0)
    forward(START, 1, 1, 0)
    arrived(dob.at[1], qr.at[1])
    differentiate(0, 0)
    differentiate(0, 1)
    forward(START, 2, 1, 1)
    forward(START, 2, 1, 0)
    forward(START, 2, 0, 0)
    attend(1)
    forward(START, 2, 0, 1)
    pass_back(START, 0)
    pass_on(START, 2)
    differentiate(1, 0)
    differentiate(1, 1)
    reduce_x(0)
    attend(2)
    pass_back(START, 1)
    differentiate(2, 0)
    differentiate(2, 1)
    reduce_x(1)
    for h in range(NH):
        arrived(attr.at[:, cols(h)], atr.at[h])
    ms[0] = project(3).astype(BF)
    ms[1] = project(1).astype(BF)
    remote(START, ms, mr, mss.at[0], msr.at[0], sibling)
    pass_back(START, 2)
    crossing_sum = project(2)
    arrived(mr, msr.at[0])
    ms2[...] = (crossing_sum + mr[0].astype(F32)).astype(BF)
    remote(START, ms2, mr2, mss.at[1], msr.at[1], across)
    kept = project(0) + mr[1].astype(F32)
    reduce_x(2)
    reduce_z(0)
    reduce_z(1)
    reduce_z(2)
    arrived(mr2, msr.at[1])
    mo[...] = (kept + mr2[...].astype(F32)).astype(BF)
    mixed_copy = local(mo, mixed, lsem.at[5])
    send_z(WAIT, 0, 4)
    send_z(WAIT, 0, 7)
    send_z(WAIT, 1, 4)
    send_z(WAIT, 1, 7)
    send_z(WAIT, 2, 4)
    send_z(WAIT, 2, 7)

    for n in range(3):
        send_gathered(WAIT, n)
    send_queries(WAIT)
    send_attn_grad(WAIT)
    remote(WAIT, ms, mr, mss.at[0], msr.at[0], sibling)
    remote(WAIT, ms2, mr2, mss.at[1], msr.at[1], across)
    for h in range(NH):
        for send in (
            send_swap, send_own_x, send_other_x, pass_on, pass_back, send_attended, send_query_grad, send_reduced,
            send_total,
        ):
            send(WAIT, h)
        for n in range(2):
            forward(WAIT, h, n, 0)
            forward(WAIT, h, n, 1)
            send_back(WAIT, h, n)
        arrived(dq_out.at[:, their_cols(h)], dqr.at[h])
        arrived(dk_out.at[:, their_cols(h)], byr.at[h, 0])
        arrived(dv_out.at[:, their_cols(h)], byr.at[h, 1])
    mixed_copy.wait()

def hand_over(*refs):
    sources, results, held, ins, outs = refs[:4], refs[4:8], refs[8], refs[9], refs[10]
    arriving = [pltpu.make_async_copy(sources[n], held.at[n], ins.at[n]) for n in range(4)]
    leaving = [pltpu.make_async_copy(held.at[n], results[n], outs.at[n]) for n in range(4)]
    for copy in arriving:
        copy.start()
    for n in range(4):
        arriving[n].wait()
        leaving[n].start()
    for copy in leaving:
        copy.wait()


def on_device(queries, keys, values, w_out, out_grad, tile_valid):
    dma = pltpu.SemaphoreType.DMA
    any_space = pl.BlockSpec(memory_space=pl.ANY)
    block = jax.ShapeDtypeStruct(queries.shape, BF)
    results = pl.pallas_call(
        kernel,
        out_shape=(block, block, block, block),
        in_specs=[any_space] * 5 + [pl.BlockSpec(memory_space=pltpu.SMEM)],
        out_specs=(any_space, any_space, any_space, any_space),
        scratch_shapes=[
            pltpu.VMEM((NH, 12 * T, 2 * HD), BF),
            pltpu.VMEM((NH, T, 2 * HD), BF),
            pltpu.VMEM((T, HALF), BF),
            pltpu.VMEM((2, T, HALF), BF),
            pltpu.VMEM((2, T, HALF), BF),
            pltpu.VMEM((T, HALF), BF),
            pltpu.VMEM((4, T, FULL), BF),
            pltpu.VMEM((4 * FULL, HALF), BF),
            pltpu.VMEM((4 * FULL, HALF), BF),
            pltpu.VMEM((2, T, HALF), BF),
            pltpu.VMEM((T, HALF), BF),
            pltpu.VMEM((2, T, HALF), BF),
            pltpu.VMEM((2, T, WIN), BF),
            pltpu.VMEM((2, T, HD), F32),
            pltpu.VMEM((2, 1, WIN), F32),
            pltpu.VMEM((NH, 2, SIDE, 2 * HD), BF),
            pltpu.VMEM((NH, 2, SIDE, 2 * HD), BF),
            pltpu.VMEM((NH, 2 * SIDE, 2 * HD), F32),
            pltpu.VMEM((NH, 2, 2 * T, 2 * HD), BF),
            pltpu.VMEM((NH, 2, 2 * T, 2 * HD), BF),
            pltpu.VMEM((NH, 2, T, 2 * HD), BF),
            pltpu.VMEM((2, T, FULL), BF),
            pltpu.VMEM((2, T, FULL), BF),
            pltpu.VMEM((T, FULL), BF),
            pltpu.VMEM((T, FULL), BF),
            pltpu.VMEM((T, FULL), BF),
            pltpu.VMEM((NH, T, 2 * HD), BF),
            pltpu.VMEM((NH, T, 2 * HD), BF),
            pltpu.VMEM((NH, T, 2 * HD), BF),
            dma((6,)),
            dma((NH, 4)),
            dma((NH, 14)),
            dma((NH, 12)),
            dma((NH, 2, 3)),
            dma((NH, 2, 3)),
            dma((NH, 2)),
            dma((NH, 2)),
            dma((NH, 2)),
            dma((NH, 2)),
            dma((3,)),
            dma((3,)),
            dma((2,)),
            dma((2,)),
            dma((NH,)),
            dma((NH,)),
            dma((NH,)),
            dma((NH,)),
            dma((2,)),
            dma((2,)),
            dma((NH, 4)),
            dma((NH, 2)),
            dma((NH, 2)),
            dma((NH,)),
        ],
        compiler_params=pltpu.CompilerParams(
            collective_id=0, has_side_effects=True, vmem_limit_bytes=56 * 1024 * 1024
        ),
    )(queries, keys, values, w_out, out_grad, tile_valid)
    return pl.pallas_call(
        hand_over,
        out_shape=(block, block, block, block),
        in_specs=[any_space] * 4,
        out_specs=(any_space, any_space, any_space, any_space),
        scratch_shapes=[pltpu.VMEM((4, *queries.shape), BF), dma((4,)), dma((4,))],
        compiler_params=pltpu.CompilerParams(vmem_limit_bytes=56 * 1024 * 1024),
    )(*results)


def solution(mesh):
    return jax.shard_map(
        on_device,
        mesh=mesh,
        in_specs=(
            P("tile", "head"),
            P("tile", "head"),
            P("tile", "head"),
            P(None, "head"),
            P("tile", "head"),
            P(),
        ),
        out_specs=(P("tile", "head"), P("tile", "head"), P("tile", "head"), P("tile", "head")),
        check_vma=False,
    )
```

```python
import jax
import jax.numpy as jnp
from jax import lax
from jax.experimental import pallas as pl
from jax.experimental.pallas import tpu as pltpu
from jax.sharding import PartitionSpec as P

HD = 128
GT = 4
GH = 16
T = 160
NH = 3
HALF = NH * HD
FULL = 2 * HALF
WIN = 9 * T
SIDE = 3 * T
LOG2E = 1.4426950408889634
DIRECT_OUT = (0,)
DIRECT_BACK = (2,)
SPLIT = (2,)
MESH = pl.DeviceIdType.MESH
BF = jnp.bfloat16
F32 = jnp.float32


def nt(a, b):
    return lax.dot_general(a, b, (((1,), (1,)), ((), ())), preferred_element_type=F32)


def nn(a, b):
    return lax.dot_general(a, b, (((1,), (0,)), ((), ())), preferred_element_type=F32)


def tn(a, b):
    return lax.dot_general(a, b, (((0,), (0,)), ((), ())), preferred_element_type=F32)


def kernel(
    q_in, k_in, v_in, w_in, g_in, valid,
    mixed, dq_out, dk_out, dv_out,
    kv, kvo, qo, qb, dob, dop, gall, wm, wo, att, attr, dqb, pb, rb_sum, bias,
    xs, rx, acc, zs, rz, ys, ms, mr, ms2, mr2, mo, rb, rb2, rc,
    lsem, hsem, fs, fr, bxs, bxr, bzs, bzr, bys, byr, gs, gr, qs, qr, dqs, dqr, ats, atr, mss, msr, rls, rlr, bcs, bcr,
):
    i = lax.axis_index("tile")
    j = lax.axis_index("head")
    t = i // GH
    g = i % GH
    p = g % 2
    u = g // 2
    d = 2 * p - 1
    e = (u == 3).astype(jnp.int32) - (u == 4).astype(jnp.int32)
    partner = (i + 1 - 2 * p, j)
    near = (t * GH + (g + 2 * d + GH) % GH, j)
    far = (t * GH + (g - 2 * d + GH) % GH, j)
    up = (((t + 1) % GT) * GH + g, j)
    down = (((t + GT - 1) % GT) * GH + g, j)
    eight_off = (t * GH + (g + GH // 2) % GH, j)
    six_off = (t * GH + (g + 6 + 4 * (u == 7).astype(jnp.int32)) % GH, j)
    relay = (t * GH + (g + GH - 6 * e) % GH, j)
    relay_to = eight_off
    back = (((t - e + GT) % GT) * GH + (g + 2 * e), j)
    j1 = j + 1 - 2 * (j % 2)
    j2 = (j + 2) % 4
    j3 = (j1 + 2) % 4
    sibling = (i, j1)
    across = (i, j2)
    has_up = t < GT - 1
    has_down = t > 0
    has_near = (u + d >= 0) & (u + d < GH // 2)
    has_far = (u - d >= 0) & (u - d < GH // 2)
    near_cross = e == d
    far_cross = e == -d
    is_cross = e != 0
    is_relay = (u == 0) | (u == 7)
    has_back = (t - e >= 0) & (t - e < GT)
    has_ahead = (t + e >= 0) & (t + e < GT)
    mine = pl.multiple_of(p * HALF, 128)
    theirs = pl.multiple_of((1 - p) * HALF, 128)
    scale = HD ** (-0.5)

    @pl.when(jnp.logical_not(has_down))
    def _():
        for s in (0, 3, 6, 9):
            kv[:, pl.ds(s * T, T), :] = jnp.zeros((NH, T, 2 * HD), BF)
        rz[:, 1] = jnp.zeros((NH, 2 * T, 2 * HD), BF)

    @pl.when(jnp.logical_not(has_up))
    def _():
        for s in (2, 5, 8, 11):
            kv[:, pl.ds(s * T, T), :] = jnp.zeros((NH, T, 2 * HD), BF)
        rz[:, 0] = jnp.zeros((NH, 2 * T, 2 * HD), BF)

    for n, side, there, crossing in ((0, 0, has_near, near_cross), (1, 3, has_far, far_cross)):
        @pl.when(jnp.logical_not(there))
        def _():
            kv[:, pl.ds(side * SIDE, SIDE), :] = jnp.zeros((NH, SIDE, 2 * HD), BF)

        @pl.when(jnp.logical_not(there) | crossing)
        def _():
            rx[:, n] = jnp.zeros((NH, SIDE, 2 * HD), BF)

    barrier = pltpu.get_barrier_semaphore()
    greeted = 0
    for peer, cond in (
        (partner, None), (sibling, None), (across, None), (near, has_near), (far, has_far), (up, has_up),
        (down, has_down), (eight_off, is_cross | is_relay), (six_off, is_relay),
        (relay, is_cross), (back, is_cross & has_back),
    ):
        if cond is None:
            pl.semaphore_signal(barrier, inc=1, device_id=peer, device_id_type=MESH)
            greeted += 1
        else:
            @pl.when(cond)
            def _():
                pl.semaphore_signal(barrier, inc=1, device_id=peer, device_id_type=MESH)
            greeted += cond.astype(jnp.int32)

    START, WAIT = 0, 1

    def when(cond, action):
        if cond is None:
            action()
        else:
            @pl.when(cond)
            def _():
                action()

    def remote(act, src, dst, send, recv, device, cond=None):
        copy = pltpu.make_async_remote_copy(
            src_ref=src, dst_ref=dst, send_sem=send, recv_sem=recv, device_id=device, device_id_type=MESH
        )
        when(cond, copy.start if act == START else copy.wait_send)

    def arrived(dst, recv, cond=None):
        copy = pltpu.make_async_remote_copy(
            src_ref=dst, dst_ref=dst, send_sem=lsem.at[0], recv_sem=recv, device_id=partner, device_id_type=MESH
        )
        when(cond, copy.wait_recv)

    def slot(h, s):
        return kv.at[h, pl.ds(s * T, T), :]

    def cols(h):
        return pl.ds(pl.multiple_of(h * HD, HD), HD)

    def mine_cols(h):
        return pl.ds(pl.multiple_of(mine + h * HD, HD), HD)

    def their_cols(h):
        return pl.ds(pl.multiple_of(theirs + h * HD, HD), HD)

    def local(src, dst, sem):
        copy = pltpu.make_async_copy(src, dst, sem)
        copy.start()
        return copy

    staged = [
        [
            local(k_in.at[:, their_cols(h)], kvo.at[h, :, pl.ds(0, HD)], hsem.at[h, 0]),
            local(v_in.at[:, their_cols(h)], kvo.at[h, :, pl.ds(HD, HD)], hsem.at[h, 1]),
        ]
        for h in range(NH)
    ]
    kept_tiles = [
        [
            local(k_in.at[:, mine_cols(h)], slot(h, 4).at[:, pl.ds(0, HD)], hsem.at[h, 2]),
            local(v_in.at[:, mine_cols(h)], slot(h, 4).at[:, pl.ds(HD, HD)], hsem.at[h, 3]),
        ]
        for h in range(NH)
    ]
    g_copy = local(g_in, gall.at[0], lsem.at[0])
    q_copy = local(q_in.at[:, pl.ds(mine, HALF)], qb.at[0], lsem.at[1])
    qo_copy = local(q_in.at[:, pl.ds(theirs, HALF)], qo, lsem.at[2])
    w_copies = [
        local(w_in.at[:, pl.ds(theirs, HALF)], wo, lsem.at[3]),
        local(w_in.at[:, pl.ds(mine, HALF)], wm, lsem.at[4]),
    ]

    lanes = lax.broadcasted_iota(jnp.int32, (1, WIN), 1)
    ones = jnp.ones((WIN, HD), BF)
    for a in range(2):
        row = jnp.zeros((1, WIN), F32)
        for n in range(9):
            g_slot, t_slot = a + n // 3, n % 3
            t_abs = t + t_slot - 1
            g_abs = g + (g_slot - 1) * (1 - 2 * p)
            if t_slot == 1 and g_slot == a + 1:
                value = jnp.float32(0.0)
            else:
                flag = valid[((t_abs + GT) % GT) * GH + (g_abs + GH) % GH]
                inside = (t_abs >= 0) & (t_abs < GT) & (g_abs >= 0) & (g_abs < GH)
                value = jnp.where(inside & (flag > 0), 0.0, -jnp.inf).astype(F32)
            row = jnp.where((lanes >= n * T) & (lanes < (n + 1) * T), value, row)
        bias[a] = row

    pl.semaphore_wait(barrier, greeted)

    def send_side(act, h, s, target, n, device, there, crossing):
        tile = slot(h, s)
        direct = there if h in DIRECT_OUT else there & jnp.logical_not(crossing)
        remote(act, tile, slot(h, target), fs.at[h, n], fr.at[h, target], device, direct)
        if h not in DIRECT_OUT:
            remote(act, tile, rb.at[h], rls.at[h, 0], rlr.at[h, 0], relay, crossing)
        remote(
            act, tile, slot(h, target + e), fs.at[h, n + 1], fr.at[h, target + e], back, crossing & has_back
        )

    def send_swap(act, h):
        remote(act, kvo.at[h], slot(h, 7), fs.at[h, 12], fr.at[h, 7], partner)

    def send_z(act, h, s):
        remote(act, slot(h, s), slot(h, s - 1), fs.at[h, 0 if s == 4 else 2], fr.at[h, s - 1], up, has_up)
        remote(act, slot(h, s), slot(h, s + 1), fs.at[h, 1 if s == 4 else 3], fr.at[h, s + 1], down, has_down)

    def send_own_x(act, h):
        send_side(act, h, 4, 10, 4, near, has_near, near_cross)

    def send_other_x(act, h):
        send_side(act, h, 7, 1, 6, far, has_far, far_cross)

    def pass_on(act, h):
        if h in DIRECT_OUT:
            return
        if act == START:
            arrived(rb.at[h], rlr.at[h, 0], is_relay)
        target = jnp.where((u == 0) == (p == 1), 10, 1)
        remote(act, rb.at[h], slot(h, target), rls.at[h, 1], fr.at[h, target], relay_to, is_relay)

    def forward(act, h, n, k):
        target, device, there, crossing = ((9, near, has_near, near_cross), (0, far, has_far, far_cross))[n]
        exists, way = ((has_down, 1), (has_up, -1))[k]
        source = slot(h, 3 + 3 * n + 2 * k)
        if act == START:
            arrived(source, fr.at[h, 3 + 3 * n + 2 * k], exists)
        remote(
            act, source, slot(h, target + 2 * k), fs.at[h, 8 + 2 * n + k], fr.at[h, target + 2 * k], device,
            exists & there & (jnp.logical_not(crossing) | (e == way)),
        )

    def parts_of(h):
        return (1, 0) if h in SPLIT else (None,)

    def lanes_of(part):
        return (0, pl.ds(0, 2 * HD)) if part is None else (part, pl.ds(part * HD, HD))

    def send_back(act, h, n, part):
        k, lane = lanes_of(part)
        device, there, crossing = ((far, has_far, far_cross), (near, has_near, near_cross))[n]
        remote(
            act, xs.at[h, n, :, lane], rx.at[h, n, :, lane], bxs.at[h, n, k, 0], bxr.at[h, n, k, 0], device,
            there & jnp.logical_not(crossing),
        )
        middle = pl.ds(T, T)
        if h in DIRECT_BACK:
            remote(
                act, xs.at[h, n, middle, lane], rx.at[h, n, middle, lane], bxs.at[h, n, k, 2], bxr.at[h, n, k, 1],
                device, crossing,
            )
        else:
            remote(act, xs.at[h, n, middle], rb2.at[h], rls.at[h, 2], rlr.at[h, 1], relay, crossing)
        rows = pl.ds((1 + e) * T, T)
        remote(
            act, xs.at[h, n, rows, lane], rx.at[h, n, rows, lane], bxs.at[h, n, k, 1], bxr.at[h, n, k, 2], device,
            crossing & has_ahead,
        )
        remote(
            act, xs.at[h, n, pl.ds((1 - e) * T, T), lane], rc.at[h, :, lane], bcs.at[h, n, k], bcr.at[h, k], back,
            crossing & has_back,
        )

    def pass_back(act, h):
        if h in DIRECT_BACK:
            return
        if act == START:
            arrived(rb2.at[h], rlr.at[h, 1], is_relay)
        n = jnp.where(u == 0, p, 1 - p)
        remote(act, rb2.at[h], rx.at[h, n, pl.ds(T, T)], rls.at[h, 3], bxr.at[h, n, 0, 1], relay_to, is_relay)

    def send_attended(act, h):
        remote(act, att.at[1, :, cols(h)], attr.at[:, cols(h)], ats.at[h], atr.at[h], partner)

    def send_query_grad(act, h):
        remote(act, dqb.at[1, :, cols(h)], dq_out.at[:, mine_cols(h)], dqs.at[h], dqr.at[h], partner)
        copy = pltpu.make_async_copy(dqb.at[0, :, cols(h)], dq_out.at[:, mine_cols(h)], hsem.at[h, 2])
        if act == START:
            copy.start()
        else:
            copy.wait()

    def send_reduced(act, h, part):
        k, lane = lanes_of(part)
        remote(act, zs.at[h, 0, :, lane], rz.at[h, 0, :, lane], bzs.at[h, 0, k], bzr.at[h, 0, k], down, has_down)
        remote(act, zs.at[h, 1, :, lane], rz.at[h, 1, :, lane], bzs.at[h, 1, k], bzr.at[h, 1, k], up, has_up)

    def send_total(act, h, part):
        for n, out in enumerate((dk_out, dv_out)):
            if part is not None and n != part:
                continue
            lane = pl.ds(n * HD, HD)
            remote(act, ys.at[h, 1, :, lane], out.at[:, mine_cols(h)], bys.at[h, n], byr.at[h, n], partner)
            copy = pltpu.make_async_copy(ys.at[h, 0, :, lane], out.at[:, mine_cols(h)], hsem.at[h, n])
            if act == START:
                copy.start()
            else:
                copy.wait()

    def attend(h):
        for s, there in ((9, has_far & has_down), (10, has_far), (11, has_far & has_up),
                         (0, has_near & has_down), (1, has_near), (2, has_near & has_up)):
            arrived(slot(h, s), fr.at[h, s], there)
        for a in range(2):
            window = pl.ds(a * SIDE, WIN)
            s = nt(qb[a, :, cols(h)], kv[h, window, pl.ds(0, HD)]) * (scale * LOG2E) + bias[a]
            x = jnp.exp2(s - jnp.max(s, axis=1, keepdims=True)).astype(BF)
            pb[a] = x
            total = nn(x, jnp.concatenate([kv[h, window, pl.ds(HD, HD)], ones], axis=1))
            inverse = 1.0 / total[:, HD:]
            rb_sum[a] = inverse
            att[a, :, cols(h)] = (total[:, :HD] * inverse).astype(BF)
        send_attended(START, h)

    def add_part(h, a, part, grad):
        lane = pl.ds(part * HD, HD)
        if a == 0:
            xs[h, 1, :, lane] = grad[:SIDE].astype(BF)
            acc[h, :, lane] = grad[SIDE:]
        else:
            acc[h, :, lane] += grad[:2 * SIDE]
            xs[h, 0, :, lane] = grad[2 * SIDE:].astype(BF)

    def value_part(h, a):
        add_part(h, a, 1, tn(pb[a], (dob[a, :, cols(h)].astype(F32) * rb_sum[a]).astype(BF)))

    def key_part(h, a):
        q = qb[a, :, cols(h)]
        do = dob[a, :, cols(h)].astype(F32)
        window = pl.ds(a * SIDE, WIN)
        k = kv[h, window, pl.ds(0, HD)]
        scaled = rb_sum[a] * scale
        row_dot = jnp.sum(do * att[a, :, cols(h)].astype(F32) * scaled, axis=1, keepdims=True)
        weight_grad = nt((do * scaled).astype(BF), kv[h, window, pl.ds(HD, HD)])
        score_grad = pb[a] * (weight_grad - row_dot).astype(BF)
        dqb[a, :, cols(h)] = nn(score_grad, k).astype(BF)
        add_part(h, a, 0, tn(score_grad, q))

    def differentiate(h, a):
        key_part(h, a)
        value_part(h, a)
        send_back(START, h, 1 - a, None)
        if a == 1:
            send_query_grad(START, h)

    def differentiate_values(h):
        for a in range(2):
            value_part(h, a)
            send_back(START, h, 1 - a, 1)

    def differentiate_keys(h):
        for a in range(2):
            key_part(h, a)
            send_back(START, h, 1 - a, 0)
        send_query_grad(START, h)

    def reduce_x(h, part):
        k, lane = lanes_of(part)
        for n, there, crossing in ((0, has_near, near_cross), (1, has_far, far_cross)):
            arrived(rx.at[h, n, :, lane], bxr.at[h, n, k, 0], there & jnp.logical_not(crossing))
            arrived(rx.at[h, n, pl.ds(T, T), lane], bxr.at[h, n, k, 1], crossing)
            arrived(rx.at[h, n, pl.ds((1 - e) * T, T), lane], bxr.at[h, n, k, 2], crossing & has_back)
        for n in range(2):
            for side, row in ((0, 0), (1, 2 * T)):
                zs[h, side, pl.ds(n * T, T), lane] = (
                    acc[h, pl.ds(n * SIDE + row, T), lane] + rx[h, n, pl.ds(row, T), lane].astype(F32)
                ).astype(BF)
            acc[h, pl.ds(n * SIDE + T, T), lane] += rx[h, n, pl.ds(T, T), lane].astype(F32)
        send_reduced(START, h, part)

    def reduce_z(h, part):
        k, lane = lanes_of(part)
        arrived(rz.at[h, 0, :, lane], bzr.at[h, 0, k], has_up)
        arrived(rz.at[h, 1, :, lane], bzr.at[h, 1, k], has_down)
        arrived(rc.at[h, :, lane], bcr.at[h, k], is_cross & has_back)
        for n, crossing in ((0, near_cross), (1, far_cross)):
            @pl.when(crossing & has_back)
            def _():
                acc[h, pl.ds(n * SIDE + T, T), lane] += rc[h, :, lane].astype(F32)

        for n in range(2):
            rows = pl.ds(n * T, T)
            ys[h, n, :, lane] = (
                acc[h, pl.ds(n * SIDE + T, T), lane]
                + rz[h, 0, rows, lane].astype(F32)
                + rz[h, 1, rows, lane].astype(F32)
            ).astype(BF)
        send_total(START, h, part)

    blocks = (j, j1, j2, j3)
    rows = [pl.ds(pl.multiple_of(block * FULL, FULL), FULL) for block in blocks]

    def send_gathered(act, n):
        source, target, device, k = ((0, 2, across, 1), (0, 1, sibling, 0), (2, 3, sibling, 2))[n]
        remote(act, gall.at[source], gall.at[target], gs.at[k], gr.at[k], device)

    def send_queries(act):
        remote(act, qo, qb.at[1], qs.at[0], qr.at[0], partner)

    def attn_grad(weights_ref):
        total = nn(gall[0], weights_ref[rows[0], :])
        for k in range(1, 4):
            total = total + nn(gall[k], weights_ref[rows[k], :])
        return total.astype(BF)

    def send_attn_grad(act):
        remote(act, dop, dob.at[1], qs.at[1], qr.at[1], partner)

    def project(n):
        return nt(att[0], wm[rows[n], :]) + nt(attr[...], wo[rows[n], :])

    for copy in staged[0]:
        copy.wait()
    send_swap(START, 0)
    for copy in kept_tiles[0]:
        copy.wait()
    send_z(START, 0, 4)
    for copy in staged[1]:
        copy.wait()
    send_swap(START, 1)
    arrived(slot(0, 7), fr.at[0, 7])
    send_z(START, 0, 7)
    g_copy.wait()
    send_gathered(START, 0)
    send_own_x(START, 0)
    for copy in kept_tiles[1]:
        copy.wait()
    send_z(START, 1, 4)
    for copy in staged[2]:
        copy.wait()
    send_swap(START, 2)
    arrived(slot(1, 7), fr.at[1, 7])
    send_z(START, 1, 7)
    forward(START, 0, 0, 0)
    send_other_x(START, 0)
    forward(START, 0, 0, 1)
    forward(START, 0, 1, 0)
    qo_copy.wait()
    send_queries(START)
    send_other_x(START, 1)
    send_own_x(START, 1)
    arrived(gall.at[2], gr.at[1])
    send_gathered(START, 2)
    send_gathered(START, 1)
    forward(START, 0, 1, 1)
    pass_on(START, 0)
    arrived(slot(2, 7), fr.at[2, 7])
    send_z(START, 2, 7)
    forward(START, 1, 0, 0)
    for copy in w_copies:
        copy.wait()
    arrived(gall.at[1], gr.at[0])
    arrived(gall.at[3], gr.at[2])
    dop[...] = attn_grad(wo)
    send_attn_grad(START)
    dob[0] = attn_grad(wm)
    for copy in kept_tiles[2]:
        copy.wait()
    send_z(START, 2, 4)
    forward(START, 1, 1, 1)
    send_other_x(START, 2)
    send_own_x(START, 2)
    pass_on(START, 1)
    forward(START, 1, 0, 1)
    q_copy.wait()
    arrived(qb.at[1], qr.at[0])
    attend(0)
    forward(START, 1, 1, 0)
    arrived(dob.at[1], qr.at[1])
    differentiate(0, 0)
    differentiate(0, 1)
    forward(START, 2, 1, 1)
    forward(START, 2, 1, 0)
    forward(START, 2, 0, 0)
    attend(1)
    forward(START, 2, 0, 1)
    pass_back(START, 0)
    pass_on(START, 2)
    differentiate(1, 0)
    differentiate(1, 1)
    reduce_x(0, None)
    attend(2)
    pass_back(START, 1)
    differentiate_values(2)
    differentiate_keys(2)
    reduce_x(1, None)
    for h in range(NH):
        arrived(attr.at[:, cols(h)], atr.at[h])
    ms[0] = project(3).astype(BF)
    ms[1] = project(1).astype(BF)
    remote(START, ms, mr, mss.at[0], msr.at[0], sibling)
    reduce_x(2, 1)
    crossing_sum = project(2)
    arrived(mr, msr.at[0])
    ms2[...] = (crossing_sum + mr[0].astype(F32)).astype(BF)
    remote(START, ms2, mr2, mss.at[1], msr.at[1], across)
    kept = project(0) + mr[1].astype(F32)
    reduce_x(2, 0)
    reduce_z(0, None)
    reduce_z(1, None)
    reduce_z(2, 1)
    reduce_z(2, 0)
    arrived(mr2, msr.at[1])
    mo[...] = (kept + mr2[...].astype(F32)).astype(BF)
    mixed_copy = local(mo, mixed, lsem.at[5])
    send_z(WAIT, 0, 4)
    send_z(WAIT, 0, 7)
    send_z(WAIT, 1, 4)
    send_z(WAIT, 1, 7)
    send_z(WAIT, 2, 4)
    send_z(WAIT, 2, 7)

    for n in range(3):
        send_gathered(WAIT, n)
    send_queries(WAIT)
    send_attn_grad(WAIT)
    remote(WAIT, ms, mr, mss.at[0], msr.at[0], sibling)
    remote(WAIT, ms2, mr2, mss.at[1], msr.at[1], across)
    for h in range(NH):
        for send in (
            send_swap, send_own_x, send_other_x, pass_on, pass_back, send_attended, send_query_grad,
        ):
            send(WAIT, h)
        for n in range(2):
            forward(WAIT, h, n, 0)
            forward(WAIT, h, n, 1)
            for part in parts_of(h):
                send_back(WAIT, h, n, part)
        for part in parts_of(h):
            send_reduced(WAIT, h, part)
            send_total(WAIT, h, part)
        arrived(dq_out.at[:, their_cols(h)], dqr.at[h])
        arrived(dk_out.at[:, their_cols(h)], byr.at[h, 0])
        arrived(dv_out.at[:, their_cols(h)], byr.at[h, 1])
    mixed_copy.wait()

def hand_over(*refs):
    sources, results, held, ins, outs = refs[:4], refs[4:8], refs[8], refs[9], refs[10]
    arriving = [pltpu.make_async_copy(sources[n], held.at[n], ins.at[n]) for n in range(4)]
    leaving = [pltpu.make_async_copy(held.at[n], results[n], outs.at[n]) for n in range(4)]
    for copy in arriving:
        copy.start()
    for n in range(4):
        arriving[n].wait()
        leaving[n].start()
    for copy in leaving:
        copy.wait()


def on_device(queries, keys, values, w_out, out_grad, tile_valid):
    dma = pltpu.SemaphoreType.DMA
    any_space = pl.BlockSpec(memory_space=pl.ANY)
    block = jax.ShapeDtypeStruct(queries.shape, BF)
    results = pl.pallas_call(
        kernel,
        out_shape=(block, block, block, block),
        in_specs=[any_space] * 5 + [pl.BlockSpec(memory_space=pltpu.SMEM)],
        out_specs=(any_space, any_space, any_space, any_space),
        scratch_shapes=[
            pltpu.VMEM((NH, 12 * T, 2 * HD), BF),
            pltpu.VMEM((NH, T, 2 * HD), BF),
            pltpu.VMEM((T, HALF), BF),
            pltpu.VMEM((2, T, HALF), BF),
            pltpu.VMEM((2, T, HALF), BF),
            pltpu.VMEM((T, HALF), BF),
            pltpu.VMEM((4, T, FULL), BF),
            pltpu.VMEM((4 * FULL, HALF), BF),
            pltpu.VMEM((4 * FULL, HALF), BF),
            pltpu.VMEM((2, T, HALF), BF),
            pltpu.VMEM((T, HALF), BF),
            pltpu.VMEM((2, T, HALF), BF),
            pltpu.VMEM((2, T, WIN), BF),
            pltpu.VMEM((2, T, HD), F32),
            pltpu.VMEM((2, 1, WIN), F32),
            pltpu.VMEM((NH, 2, SIDE, 2 * HD), BF),
            pltpu.VMEM((NH, 2, SIDE, 2 * HD), BF),
            pltpu.VMEM((NH, 2 * SIDE, 2 * HD), F32),
            pltpu.VMEM((NH, 2, 2 * T, 2 * HD), BF),
            pltpu.VMEM((NH, 2, 2 * T, 2 * HD), BF),
            pltpu.VMEM((NH, 2, T, 2 * HD), BF),
            pltpu.VMEM((2, T, FULL), BF),
            pltpu.VMEM((2, T, FULL), BF),
            pltpu.VMEM((T, FULL), BF),
            pltpu.VMEM((T, FULL), BF),
            pltpu.VMEM((T, FULL), BF),
            pltpu.VMEM((NH, T, 2 * HD), BF),
            pltpu.VMEM((NH, T, 2 * HD), BF),
            pltpu.VMEM((NH, T, 2 * HD), BF),
            dma((6,)),
            dma((NH, 4)),
            dma((NH, 14)),
            dma((NH, 12)),
            dma((NH, 2, 2, 3)),
            dma((NH, 2, 2, 3)),
            dma((NH, 2, 2)),
            dma((NH, 2, 2)),
            dma((NH, 2)),
            dma((NH, 2)),
            dma((3,)),
            dma((3,)),
            dma((2,)),
            dma((2,)),
            dma((NH,)),
            dma((NH,)),
            dma((NH,)),
            dma((NH,)),
            dma((2,)),
            dma((2,)),
            dma((NH, 4)),
            dma((NH, 2)),
            dma((NH, 2, 2)),
            dma((NH, 2)),
        ],
        compiler_params=pltpu.CompilerParams(
            collective_id=0, has_side_effects=True, vmem_limit_bytes=56 * 1024 * 1024
        ),
    )(queries, keys, values, w_out, out_grad, tile_valid)
    return pl.pallas_call(
        hand_over,
        out_shape=(block, block, block, block),
        in_specs=[any_space] * 4,
        out_specs=(any_space, any_space, any_space, any_space),
        scratch_shapes=[pltpu.VMEM((4, *queries.shape), BF), dma((4,)), dma((4,))],
        compiler_params=pltpu.CompilerParams(vmem_limit_bytes=56 * 1024 * 1024),
    )(*results)


def solution(mesh):
    return jax.shard_map(
        on_device,
        mesh=mesh,
        in_specs=(
            P("tile", "head"),
            P("tile", "head"),
            P("tile", "head"),
            P(None, "head"),
            P("tile", "head"),
            P(),
        ),
        out_specs=(P("tile", "head"), P("tile", "head"), P("tile", "head"), P("tile", "head")),
        check_vma=False,
    )
```

```python
import jax
import jax.numpy as jnp
from jax import lax
from jax.experimental import pallas as pl
from jax.experimental.pallas import tpu as pltpu
from jax.sharding import PartitionSpec as P

HD = 128
GT = 4
GH = 16
T = 160
NH = 3
HALF = NH * HD
FULL = 2 * HALF
WIN = 9 * T
SIDE = 3 * T
LOG2E = 1.4426950408889634
DIRECT_OUT = (0,)
DIRECT_BACK = (2,)
SPLIT = ()
MESH = pl.DeviceIdType.MESH
BF = jnp.bfloat16
F32 = jnp.float32


def nt(a, b):
    return lax.dot_general(a, b, (((1,), (1,)), ((), ())), preferred_element_type=F32)


def nn(a, b):
    return lax.dot_general(a, b, (((1,), (0,)), ((), ())), preferred_element_type=F32)


def tn(a, b):
    return lax.dot_general(a, b, (((0,), (0,)), ((), ())), preferred_element_type=F32)


def kernel(
    q_in, k_in, v_in, w_in, g_in, valid,
    mixed, dq_out, dk_out, dv_out,
    kv, kvo, qo, qb, dob, dop, gall, wm, wo, att, attr, dqb, dql, pb, rb_sum, bias,
    xs, rx, acc, zs, rz, ys, yr, ms, mr, ms2, mr2, res, kin, vin, qin, rb, rb2, rc,
    lsem, hsem, fs, fr, bxs, bxr, bzs, bzr, bys, byr, gs, gr, qs, qr, dqs, dqr, ats, atr, mss, msr, rls, rlr, bcs, bcr,
):
    i = lax.axis_index("tile")
    j = lax.axis_index("head")
    t = i // GH
    g = i % GH
    p = g % 2
    u = g // 2
    d = 2 * p - 1
    e = (u == 3).astype(jnp.int32) - (u == 4).astype(jnp.int32)
    partner = (i + 1 - 2 * p, j)
    near = (t * GH + (g + 2 * d + GH) % GH, j)
    far = (t * GH + (g - 2 * d + GH) % GH, j)
    up = (((t + 1) % GT) * GH + g, j)
    down = (((t + GT - 1) % GT) * GH + g, j)
    eight_off = (t * GH + (g + GH // 2) % GH, j)
    six_off = (t * GH + (g + 6 + 4 * (u == 7).astype(jnp.int32)) % GH, j)
    relay = (t * GH + (g + GH - 6 * e) % GH, j)
    relay_to = eight_off
    back = (((t - e + GT) % GT) * GH + (g + 2 * e), j)
    j1 = j + 1 - 2 * (j % 2)
    j2 = (j + 2) % 4
    j3 = (j1 + 2) % 4
    sibling = (i, j1)
    across = (i, j2)
    has_up = t < GT - 1
    has_down = t > 0
    has_near = (u + d >= 0) & (u + d < GH // 2)
    has_far = (u - d >= 0) & (u - d < GH // 2)
    near_cross = e == d
    far_cross = e == -d
    is_cross = e != 0
    is_relay = (u == 0) | (u == 7)
    has_back = (t - e >= 0) & (t - e < GT)
    has_ahead = (t + e >= 0) & (t + e < GT)
    mine = pl.multiple_of(p * HALF, 128)
    theirs = pl.multiple_of((1 - p) * HALF, 128)
    scale = HD ** (-0.5)

    @pl.when(jnp.logical_not(has_down))
    def _():
        for s in (0, 3, 6, 9):
            kv[:, pl.ds(s * T, T), :] = jnp.zeros((NH, T, 2 * HD), BF)
        rz[:, 1] = jnp.zeros((NH, 2 * T, 2 * HD), BF)

    @pl.when(jnp.logical_not(has_up))
    def _():
        for s in (2, 5, 8, 11):
            kv[:, pl.ds(s * T, T), :] = jnp.zeros((NH, T, 2 * HD), BF)
        rz[:, 0] = jnp.zeros((NH, 2 * T, 2 * HD), BF)

    for n, side, there, crossing in ((0, 0, has_near, near_cross), (1, 3, has_far, far_cross)):
        @pl.when(jnp.logical_not(there))
        def _():
            kv[:, pl.ds(side * SIDE, SIDE), :] = jnp.zeros((NH, SIDE, 2 * HD), BF)

        @pl.when(jnp.logical_not(there) | crossing)
        def _():
            rx[:, n] = jnp.zeros((NH, SIDE, 2 * HD), BF)

    barrier = pltpu.get_barrier_semaphore()
    greeted = 0
    for peer, cond in (
        (partner, None), (sibling, None), (across, None), (near, has_near), (far, has_far), (up, has_up),
        (down, has_down), (eight_off, is_cross | is_relay), (six_off, is_relay),
        (relay, is_cross), (back, is_cross & has_back),
    ):
        if cond is None:
            pl.semaphore_signal(barrier, inc=1, device_id=peer, device_id_type=MESH)
            greeted += 1
        else:
            @pl.when(cond)
            def _():
                pl.semaphore_signal(barrier, inc=1, device_id=peer, device_id_type=MESH)
            greeted += cond.astype(jnp.int32)

    START, WAIT = 0, 1

    def when(cond, action):
        if cond is None:
            action()
        else:
            @pl.when(cond)
            def _():
                action()

    def remote(act, src, dst, send, recv, device, cond=None):
        copy = pltpu.make_async_remote_copy(
            src_ref=src, dst_ref=dst, send_sem=send, recv_sem=recv, device_id=device, device_id_type=MESH
        )
        when(cond, copy.start if act == START else copy.wait_send)

    def arrived(dst, recv, cond=None):
        copy = pltpu.make_async_remote_copy(
            src_ref=dst, dst_ref=dst, send_sem=lsem.at[0], recv_sem=recv, device_id=partner, device_id_type=MESH
        )
        when(cond, copy.wait_recv)

    def slot(h, s):
        return kv.at[h, pl.ds(s * T, T), :]

    def cols(h):
        return pl.ds(pl.multiple_of(h * HD, HD), HD)

    def mine_cols(h):
        return pl.ds(pl.multiple_of(mine + h * HD, HD), HD)

    def their_cols(h):
        return pl.ds(pl.multiple_of(theirs + h * HD, HD), HD)

    def local(src, dst, sem):
        copy = pltpu.make_async_copy(src, dst, sem)
        copy.start()
        return copy

    k_copy = local(k_in, kin, hsem.at[0])
    v_copy = local(v_in, vin, hsem.at[1])
    g_copy = local(g_in, gall.at[0], lsem.at[0])
    q_copy = local(q_in, qin, lsem.at[1])
    w_copies = [
        local(w_in.at[:, pl.ds(theirs, HALF)], wo, lsem.at[3]),
        local(w_in.at[:, pl.ds(mine, HALF)], wm, lsem.at[4]),
    ]

    lanes = lax.broadcasted_iota(jnp.int32, (1, WIN), 1)
    ones = jnp.ones((WIN, HD), BF)
    for a in range(2):
        row = jnp.zeros((1, WIN), F32)
        for n in range(9):
            g_slot, t_slot = a + n // 3, n % 3
            t_abs = t + t_slot - 1
            g_abs = g + (g_slot - 1) * (1 - 2 * p)
            if t_slot == 1 and g_slot == a + 1:
                value = jnp.float32(0.0)
            else:
                flag = valid[((t_abs + GT) % GT) * GH + (g_abs + GH) % GH]
                inside = (t_abs >= 0) & (t_abs < GT) & (g_abs >= 0) & (g_abs < GH)
                value = jnp.where(inside & (flag > 0), 0.0, -jnp.inf).astype(F32)
            row = jnp.where((lanes >= n * T) & (lanes < (n + 1) * T), value, row)
        bias[a] = row

    pl.semaphore_wait(barrier, greeted)

    def send_side(act, h, s, target, n, device, there, crossing):
        tile = slot(h, s)
        direct = there if h in DIRECT_OUT else there & jnp.logical_not(crossing)
        remote(act, tile, slot(h, target), fs.at[h, n], fr.at[h, target], device, direct)
        if h not in DIRECT_OUT:
            remote(act, tile, rb.at[h], rls.at[h, 0], rlr.at[h, 0], relay, crossing)
        remote(
            act, tile, slot(h, target + e), fs.at[h, n + 1], fr.at[h, target + e], back, crossing & has_back
        )

    def send_swap(act, h):
        remote(act, kvo.at[h], slot(h, 7), fs.at[h, 12], fr.at[h, 7], partner)

    def send_z(act, h, s):
        remote(act, slot(h, s), slot(h, s - 1), fs.at[h, 0 if s == 4 else 2], fr.at[h, s - 1], up, has_up)
        remote(act, slot(h, s), slot(h, s + 1), fs.at[h, 1 if s == 4 else 3], fr.at[h, s + 1], down, has_down)

    def send_own_x(act, h):
        send_side(act, h, 4, 10, 4, near, has_near, near_cross)

    def send_other_x(act, h):
        send_side(act, h, 7, 1, 6, far, has_far, far_cross)

    def pass_on(act, h):
        if h in DIRECT_OUT:
            return
        if act == START:
            arrived(rb.at[h], rlr.at[h, 0], is_relay)
        target = jnp.where((u == 0) == (p == 1), 10, 1)
        remote(act, rb.at[h], slot(h, target), rls.at[h, 1], fr.at[h, target], relay_to, is_relay)

    def forward(act, h, n, k):
        target, device, there, crossing = ((9, near, has_near, near_cross), (0, far, has_far, far_cross))[n]
        exists, way = ((has_down, 1), (has_up, -1))[k]
        source = slot(h, 3 + 3 * n + 2 * k)
        if act == START:
            arrived(source, fr.at[h, 3 + 3 * n + 2 * k], exists)
        remote(
            act, source, slot(h, target + 2 * k), fs.at[h, 8 + 2 * n + k], fr.at[h, target + 2 * k], device,
            exists & there & (jnp.logical_not(crossing) | (e == way)),
        )

    def parts_of(h):
        return (1, 0) if h in SPLIT else (None,)

    def lanes_of(part):
        return (0, pl.ds(0, 2 * HD)) if part is None else (part, pl.ds(part * HD, HD))

    def send_back(act, h, n, part):
        k, lane = lanes_of(part)
        device, there, crossing = ((far, has_far, far_cross), (near, has_near, near_cross))[n]
        remote(
            act, xs.at[h, n, :, lane], rx.at[h, n, :, lane], bxs.at[h, n, k, 0], bxr.at[h, n, k, 0], device,
            there & jnp.logical_not(crossing),
        )
        middle = pl.ds(T, T)
        if h in DIRECT_BACK:
            remote(
                act, xs.at[h, n, middle, lane], rx.at[h, n, middle, lane], bxs.at[h, n, k, 2], bxr.at[h, n, k, 1],
                device, crossing,
            )
        else:
            remote(act, xs.at[h, n, middle], rb2.at[h], rls.at[h, 2], rlr.at[h, 1], relay, crossing)
        rows = pl.ds((1 + e) * T, T)
        remote(
            act, xs.at[h, n, rows, lane], rx.at[h, n, rows, lane], bxs.at[h, n, k, 1], bxr.at[h, n, k, 2], device,
            crossing & has_ahead,
        )
        remote(
            act, xs.at[h, n, pl.ds((1 - e) * T, T), lane], rc.at[h, :, lane], bcs.at[h, n, k], bcr.at[h, k], back,
            crossing & has_back,
        )

    def pass_back(act, h):
        if h in DIRECT_BACK:
            return
        if act == START:
            arrived(rb2.at[h], rlr.at[h, 1], is_relay)
        n = jnp.where(u == 0, p, 1 - p)
        remote(act, rb2.at[h], rx.at[h, n, pl.ds(T, T)], rls.at[h, 3], bxr.at[h, n, 0, 1], relay_to, is_relay)

    def send_attended(act, h):
        remote(act, att.at[1, :, cols(h)], attr.at[:, cols(h)], ats.at[h], atr.at[h], partner)

    def send_query_grad(act, h):
        remote(act, dqb.at[:, cols(h)], dql.at[:, cols(h)], dqs.at[h], dqr.at[h], partner)

    def send_reduced(act, h, part):
        k, lane = lanes_of(part)
        remote(act, zs.at[h, 0, :, lane], rz.at[h, 0, :, lane], bzs.at[h, 0, k], bzr.at[h, 0, k], down, has_down)
        remote(act, zs.at[h, 1, :, lane], rz.at[h, 1, :, lane], bzs.at[h, 1, k], bzr.at[h, 1, k], up, has_up)

    def send_total(act, h):
        remote(act, ys.at[h], yr.at[h], bys.at[h], byr.at[h], partner)

    def attend(h):
        for s, there in ((9, has_far & has_down), (10, has_far), (11, has_far & has_up),
                         (0, has_near & has_down), (1, has_near), (2, has_near & has_up)):
            arrived(slot(h, s), fr.at[h, s], there)
        for a in range(2):
            window = pl.ds(a * SIDE, WIN)
            s = nt(qb[a, :, cols(h)], kv[h, window, pl.ds(0, HD)]) * (scale * LOG2E) + bias[a]
            x = jnp.exp2(s - jnp.max(s, axis=1, keepdims=True)).astype(BF)
            pb[a] = x
            total = nn(x, jnp.concatenate([kv[h, window, pl.ds(HD, HD)], ones], axis=1))
            inverse = 1.0 / total[:, HD:]
            rb_sum[a] = inverse
            att[a, :, cols(h)] = (total[:, :HD] * inverse).astype(BF)
        send_attended(START, h)

    def add_part(h, a, part, grad):
        lane = pl.ds(part * HD, HD)
        if a == 0:
            xs[h, 1, :, lane] = grad[:SIDE].astype(BF)
            acc[h, :, lane] = grad[SIDE:]
        else:
            acc[h, :, lane] += grad[:2 * SIDE]
            xs[h, 0, :, lane] = grad[2 * SIDE:].astype(BF)

    def value_part(h, a):
        add_part(h, a, 1, tn(pb[a], (dob[a, :, cols(h)].astype(F32) * rb_sum[a]).astype(BF)))

    def key_part(h, a):
        q = qb[a, :, cols(h)]
        do = dob[a, :, cols(h)].astype(F32)
        window = pl.ds(a * SIDE, WIN)
        k = kv[h, window, pl.ds(0, HD)]
        scaled = rb_sum[a] * scale
        row_dot = jnp.sum(do * att[a, :, cols(h)].astype(F32) * scaled, axis=1, keepdims=True)
        weight_grad = nt((do * scaled).astype(BF), kv[h, window, pl.ds(HD, HD)])
        score_grad = pb[a] * (weight_grad - row_dot).astype(BF)
        query_grad = nn(score_grad, k).astype(BF)
        if a == 0:
            res[1, :, mine_cols(h)] = query_grad
        else:
            dqb[:, cols(h)] = query_grad
        add_part(h, a, 0, tn(score_grad, q))

    def differentiate(h, a):
        key_part(h, a)
        value_part(h, a)
        send_back(START, h, 1 - a, None)
        if a == 1:
            send_query_grad(START, h)

    def reduce_x(h, part):
        k, lane = lanes_of(part)
        for n, there, crossing in ((0, has_near, near_cross), (1, has_far, far_cross)):
            arrived(rx.at[h, n, :, lane], bxr.at[h, n, k, 0], there & jnp.logical_not(crossing))
            arrived(rx.at[h, n, pl.ds(T, T), lane], bxr.at[h, n, k, 1], crossing)
            arrived(rx.at[h, n, pl.ds((1 - e) * T, T), lane], bxr.at[h, n, k, 2], crossing & has_back)
        for n in range(2):
            for side, row in ((0, 0), (1, 2 * T)):
                zs[h, side, pl.ds(n * T, T), lane] = (
                    acc[h, pl.ds(n * SIDE + row, T), lane] + rx[h, n, pl.ds(row, T), lane].astype(F32)
                ).astype(BF)
            acc[h, pl.ds(n * SIDE + T, T), lane] += rx[h, n, pl.ds(T, T), lane].astype(F32)
        send_reduced(START, h, part)

    def reduce_z(h, part):
        k, lane = lanes_of(part)
        arrived(rz.at[h, 0, :, lane], bzr.at[h, 0, k], has_up)
        arrived(rz.at[h, 1, :, lane], bzr.at[h, 1, k], has_down)
        arrived(rc.at[h, :, lane], bcr.at[h, k], is_cross & has_back)
        for n, crossing in ((0, near_cross), (1, far_cross)):
            @pl.when(crossing & has_back)
            def _():
                acc[h, pl.ds(n * SIDE + T, T), lane] += rc[h, :, lane].astype(F32)

        sums = [
            (
                acc[h, pl.ds(n * SIDE + T, T), :]
                + rz[h, 0, pl.ds(n * T, T), :].astype(F32)
                + rz[h, 1, pl.ds(n * T, T), :].astype(F32)
            ).astype(BF)
            for n in range(2)
        ]
        ys[h] = sums[1]
        send_total(START, h)
        res[2, :, mine_cols(h)] = sums[0][:, :HD]
        res[3, :, mine_cols(h)] = sums[0][:, HD:]

    k_copy.wait()
    v_copy.wait()
    blocks = (j, j1, j2, j3)
    rows = [pl.ds(pl.multiple_of(block * FULL, FULL), FULL) for block in blocks]

    def send_gathered(act, n):
        source, target, device, k = ((0, 2, across, 1), (0, 1, sibling, 0), (2, 3, sibling, 2))[n]
        remote(act, gall.at[source], gall.at[target], gs.at[k], gr.at[k], device)

    def send_queries(act):
        remote(act, qo, qb.at[1], qs.at[0], qr.at[0], partner)

    def attn_grad(weights_ref):
        total = nn(gall[0], weights_ref[rows[0], :])
        for k in range(1, 4):
            total = total + nn(gall[k], weights_ref[rows[k], :])
        return total.astype(BF)

    def send_attn_grad(act):
        remote(act, dop, dob.at[1], qs.at[1], qr.at[1], partner)

    def project(n):
        return nt(att[0], wm[rows[n], :]) + nt(attr[...], wo[rows[n], :])

    kvo[0, :, :HD] = kin[:, their_cols(0)]
    kvo[0, :, HD:] = vin[:, their_cols(0)]
    send_swap(START, 0)
    kv[0, pl.ds(4 * T, T), :HD] = kin[:, mine_cols(0)]
    kv[0, pl.ds(4 * T, T), HD:] = vin[:, mine_cols(0)]
    send_z(START, 0, 4)
    kvo[1, :, :HD] = kin[:, their_cols(1)]
    kvo[1, :, HD:] = vin[:, their_cols(1)]
    send_swap(START, 1)
    arrived(slot(0, 7), fr.at[0, 7])
    send_z(START, 0, 7)
    g_copy.wait()
    send_gathered(START, 0)
    send_own_x(START, 0)
    kv[1, pl.ds(4 * T, T), :HD] = kin[:, mine_cols(1)]
    kv[1, pl.ds(4 * T, T), HD:] = vin[:, mine_cols(1)]
    send_z(START, 1, 4)
    kvo[2, :, :HD] = kin[:, their_cols(2)]
    kvo[2, :, HD:] = vin[:, their_cols(2)]
    send_swap(START, 2)
    arrived(slot(1, 7), fr.at[1, 7])
    send_z(START, 1, 7)
    forward(START, 0, 0, 0)
    send_other_x(START, 0)
    forward(START, 0, 0, 1)
    forward(START, 0, 1, 0)
    q_copy.wait()
    qo[...] = qin[:, pl.ds(theirs, HALF)]
    qb[0] = qin[:, pl.ds(mine, HALF)]
    send_queries(START)
    send_other_x(START, 1)
    send_own_x(START, 1)
    arrived(gall.at[2], gr.at[1])
    send_gathered(START, 2)
    send_gathered(START, 1)
    forward(START, 0, 1, 1)
    pass_on(START, 0)
    arrived(slot(2, 7), fr.at[2, 7])
    send_z(START, 2, 7)
    forward(START, 1, 0, 0)
    for copy in w_copies:
        copy.wait()
    arrived(gall.at[1], gr.at[0])
    arrived(gall.at[3], gr.at[2])
    dop[...] = attn_grad(wo)
    send_attn_grad(START)
    dob[0] = attn_grad(wm)
    kv[2, pl.ds(4 * T, T), :HD] = kin[:, mine_cols(2)]
    kv[2, pl.ds(4 * T, T), HD:] = vin[:, mine_cols(2)]
    send_z(START, 2, 4)
    forward(START, 1, 1, 1)
    send_other_x(START, 2)
    send_own_x(START, 2)
    pass_on(START, 1)
    forward(START, 1, 0, 1)
    arrived(qb.at[1], qr.at[0])
    attend(0)
    forward(START, 1, 1, 0)
    arrived(dob.at[1], qr.at[1])
    differentiate(0, 0)
    differentiate(0, 1)
    forward(START, 2, 1, 1)
    forward(START, 2, 1, 0)
    forward(START, 2, 0, 0)
    attend(1)
    forward(START, 2, 0, 1)
    pass_back(START, 0)
    pass_on(START, 2)
    differentiate(1, 0)
    differentiate(1, 1)
    reduce_x(0, None)
    attend(2)
    pass_back(START, 1)
    differentiate(2, 0)
    differentiate(2, 1)
    reduce_x(1, None)
    for h in range(NH):
        arrived(attr.at[:, cols(h)], atr.at[h])
    ms[0] = project(3).astype(BF)
    ms[1] = project(1).astype(BF)
    remote(START, ms, mr, mss.at[0], msr.at[0], sibling)
    pass_back(START, 2)
    crossing_sum = project(2)
    arrived(mr, msr.at[0])
    ms2[...] = (crossing_sum + mr[0].astype(F32)).astype(BF)
    remote(START, ms2, mr2, mss.at[1], msr.at[1], across)
    kept = project(0) + mr[1].astype(F32)
    reduce_x(2, None)
    reduce_z(0, None)
    reduce_z(1, None)
    reduce_z(2, None)
    arrived(mr2, msr.at[1])
    res[0] = (kept + mr2[...].astype(F32)).astype(BF)
    finals = [local(res.at[0], mixed, lsem.at[5])]
    send_z(WAIT, 0, 4)
    send_z(WAIT, 0, 7)
    send_z(WAIT, 1, 4)
    send_z(WAIT, 1, 7)
    send_z(WAIT, 2, 4)
    send_z(WAIT, 2, 7)

    for h in range(NH):
        arrived(dql.at[:, cols(h)], dqr.at[h])
        res[1, :, their_cols(h)] = dql[:, cols(h)]
    finals.append(local(res.at[1], dq_out, lsem.at[6]))
    for h in range(NH):
        arrived(yr.at[h], byr.at[h])
        res[2, :, their_cols(h)] = yr[h, :, :HD]
        res[3, :, their_cols(h)] = yr[h, :, HD:]
    finals.append(local(res.at[2], dk_out, lsem.at[7]))
    finals.append(local(res.at[3], dv_out, lsem.at[8]))
    for n in range(3):
        send_gathered(WAIT, n)
    send_queries(WAIT)
    send_attn_grad(WAIT)
    remote(WAIT, ms, mr, mss.at[0], msr.at[0], sibling)
    remote(WAIT, ms2, mr2, mss.at[1], msr.at[1], across)
    for h in range(NH):
        for send in (
            send_swap, send_own_x, send_other_x, pass_on, pass_back, send_attended, send_query_grad, send_total,
        ):
            send(WAIT, h)
        for n in range(2):
            forward(WAIT, h, n, 0)
            forward(WAIT, h, n, 1)
            send_back(WAIT, h, n, None)
        send_reduced(WAIT, h, None)
    for copy in finals:
        copy.wait()

def hand_over(*refs):
    sources, results, held, ins, outs = refs[:4], refs[4:8], refs[8], refs[9], refs[10]
    arriving = [pltpu.make_async_copy(sources[n], held.at[n], ins.at[n]) for n in range(4)]
    leaving = [pltpu.make_async_copy(held.at[n], results[n], outs.at[n]) for n in range(4)]
    for copy in arriving:
        copy.start()
    for n in range(4):
        arriving[n].wait()
        leaving[n].start()
    for copy in leaving:
        copy.wait()


def on_device(queries, keys, values, w_out, out_grad, tile_valid):
    dma = pltpu.SemaphoreType.DMA
    any_space = pl.BlockSpec(memory_space=pl.ANY)
    block = jax.ShapeDtypeStruct(queries.shape, BF)
    results = pl.pallas_call(
        kernel,
        out_shape=(block, block, block, block),
        in_specs=[any_space] * 5 + [pl.BlockSpec(memory_space=pltpu.SMEM)],
        out_specs=(any_space, any_space, any_space, any_space),
        scratch_shapes=[
            pltpu.VMEM((NH, 12 * T, 2 * HD), BF),
            pltpu.VMEM((NH, T, 2 * HD), BF),
            pltpu.VMEM((T, HALF), BF),
            pltpu.VMEM((2, T, HALF), BF),
            pltpu.VMEM((2, T, HALF), BF),
            pltpu.VMEM((T, HALF), BF),
            pltpu.VMEM((4, T, FULL), BF),
            pltpu.VMEM((4 * FULL, HALF), BF),
            pltpu.VMEM((4 * FULL, HALF), BF),
            pltpu.VMEM((2, T, HALF), BF),
            pltpu.VMEM((T, HALF), BF),
            pltpu.VMEM((T, HALF), BF),
            pltpu.VMEM((T, HALF), BF),
            pltpu.VMEM((2, T, WIN), BF),
            pltpu.VMEM((2, T, HD), F32),
            pltpu.VMEM((2, 1, WIN), F32),
            pltpu.VMEM((NH, 2, SIDE, 2 * HD), BF),
            pltpu.VMEM((NH, 2, SIDE, 2 * HD), BF),
            pltpu.VMEM((NH, 2 * SIDE, 2 * HD), F32),
            pltpu.VMEM((NH, 2, 2 * T, 2 * HD), BF),
            pltpu.VMEM((NH, 2, 2 * T, 2 * HD), BF),
            pltpu.VMEM((NH, T, 2 * HD), BF),
            pltpu.VMEM((NH, T, 2 * HD), BF),
            pltpu.VMEM((2, T, FULL), BF),
            pltpu.VMEM((2, T, FULL), BF),
            pltpu.VMEM((T, FULL), BF),
            pltpu.VMEM((T, FULL), BF),
            pltpu.VMEM((4, T, FULL), BF),
            pltpu.VMEM((T, FULL), BF),
            pltpu.VMEM((T, FULL), BF),
            pltpu.VMEM((T, FULL), BF),
            pltpu.VMEM((NH, T, 2 * HD), BF),
            pltpu.VMEM((NH, T, 2 * HD), BF),
            pltpu.VMEM((NH, T, 2 * HD), BF),
            dma((9,)),
            dma((2,)),
            dma((NH, 14)),
            dma((NH, 12)),
            dma((NH, 2, 2, 3)),
            dma((NH, 2, 2, 3)),
            dma((NH, 2, 2)),
            dma((NH, 2, 2)),
            dma((NH,)),
            dma((NH,)),
            dma((3,)),
            dma((3,)),
            dma((2,)),
            dma((2,)),
            dma((NH,)),
            dma((NH,)),
            dma((NH,)),
            dma((NH,)),
            dma((2,)),
            dma((2,)),
            dma((NH, 4)),
            dma((NH, 2)),
            dma((NH, 2, 2)),
            dma((NH, 2)),
        ],
        compiler_params=pltpu.CompilerParams(
            collective_id=0, has_side_effects=True, vmem_limit_bytes=56 * 1024 * 1024
        ),
    )(queries, keys, values, w_out, out_grad, tile_valid)
    return pl.pallas_call(
        hand_over,
        out_shape=(block, block, block, block),
        in_specs=[any_space] * 4,
        out_specs=(any_space, any_space, any_space, any_space),
        scratch_shapes=[pltpu.VMEM((4, *queries.shape), BF), dma((4,)), dma((4,))],
        compiler_params=pltpu.CompilerParams(vmem_limit_bytes=56 * 1024 * 1024),
    )(*results)


def solution(mesh):
    return jax.shard_map(
        on_device,
        mesh=mesh,
        in_specs=(
            P("tile", "head"),
            P("tile", "head"),
            P("tile", "head"),
            P(None, "head"),
            P("tile", "head"),
            P(),
        ),
        out_specs=(P("tile", "head"), P("tile", "head"), P("tile", "head"), P("tile", "head")),
        check_vma=False,
    )
```

```python
import jax
import jax.numpy as jnp
from jax import lax
from jax.experimental import pallas as pl
from jax.experimental.pallas import tpu as pltpu
from jax.sharding import PartitionSpec as P

HD = 128
GT = 4
GH = 16
T = 160
NH = 3
HALF = NH * HD
FULL = 2 * HALF
WIN = 9 * T
SIDE = 3 * T
LOG2E = 1.4426950408889634
DIRECT_OUT = (0,)
DIRECT_BACK = (2,)
MESH = pl.DeviceIdType.MESH
BF = jnp.bfloat16
F32 = jnp.float32


def nt(a, b):
    return lax.dot_general(a, b, (((1,), (1,)), ((), ())), preferred_element_type=F32)


def nn(a, b):
    return lax.dot_general(a, b, (((1,), (0,)), ((), ())), preferred_element_type=F32)


def tn(a, b):
    return lax.dot_general(a, b, (((0,), (0,)), ((), ())), preferred_element_type=F32)


def kernel(
    q_in, k_in, v_in, w_in, g_in, valid,
    mixed, dq_out, dk_out, dv_out,
    kv, kvo, qo, qb, dob, dop, gall, wm, wo, att, attr, dqb, pb, rb_sum, bias,
    xs, rx, acc, zs, rz, ys, ms, mr, ms2, mr2, mo, rb, rb2, rc,
    lsem, hsem, fs, fr, bxs, bxr, bzs, bzr, bys, byr, gs, gr, qs, qr, dqs, dqr, ats, atr, mss, msr, rls, rlr, bcs, bcr,
):
    i = lax.axis_index("tile")
    j = lax.axis_index("head")
    t = i // GH
    g = i % GH
    p = g % 2
    u = g // 2
    d = 2 * p - 1
    e = (u == 3).astype(jnp.int32) - (u == 4).astype(jnp.int32)
    partner = (i + 1 - 2 * p, j)
    near = (t * GH + (g + 2 * d + GH) % GH, j)
    far = (t * GH + (g - 2 * d + GH) % GH, j)
    up = (((t + 1) % GT) * GH + g, j)
    down = (((t + GT - 1) % GT) * GH + g, j)
    eight_off = (t * GH + (g + GH // 2) % GH, j)
    six_off = (t * GH + (g + 6 + 4 * (u == 7).astype(jnp.int32)) % GH, j)
    relay = (t * GH + (g + GH - 6 * e) % GH, j)
    relay_to = eight_off
    back = (((t - e + GT) % GT) * GH + (g + 2 * e), j)
    j1 = j + 1 - 2 * (j % 2)
    j2 = (j + 2) % 4
    j3 = (j1 + 2) % 4
    sibling = (i, j1)
    across = (i, j2)
    has_up = t < GT - 1
    has_down = t > 0
    has_near = (u + d >= 0) & (u + d < GH // 2)
    has_far = (u - d >= 0) & (u - d < GH // 2)
    near_cross = e == d
    far_cross = e == -d
    is_cross = e != 0
    is_relay = (u == 0) | (u == 7)
    has_back = (t - e >= 0) & (t - e < GT)
    has_ahead = (t + e >= 0) & (t + e < GT)
    mine = pl.multiple_of(p * HALF, 128)
    theirs = pl.multiple_of((1 - p) * HALF, 128)
    scale = HD ** (-0.5)

    @pl.when(jnp.logical_not(has_down))
    def _():
        for s in (0, 3, 6, 9):
            kv[:, pl.ds(s * T, T), :] = jnp.zeros((NH, T, 2 * HD), BF)
        rz[:, 1] = jnp.zeros((NH, 2 * T, 2 * HD), BF)

    @pl.when(jnp.logical_not(has_up))
    def _():
        for s in (2, 5, 8, 11):
            kv[:, pl.ds(s * T, T), :] = jnp.zeros((NH, T, 2 * HD), BF)
        rz[:, 0] = jnp.zeros((NH, 2 * T, 2 * HD), BF)

    for n, side, there, crossing in ((0, 0, has_near, near_cross), (1, 3, has_far, far_cross)):
        @pl.when(jnp.logical_not(there))
        def _():
            kv[:, pl.ds(side * SIDE, SIDE), :] = jnp.zeros((NH, SIDE, 2 * HD), BF)

        @pl.when(jnp.logical_not(there) | crossing)
        def _():
            rx[:, n] = jnp.zeros((NH, SIDE, 2 * HD), BF)

    barrier = pltpu.get_barrier_semaphore()
    greeted = 0
    for peer, cond in (
        (partner, None), (sibling, None), (across, None), (near, has_near), (far, has_far), (up, has_up),
        (down, has_down), (eight_off, is_cross | is_relay), (six_off, is_relay),
        (relay, is_cross), (back, is_cross & has_back),
    ):
        if cond is None:
            pl.semaphore_signal(barrier, inc=1, device_id=peer, device_id_type=MESH)
            greeted += 1
        else:
            @pl.when(cond)
            def _():
                pl.semaphore_signal(barrier, inc=1, device_id=peer, device_id_type=MESH)
            greeted += cond.astype(jnp.int32)

    START, WAIT = 0, 1

    def when(cond, action):
        if cond is None:
            action()
        else:
            @pl.when(cond)
            def _():
                action()

    def remote(act, src, dst, send, recv, device, cond=None):
        copy = pltpu.make_async_remote_copy(
            src_ref=src, dst_ref=dst, send_sem=send, recv_sem=recv, device_id=device, device_id_type=MESH
        )
        when(cond, copy.start if act == START else copy.wait_send)

    def arrived(dst, recv, cond=None):
        copy = pltpu.make_async_remote_copy(
            src_ref=dst, dst_ref=dst, send_sem=lsem.at[0], recv_sem=recv, device_id=partner, device_id_type=MESH
        )
        when(cond, copy.wait_recv)

    def slot(h, s):
        return kv.at[h, pl.ds(s * T, T), :]

    def cols(h):
        return pl.ds(pl.multiple_of(h * HD, HD), HD)

    def mine_cols(h):
        return pl.ds(pl.multiple_of(mine + h * HD, HD), HD)

    def their_cols(h):
        return pl.ds(pl.multiple_of(theirs + h * HD, HD), HD)

    def local(src, dst, sem):
        copy = pltpu.make_async_copy(src, dst, sem)
        copy.start()
        return copy

    staged = [
        [
            local(k_in.at[:, their_cols(h)], kvo.at[h, :, pl.ds(0, HD)], hsem.at[h, 0]),
            local(v_in.at[:, their_cols(h)], kvo.at[h, :, pl.ds(HD, HD)], hsem.at[h, 1]),
        ]
        for h in range(NH)
    ]
    kept_tiles = [
        [
            local(k_in.at[:, mine_cols(h)], slot(h, 4).at[:, pl.ds(0, HD)], hsem.at[h, 2]),
            local(v_in.at[:, mine_cols(h)], slot(h, 4).at[:, pl.ds(HD, HD)], hsem.at[h, 3]),
        ]
        for h in range(NH)
    ]
    g_copy = local(g_in, gall.at[0], lsem.at[0])
    q_copy = local(q_in.at[:, pl.ds(mine, HALF)], qb.at[0], lsem.at[1])
    qo_copy = local(q_in.at[:, pl.ds(theirs, HALF)], qo, lsem.at[2])
    w_copies = [
        local(w_in.at[:, pl.ds(theirs, HALF)], wo, lsem.at[3]),
        local(w_in.at[:, pl.ds(mine, HALF)], wm, lsem.at[4]),
    ]

    lanes = lax.broadcasted_iota(jnp.int32, (1, WIN), 1)
    ones = jnp.ones((WIN, HD), BF)
    for a in range(2):
        row = jnp.zeros((1, WIN), F32)
        for n in range(9):
            g_slot, t_slot = a + n // 3, n % 3
            t_abs = t + t_slot - 1
            g_abs = g + (g_slot - 1) * (1 - 2 * p)
            if t_slot == 1 and g_slot == a + 1:
                value = jnp.float32(0.0)
            else:
                flag = valid[((t_abs + GT) % GT) * GH + (g_abs + GH) % GH]
                inside = (t_abs >= 0) & (t_abs < GT) & (g_abs >= 0) & (g_abs < GH)
                value = jnp.where(inside & (flag > 0), 0.0, -jnp.inf).astype(F32)
            row = jnp.where((lanes >= n * T) & (lanes < (n + 1) * T), value, row)
        bias[a] = row

    pl.semaphore_wait(barrier, greeted)

    def send_side(act, h, s, target, n, device, there, crossing):
        tile = slot(h, s)
        direct = there if h in DIRECT_OUT else there & jnp.logical_not(crossing)
        remote(act, tile, slot(h, target), fs.at[h, n], fr.at[h, target], device, direct)
        if h not in DIRECT_OUT:
            remote(act, tile, rb.at[h], rls.at[h, 0], rlr.at[h, 0], relay, crossing)
        remote(
            act, tile, slot(h, target + e), fs.at[h, n + 1], fr.at[h, target + e], back, crossing & has_back
        )

    def send_swap(act, h):
        remote(act, kvo.at[h], slot(h, 7), fs.at[h, 12], fr.at[h, 7], partner)

    def send_z(act, h, s):
        remote(act, slot(h, s), slot(h, s - 1), fs.at[h, 0 if s == 4 else 2], fr.at[h, s - 1], up, has_up)
        remote(act, slot(h, s), slot(h, s + 1), fs.at[h, 1 if s == 4 else 3], fr.at[h, s + 1], down, has_down)

    def send_own_x(act, h):
        send_side(act, h, 4, 10, 4, near, has_near, near_cross)

    def send_other_x(act, h):
        send_side(act, h, 7, 1, 6, far, has_far, far_cross)

    def pass_on(act, h):
        if h in DIRECT_OUT:
            return
        if act == START:
            arrived(rb.at[h], rlr.at[h, 0], is_relay)
        target = jnp.where((u == 0) == (p == 1), 10, 1)
        remote(act, rb.at[h], slot(h, target), rls.at[h, 1], fr.at[h, target], relay_to, is_relay)

    def forward(act, h, n, k):
        target, device, there, crossing = ((9, near, has_near, near_cross), (0, far, has_far, far_cross))[n]
        exists, way = ((has_down, 1), (has_up, -1))[k]
        source = slot(h, 3 + 3 * n + 2 * k)
        if act == START:
            arrived(source, fr.at[h, 3 + 3 * n + 2 * k], exists)
        remote(
            act, source, slot(h, target + 2 * k), fs.at[h, 8 + 2 * n + k], fr.at[h, target + 2 * k], device,
            exists & there & (jnp.logical_not(crossing) | (e == way)),
        )

    def send_back(act, h, n):
        device, there, crossing = ((far, has_far, far_cross), (near, has_near, near_cross))[n]
        remote(
            act, xs.at[h, n], rx.at[h, n], bxs.at[h, n, 0], bxr.at[h, n, 0], device,
            there & jnp.logical_not(crossing),
        )
        middle = xs.at[h, n, pl.ds(T, T)]
        if h in DIRECT_BACK:
            remote(act, middle, rx.at[h, n, pl.ds(T, T)], bxs.at[h, n, 2], bxr.at[h, n, 1], device, crossing)
        else:
            remote(act, middle, rb2.at[h], rls.at[h, 2], rlr.at[h, 1], relay, crossing)
        rows = pl.ds((1 + e) * T, T)
        remote(
            act, xs.at[h, n, rows], rx.at[h, n, rows], bxs.at[h, n, 1], bxr.at[h, n, 2], device, crossing & has_ahead
        )
        remote(
            act, xs.at[h, n, pl.ds((1 - e) * T, T)], rc.at[h], bcs.at[h, n], bcr.at[h], back, crossing & has_back
        )

    def pass_back(act, h):
        if h in DIRECT_BACK:
            return
        if act == START:
            arrived(rb2.at[h], rlr.at[h, 1], is_relay)
        n = jnp.where(u == 0, p, 1 - p)
        remote(act, rb2.at[h], rx.at[h, n, pl.ds(T, T)], rls.at[h, 3], bxr.at[h, n, 1], relay_to, is_relay)

    def send_attended(act, h):
        remote(act, att.at[1, :, cols(h)], attr.at[:, cols(h)], ats.at[h], atr.at[h], partner)

    def send_query_grad(act, h):
        remote(act, dqb.at[1, :, cols(h)], dq_out.at[:, mine_cols(h)], dqs.at[h], dqr.at[h], partner)
        copy = pltpu.make_async_copy(dqb.at[0, :, cols(h)], dq_out.at[:, mine_cols(h)], hsem.at[h, 2])
        if act == START:
            copy.start()
        else:
            copy.wait()

    def send_reduced(act, h):
        remote(act, zs.at[h, 0], rz.at[h, 0], bzs.at[h, 0], bzr.at[h, 0], down, has_down)
        remote(act, zs.at[h, 1], rz.at[h, 1], bzs.at[h, 1], bzr.at[h, 1], up, has_up)

    def send_total(act, h):
        for part, out in enumerate((dk_out, dv_out)):
            lane = pl.ds(part * HD, HD)
            remote(act, ys.at[h, 1, :, lane], out.at[:, mine_cols(h)], bys.at[h, part], byr.at[h, part], partner)
            copy = pltpu.make_async_copy(ys.at[h, 0, :, lane], out.at[:, mine_cols(h)], hsem.at[h, part])
            if act == START:
                copy.start()
            else:
                copy.wait()

    def attend(h):
        for s, there in ((9, has_far & has_down), (10, has_far), (11, has_far & has_up),
                         (0, has_near & has_down), (1, has_near), (2, has_near & has_up)):
            arrived(slot(h, s), fr.at[h, s], there)
        for a in range(2):
            window = pl.ds(a * SIDE, WIN)
            s = nt(qb[a, :, cols(h)], kv[h, window, pl.ds(0, HD)]) * (scale * LOG2E) + bias[a]
            x = jnp.exp2(s - jnp.max(s, axis=1, keepdims=True)).astype(BF)
            pb[a] = x
            total = nn(x, jnp.concatenate([kv[h, window, pl.ds(HD, HD)], ones], axis=1))
            inverse = 1.0 / total[:, HD:]
            rb_sum[a] = inverse
            att[a, :, cols(h)] = (total[:, :HD] * inverse).astype(BF)
        send_attended(START, h)

    def differentiate(h, a):
        q = qb[a, :, cols(h)]
        do = dob[a, :, cols(h)].astype(F32)
        window = pl.ds(a * SIDE, WIN)
        k = kv[h, window, pl.ds(0, HD)]
        weights = pb[a]
        inverse = rb_sum[a]
        row_dot = jnp.sum(do * att[a, :, cols(h)].astype(F32) * (inverse * scale), axis=1, keepdims=True)
        do_sum = (do * inverse).astype(BF)
        weight_grad = nt((do * (inverse * scale)).astype(BF), kv[h, window, pl.ds(HD, HD)])
        score_grad = weights * (weight_grad - row_dot).astype(BF)
        dqb[a, :, cols(h)] = nn(score_grad, k).astype(BF)
        for part, lhs, rhs in ((0, score_grad, q), (1, weights, do_sum)):
            grad = tn(lhs, rhs)
            lane = pl.ds(part * HD, HD)
            if a == 0:
                xs[h, 1, :, lane] = grad[:SIDE].astype(BF)
                acc[h, :, lane] = grad[SIDE:]
            else:
                acc[h, :, lane] += grad[:2 * SIDE]
                xs[h, 0, :, lane] = grad[2 * SIDE:].astype(BF)
        send_back(START, h, 1 - a)
        if a == 1:
            send_query_grad(START, h)

    def reduce_x(h):
        for n, there, crossing in ((0, has_near, near_cross), (1, has_far, far_cross)):
            arrived(rx.at[h, n], bxr.at[h, n, 0], there & jnp.logical_not(crossing))
            arrived(rx.at[h, n, pl.ds(T, T)], bxr.at[h, n, 1], crossing)
            arrived(rx.at[h, n, pl.ds((1 - e) * T, T)], bxr.at[h, n, 2], crossing & has_back)
        for n in range(2):
            for part, row in ((0, 0), (1, 2 * T)):
                zs[h, part, pl.ds(n * T, T), :] = (
                    acc[h, pl.ds(n * SIDE + row, T), :] + rx[h, n, pl.ds(row, T), :].astype(F32)
                ).astype(BF)
            acc[h, pl.ds(n * SIDE + T, T), :] += rx[h, n, pl.ds(T, T), :].astype(F32)
        send_reduced(START, h)

    def reduce_z(h):
        arrived(rz.at[h, 0], bzr.at[h, 0], has_up)
        arrived(rz.at[h, 1], bzr.at[h, 1], has_down)
        arrived(rc.at[h], bcr.at[h], is_cross & has_back)
        for n, crossing in ((0, near_cross), (1, far_cross)):
            @pl.when(crossing & has_back)
            def _():
                acc[h, pl.ds(n * SIDE + T, T), :] += rc[h].astype(F32)

        for n in range(2):
            rows = pl.ds(n * T, T)
            ys[h, n] = (
                acc[h, pl.ds(n * SIDE + T, T), :] + rz[h, 0, rows, :].astype(F32) + rz[h, 1, rows, :].astype(F32)
            ).astype(BF)
        send_total(START, h)

    blocks = (j, j1, j2, j3)
    rows = [pl.ds(pl.multiple_of(block * FULL, FULL), FULL) for block in blocks]

    def attn_grad(weights_ref):
        total = nn(gall[0], weights_ref[rows[0], :])
        for n in range(1, 4):
            total = total + nn(gall[n], weights_ref[rows[n], :])
        return total.astype(BF)

    blocks = (j, j1, j2, j3)
    rows = [pl.ds(pl.multiple_of(block * FULL, FULL), FULL) for block in blocks]

    def send_gathered(act, n):
        source, target, device, k = ((0, 2, across, 1), (0, 1, sibling, 0), (2, 3, sibling, 2))[n]
        remote(act, gall.at[source], gall.at[target], gs.at[k], gr.at[k], device)

    def send_queries(act):
        remote(act, qo, qb.at[1], qs.at[0], qr.at[0], partner)

    def attn_grad(weights_ref):
        total = nn(gall[0], weights_ref[rows[0], :])
        for k in range(1, 4):
            total = total + nn(gall[k], weights_ref[rows[k], :])
        return total.astype(BF)

    def send_attn_grad(act):
        remote(act, dop, dob.at[1], qs.at[1], qr.at[1], partner)

    def project(n):
        return nt(att[0], wm[rows[n], :]) + nt(attr[...], wo[rows[n], :])

    for copy in staged[0]:
        copy.wait()
    send_swap(START, 0)
    for copy in kept_tiles[0]:
        copy.wait()
    send_z(START, 0, 4)
    send_own_x(START, 0)
    for copy in staged[1]:
        copy.wait()
    send_swap(START, 1)
    arrived(slot(0, 7), fr.at[0, 7])
    send_z(START, 0, 7)
    g_copy.wait()
    send_gathered(START, 0)
    forward(START, 0, 0, 0)
    send_other_x(START, 0)
    for copy in kept_tiles[1]:
        copy.wait()
    send_z(START, 1, 4)
    arrived(slot(1, 7), fr.at[1, 7])
    send_z(START, 1, 7)
    forward(START, 0, 0, 1)
    send_other_x(START, 1)
    qo_copy.wait()
    send_queries(START)
    forward(START, 0, 1, 1)
    arrived(gall.at[2], gr.at[1])
    send_gathered(START, 2)
    for copy in staged[2]:
        copy.wait()
    send_swap(START, 2)
    forward(START, 0, 1, 0)
    send_own_x(START, 1)
    send_gathered(START, 1)
    for copy in w_copies:
        copy.wait()
    arrived(gall.at[1], gr.at[0])
    arrived(gall.at[3], gr.at[2])
    dop[...] = attn_grad(wo)
    send_attn_grad(START)
    for copy in kept_tiles[2]:
        copy.wait()
    send_z(START, 2, 4)
    dob[0] = attn_grad(wm)
    forward(START, 1, 1, 0)
    forward(START, 1, 0, 0)
    forward(START, 1, 0, 1)
    send_own_x(START, 2)
    arrived(slot(2, 7), fr.at[2, 7])
    send_z(START, 2, 7)
    q_copy.wait()
    arrived(qb.at[1], qr.at[0])
    attend(0)
    forward(START, 1, 1, 1)
    pass_on(START, 1)
    send_other_x(START, 2)
    arrived(dob.at[1], qr.at[1])
    differentiate(0, 0)
    differentiate(0, 1)
    forward(START, 2, 1, 0)
    attend(1)
    forward(START, 2, 0, 1)
    pass_back(START, 2)
    pass_back(START, 0)
    pass_on(START, 0)
    forward(START, 2, 1, 1)
    forward(START, 2, 0, 0)
    pass_on(START, 2)
    differentiate(1, 0)
    differentiate(1, 1)
    reduce_x(0)
    pass_back(START, 1)
    attend(2)
    differentiate(2, 0)
    differentiate(2, 1)
    for h in range(NH):
        arrived(attr.at[:, cols(h)], atr.at[h])
    ms[0] = project(3).astype(BF)
    ms[1] = project(1).astype(BF)
    remote(START, ms, mr, mss.at[0], msr.at[0], sibling)
    reduce_x(1)
    reduce_z(0)
    crossing_sum = project(2)
    arrived(mr, msr.at[0])
    ms2[...] = (crossing_sum + mr[0].astype(F32)).astype(BF)
    remote(START, ms2, mr2, mss.at[1], msr.at[1], across)
    kept = project(0) + mr[1].astype(F32)
    reduce_x(2)
    reduce_z(1)
    reduce_z(2)
    arrived(mr2, msr.at[1])
    mo[...] = (kept + mr2[...].astype(F32)).astype(BF)
    mixed_copy = local(mo, mixed, lsem.at[5])
    send_z(WAIT, 0, 4)
    send_z(WAIT, 0, 7)
    send_z(WAIT, 1, 4)
    send_z(WAIT, 1, 7)
    send_z(WAIT, 2, 4)
    send_z(WAIT, 2, 7)

    for n in range(3):
        send_gathered(WAIT, n)
    send_queries(WAIT)
    send_attn_grad(WAIT)
    remote(WAIT, ms, mr, mss.at[0], msr.at[0], sibling)
    remote(WAIT, ms2, mr2, mss.at[1], msr.at[1], across)
    for h in range(NH):
        for send in (
            send_swap, send_own_x, send_other_x, pass_on, pass_back, send_attended, send_query_grad, send_reduced,
            send_total,
        ):
            send(WAIT, h)
        for n in range(2):
            forward(WAIT, h, n, 0)
            forward(WAIT, h, n, 1)
            send_back(WAIT, h, n)
        arrived(dq_out.at[:, their_cols(h)], dqr.at[h])
        arrived(dk_out.at[:, their_cols(h)], byr.at[h, 0])
        arrived(dv_out.at[:, their_cols(h)], byr.at[h, 1])
    mixed_copy.wait()

def hand_over(*refs):
    sources, results, held, ins, outs = refs[:4], refs[4:8], refs[8], refs[9], refs[10]
    arriving = [pltpu.make_async_copy(sources[n], held.at[n], ins.at[n]) for n in range(4)]
    leaving = [pltpu.make_async_copy(held.at[n], results[n], outs.at[n]) for n in range(4)]
    for copy in arriving:
        copy.start()
    for n in range(4):
        arriving[n].wait()
        leaving[n].start()
    for copy in leaving:
        copy.wait()


def on_device(queries, keys, values, w_out, out_grad, tile_valid):
    dma = pltpu.SemaphoreType.DMA
    any_space = pl.BlockSpec(memory_space=pl.ANY)
    block = jax.ShapeDtypeStruct(queries.shape, BF)
    results = pl.pallas_call(
        kernel,
        out_shape=(block, block, block, block),
        in_specs=[any_space] * 5 + [pl.BlockSpec(memory_space=pltpu.SMEM)],
        out_specs=(any_space, any_space, any_space, any_space),
        scratch_shapes=[
            pltpu.VMEM((NH, 12 * T, 2 * HD), BF),
            pltpu.VMEM((NH, T, 2 * HD), BF),
            pltpu.VMEM((T, HALF), BF),
            pltpu.VMEM((2, T, HALF), BF),
            pltpu.VMEM((2, T, HALF), BF),
            pltpu.VMEM((T, HALF), BF),
            pltpu.VMEM((4, T, FULL), BF),
            pltpu.VMEM((4 * FULL, HALF), BF),
            pltpu.VMEM((4 * FULL, HALF), BF),
            pltpu.VMEM((2, T, HALF), BF),
            pltpu.VMEM((T, HALF), BF),
            pltpu.VMEM((2, T, HALF), BF),
            pltpu.VMEM((2, T, WIN), BF),
            pltpu.VMEM((2, T, HD), F32),
            pltpu.VMEM((2, 1, WIN), F32),
            pltpu.VMEM((NH, 2, SIDE, 2 * HD), BF),
            pltpu.VMEM((NH, 2, SIDE, 2 * HD), BF),
            pltpu.VMEM((NH, 2 * SIDE, 2 * HD), F32),
            pltpu.VMEM((NH, 2, 2 * T, 2 * HD), BF),
            pltpu.VMEM((NH, 2, 2 * T, 2 * HD), BF),
            pltpu.VMEM((NH, 2, T, 2 * HD), BF),
            pltpu.VMEM((2, T, FULL), BF),
            pltpu.VMEM((2, T, FULL), BF),
            pltpu.VMEM((T, FULL), BF),
            pltpu.VMEM((T, FULL), BF),
            pltpu.VMEM((T, FULL), BF),
            pltpu.VMEM((NH, T, 2 * HD), BF),
            pltpu.VMEM((NH, T, 2 * HD), BF),
            pltpu.VMEM((NH, T, 2 * HD), BF),
            dma((6,)),
            dma((NH, 4)),
            dma((NH, 14)),
            dma((NH, 12)),
            dma((NH, 2, 3)),
            dma((NH, 2, 3)),
            dma((NH, 2)),
            dma((NH, 2)),
            dma((NH, 2)),
            dma((NH, 2)),
            dma((3,)),
            dma((3,)),
            dma((2,)),
            dma((2,)),
            dma((NH,)),
            dma((NH,)),
            dma((NH,)),
            dma((NH,)),
            dma((2,)),
            dma((2,)),
            dma((NH, 4)),
            dma((NH, 2)),
            dma((NH, 2)),
            dma((NH,)),
        ],
        compiler_params=pltpu.CompilerParams(
            collective_id=0, has_side_effects=True, vmem_limit_bytes=56 * 1024 * 1024
        ),
    )(queries, keys, values, w_out, out_grad, tile_valid)
    return pl.pallas_call(
        hand_over,
        out_shape=(block, block, block, block),
        in_specs=[any_space] * 4,
        out_specs=(any_space, any_space, any_space, any_space),
        scratch_shapes=[pltpu.VMEM((4, *queries.shape), BF), dma((4,)), dma((4,))],
        compiler_params=pltpu.CompilerParams(vmem_limit_bytes=56 * 1024 * 1024),
    )(*results)


def solution(mesh):
    return jax.shard_map(
        on_device,
        mesh=mesh,
        in_specs=(
            P("tile", "head"),
            P("tile", "head"),
            P("tile", "head"),
            P(None, "head"),
            P("tile", "head"),
            P(),
        ),
        out_specs=(P("tile", "head"), P("tile", "head"), P("tile", "head"), P("tile", "head")),
        check_vma=False,
    )
```

```python
import jax
import jax.numpy as jnp
from jax import lax
from jax.experimental import pallas as pl
from jax.experimental.pallas import tpu as pltpu
from jax.sharding import PartitionSpec as P

HD = 128
GT = 4
GH = 16
T = 160
NH = 3
HALF = NH * HD
FULL = 2 * HALF
WIN = 9 * T
SIDE = 3 * T
LOG2E = 1.4426950408889634
DIRECT_OUT = (0,)
DIRECT_BACK = (2,)
MESH = pl.DeviceIdType.MESH
BF = jnp.bfloat16
F32 = jnp.float32


def nt(a, b):
    return lax.dot_general(a, b, (((1,), (1,)), ((), ())), preferred_element_type=F32)


def nn(a, b):
    return lax.dot_general(a, b, (((1,), (0,)), ((), ())), preferred_element_type=F32)


def tn(a, b):
    return lax.dot_general(a, b, (((0,), (0,)), ((), ())), preferred_element_type=F32)


def kernel(
    q_in, k_in, v_in, w_in, g_in, valid,
    mixed, dq_out, dk_out, dv_out,
    kv, kvo, qo, qb, dob, dop, gall, wm, wo, att, attr, dqb, pb, rb_sum, bias,
    xs, rx, acc, zs, rz, ys, ms, mr, ms2, mr2, mo, rb, rb2, rc,
    lsem, hsem, fs, fr, bxs, bxr, bzs, bzr, bys, byr, gs, gr, qs, qr, dqs, dqr, ats, atr, mss, msr, rls, rlr, bcs, bcr,
):
    i = lax.axis_index("tile")
    j = lax.axis_index("head")
    t = i // GH
    g = i % GH
    p = g % 2
    u = g // 2
    d = 2 * p - 1
    e = (u == 3).astype(jnp.int32) - (u == 4).astype(jnp.int32)
    partner = (i + 1 - 2 * p, j)
    near = (t * GH + (g + 2 * d + GH) % GH, j)
    far = (t * GH + (g - 2 * d + GH) % GH, j)
    up = (((t + 1) % GT) * GH + g, j)
    down = (((t + GT - 1) % GT) * GH + g, j)
    eight_off = (t * GH + (g + GH // 2) % GH, j)
    six_off = (t * GH + (g + 6 + 4 * (u == 7).astype(jnp.int32)) % GH, j)
    relay = (t * GH + (g + GH - 6 * e) % GH, j)
    relay_to = eight_off
    back = (((t - e + GT) % GT) * GH + (g + 2 * e), j)
    j1 = j + 1 - 2 * (j % 2)
    j2 = (j + 2) % 4
    j3 = (j1 + 2) % 4
    sibling = (i, j1)
    across = (i, j2)
    has_up = t < GT - 1
    has_down = t > 0
    has_near = (u + d >= 0) & (u + d < GH // 2)
    has_far = (u - d >= 0) & (u - d < GH // 2)
    near_cross = e == d
    far_cross = e == -d
    is_cross = e != 0
    is_relay = (u == 0) | (u == 7)
    has_back = (t - e >= 0) & (t - e < GT)
    has_ahead = (t + e >= 0) & (t + e < GT)
    mine = pl.multiple_of(p * HALF, 128)
    theirs = pl.multiple_of((1 - p) * HALF, 128)
    scale = HD ** (-0.5)

    @pl.when(jnp.logical_not(has_down))
    def _():
        for s in (0, 3, 6, 9):
            kv[:, pl.ds(s * T, T), :] = jnp.zeros((NH, T, 2 * HD), BF)
        rz[:, 1] = jnp.zeros((NH, 2 * T, 2 * HD), BF)

    @pl.when(jnp.logical_not(has_up))
    def _():
        for s in (2, 5, 8, 11):
            kv[:, pl.ds(s * T, T), :] = jnp.zeros((NH, T, 2 * HD), BF)
        rz[:, 0] = jnp.zeros((NH, 2 * T, 2 * HD), BF)

    for n, side, there, crossing in ((0, 0, has_near, near_cross), (1, 3, has_far, far_cross)):
        @pl.when(jnp.logical_not(there))
        def _():
            kv[:, pl.ds(side * SIDE, SIDE), :] = jnp.zeros((NH, SIDE, 2 * HD), BF)

        @pl.when(jnp.logical_not(there) | crossing)
        def _():
            rx[:, n] = jnp.zeros((NH, SIDE, 2 * HD), BF)

    barrier = pltpu.get_barrier_semaphore()
    greeted = 0
    for peer, cond in (
        (partner, None), (sibling, None), (across, None), (near, has_near), (far, has_far), (up, has_up),
        (down, has_down), (eight_off, is_cross | is_relay), (six_off, is_relay),
        (relay, is_cross), (back, is_cross & has_back),
    ):
        if cond is None:
            pl.semaphore_signal(barrier, inc=1, device_id=peer, device_id_type=MESH)
            greeted += 1
        else:
            @pl.when(cond)
            def _():
                pl.semaphore_signal(barrier, inc=1, device_id=peer, device_id_type=MESH)
            greeted += cond.astype(jnp.int32)

    START, WAIT = 0, 1

    def when(cond, action):
        if cond is None:
            action()
        else:
            @pl.when(cond)
            def _():
                action()

    def remote(act, src, dst, send, recv, device, cond=None):
        copy = pltpu.make_async_remote_copy(
            src_ref=src, dst_ref=dst, send_sem=send, recv_sem=recv, device_id=device, device_id_type=MESH
        )
        when(cond, copy.start if act == START else copy.wait_send)

    def arrived(dst, recv, cond=None):
        copy = pltpu.make_async_remote_copy(
            src_ref=dst, dst_ref=dst, send_sem=lsem.at[0], recv_sem=recv, device_id=partner, device_id_type=MESH
        )
        when(cond, copy.wait_recv)

    def slot(h, s):
        return kv.at[h, pl.ds(s * T, T), :]

    def cols(h):
        return pl.ds(pl.multiple_of(h * HD, HD), HD)

    def mine_cols(h):
        return pl.ds(pl.multiple_of(mine + h * HD, HD), HD)

    def their_cols(h):
        return pl.ds(pl.multiple_of(theirs + h * HD, HD), HD)

    def local(src, dst, sem):
        copy = pltpu.make_async_copy(src, dst, sem)
        copy.start()
        return copy

    staged = [
        [
            local(k_in.at[:, their_cols(h)], kvo.at[h, :, pl.ds(0, HD)], hsem.at[h, 0]),
            local(v_in.at[:, their_cols(h)], kvo.at[h, :, pl.ds(HD, HD)], hsem.at[h, 1]),
        ]
        for h in range(NH)
    ]
    kept_tiles = [
        [
            local(k_in.at[:, mine_cols(h)], slot(h, 4).at[:, pl.ds(0, HD)], hsem.at[h, 2]),
            local(v_in.at[:, mine_cols(h)], slot(h, 4).at[:, pl.ds(HD, HD)], hsem.at[h, 3]),
        ]
        for h in range(NH)
    ]
    g_copy = local(g_in, gall.at[0], lsem.at[0])
    q_copy = local(q_in.at[:, pl.ds(mine, HALF)], qb.at[0], lsem.at[1])
    qo_copy = local(q_in.at[:, pl.ds(theirs, HALF)], qo, lsem.at[2])
    w_copies = [
        local(w_in.at[:, pl.ds(theirs, HALF)], wo, lsem.at[3]),
        local(w_in.at[:, pl.ds(mine, HALF)], wm, lsem.at[4]),
    ]

    lanes = lax.broadcasted_iota(jnp.int32, (1, WIN), 1)
    ones = jnp.ones((WIN, HD), BF)
    for a in range(2):
        row = jnp.zeros((1, WIN), F32)
        for n in range(9):
            g_slot, t_slot = a + n // 3, n % 3
            t_abs = t + t_slot - 1
            g_abs = g + (g_slot - 1) * (1 - 2 * p)
            if t_slot == 1 and g_slot == a + 1:
                value = jnp.float32(0.0)
            else:
                flag = valid[((t_abs + GT) % GT) * GH + (g_abs + GH) % GH]
                inside = (t_abs >= 0) & (t_abs < GT) & (g_abs >= 0) & (g_abs < GH)
                value = jnp.where(inside & (flag > 0), 0.0, -jnp.inf).astype(F32)
            row = jnp.where((lanes >= n * T) & (lanes < (n + 1) * T), value, row)
        bias[a] = row

    pl.semaphore_wait(barrier, greeted)

    def send_side(act, h, s, target, n, device, there, crossing):
        tile = slot(h, s)
        direct = there if h in DIRECT_OUT else there & jnp.logical_not(crossing)
        remote(act, tile, slot(h, target), fs.at[h, n], fr.at[h, target], device, direct)
        if h not in DIRECT_OUT:
            remote(act, tile, rb.at[h], rls.at[h, 0], rlr.at[h, 0], relay, crossing)
        remote(
            act, tile, slot(h, target + e), fs.at[h, n + 1], fr.at[h, target + e], back, crossing & has_back
        )

    def send_swap(act, h):
        remote(act, kvo.at[h], slot(h, 7), fs.at[h, 12], fr.at[h, 7], partner)

    def send_z(act, h, s):
        remote(act, slot(h, s), slot(h, s - 1), fs.at[h, 0 if s == 4 else 2], fr.at[h, s - 1], up, has_up)
        remote(act, slot(h, s), slot(h, s + 1), fs.at[h, 1 if s == 4 else 3], fr.at[h, s + 1], down, has_down)

    def send_own_x(act, h):
        send_side(act, h, 4, 10, 4, near, has_near, near_cross)

    def send_other_x(act, h):
        send_side(act, h, 7, 1, 6, far, has_far, far_cross)

    def pass_on(act, h):
        if h in DIRECT_OUT:
            return
        if act == START:
            arrived(rb.at[h], rlr.at[h, 0], is_relay)
        target = jnp.where((u == 0) == (p == 1), 10, 1)
        remote(act, rb.at[h], slot(h, target), rls.at[h, 1], fr.at[h, target], relay_to, is_relay)

    def forward(act, h, n, k):
        target, device, there, crossing = ((9, near, has_near, near_cross), (0, far, has_far, far_cross))[n]
        exists, way = ((has_down, 1), (has_up, -1))[k]
        source = slot(h, 3 + 3 * n + 2 * k)
        if act == START:
            arrived(source, fr.at[h, 3 + 3 * n + 2 * k], exists)
        remote(
            act, source, slot(h, target + 2 * k), fs.at[h, 8 + 2 * n + k], fr.at[h, target + 2 * k], device,
            exists & there & (jnp.logical_not(crossing) | (e == way)),
        )

    def send_back(act, h, n):
        device, there, crossing = ((far, has_far, far_cross), (near, has_near, near_cross))[n]
        remote(
            act, xs.at[h, n], rx.at[h, n], bxs.at[h, n, 0], bxr.at[h, n, 0], device,
            there & jnp.logical_not(crossing),
        )
        middle = xs.at[h, n, pl.ds(T, T)]
        if h in DIRECT_BACK:
            remote(act, middle, rx.at[h, n, pl.ds(T, T)], bxs.at[h, n, 2], bxr.at[h, n, 1], device, crossing)
        else:
            remote(act, middle, rb2.at[h], rls.at[h, 2], rlr.at[h, 1], relay, crossing)
        rows = pl.ds((1 + e) * T, T)
        remote(
            act, xs.at[h, n, rows], rx.at[h, n, rows], bxs.at[h, n, 1], bxr.at[h, n, 2], device, crossing & has_ahead
        )
        remote(
            act, xs.at[h, n, pl.ds((1 - e) * T, T)], rc.at[h], bcs.at[h, n], bcr.at[h], back, crossing & has_back
        )

    def pass_back(act, h):
        if h in DIRECT_BACK:
            return
        if act == START:
            arrived(rb2.at[h], rlr.at[h, 1], is_relay)
        n = jnp.where(u == 0, p, 1 - p)
        remote(act, rb2.at[h], rx.at[h, n, pl.ds(T, T)], rls.at[h, 3], bxr.at[h, n, 1], relay_to, is_relay)

    def send_attended(act, h):
        remote(act, att.at[1, :, cols(h)], attr.at[:, cols(h)], ats.at[h], atr.at[h], partner)

    def send_query_grad(act, h):
        remote(act, dqb.at[1, :, cols(h)], dq_out.at[:, mine_cols(h)], dqs.at[h], dqr.at[h], partner)
        copy = pltpu.make_async_copy(dqb.at[0, :, cols(h)], dq_out.at[:, mine_cols(h)], hsem.at[h, 2])
        if act == START:
            copy.start()
        else:
            copy.wait()

    def send_reduced(act, h):
        remote(act, zs.at[h, 0], rz.at[h, 0], bzs.at[h, 0], bzr.at[h, 0], down, has_down)
        remote(act, zs.at[h, 1], rz.at[h, 1], bzs.at[h, 1], bzr.at[h, 1], up, has_up)

    def send_total(act, h):
        for part, out in enumerate((dk_out, dv_out)):
            lane = pl.ds(part * HD, HD)
            remote(act, ys.at[h, 1, :, lane], out.at[:, mine_cols(h)], bys.at[h, part], byr.at[h, part], partner)
            copy = pltpu.make_async_copy(ys.at[h, 0, :, lane], out.at[:, mine_cols(h)], hsem.at[h, part])
            if act == START:
                copy.start()
            else:
                copy.wait()

    def attend(h):
        for s, there in ((9, has_far & has_down), (10, has_far), (11, has_far & has_up),
                         (0, has_near & has_down), (1, has_near), (2, has_near & has_up)):
            arrived(slot(h, s), fr.at[h, s], there)
        for a in range(2):
            window = pl.ds(a * SIDE, WIN)
            s = nt(qb[a, :, cols(h)], kv[h, window, pl.ds(0, HD)]) * (scale * LOG2E) + bias[a]
            x = jnp.exp2(s - jnp.max(s, axis=1, keepdims=True)).astype(BF)
            pb[a] = x
            total = nn(x, jnp.concatenate([kv[h, window, pl.ds(HD, HD)], ones], axis=1))
            inverse = 1.0 / total[:, HD:]
            rb_sum[a] = inverse
            att[a, :, cols(h)] = (total[:, :HD] * inverse).astype(BF)
        send_attended(START, h)

    def differentiate(h):
        for a in range(2):
            q = qb[a, :, cols(h)]
            do = dob[a, :, cols(h)].astype(F32)
            window = pl.ds(a * SIDE, WIN)
            k = kv[h, window, pl.ds(0, HD)]
            weights = pb[a]
            scaled = rb_sum[a] * scale
            row_dot = jnp.sum(do * att[a, :, cols(h)].astype(F32) * scaled, axis=1, keepdims=True)
            do_sum = (do * rb_sum[a]).astype(BF)
            weight_grad = nt((do * scaled).astype(BF), kv[h, window, pl.ds(HD, HD)])
            score_grad = weights * (weight_grad - row_dot).astype(BF)
            dqb[a, :, cols(h)] = nn(score_grad, k).astype(BF)
            for part, lhs, rhs in ((0, score_grad, q), (1, weights, do_sum)):
                grad = tn(lhs, rhs)
                lane = pl.ds(part * HD, HD)
                if a == 0:
                    xs[h, 1, :, lane] = grad[:SIDE].astype(BF)
                    acc[h, :, lane] = grad[SIDE:]
                else:
                    acc[h, :, lane] += grad[:2 * SIDE]
                    xs[h, 0, :, lane] = grad[2 * SIDE:].astype(BF)
        send_back(START, h, 1)
        send_back(START, h, 0)
        send_query_grad(START, h)

    def reduce_x(h):
        for n, there, crossing in ((0, has_near, near_cross), (1, has_far, far_cross)):
            arrived(rx.at[h, n], bxr.at[h, n, 0], there & jnp.logical_not(crossing))
            arrived(rx.at[h, n, pl.ds(T, T)], bxr.at[h, n, 1], crossing)
            arrived(rx.at[h, n, pl.ds((1 - e) * T, T)], bxr.at[h, n, 2], crossing & has_back)
        for n in range(2):
            for part, row in ((0, 0), (1, 2 * T)):
                zs[h, part, pl.ds(n * T, T), :] = (
                    acc[h, pl.ds(n * SIDE + row, T), :] + rx[h, n, pl.ds(row, T), :].astype(F32)
                ).astype(BF)
            acc[h, pl.ds(n * SIDE + T, T), :] += rx[h, n, pl.ds(T, T), :].astype(F32)
        send_reduced(START, h)

    def reduce_z(h):
        arrived(rz.at[h, 0], bzr.at[h, 0], has_up)
        arrived(rz.at[h, 1], bzr.at[h, 1], has_down)
        arrived(rc.at[h], bcr.at[h], is_cross & has_back)
        for n, crossing in ((0, near_cross), (1, far_cross)):
            @pl.when(crossing & has_back)
            def _():
                acc[h, pl.ds(n * SIDE + T, T), :] += rc[h].astype(F32)

        for n in range(2):
            rows = pl.ds(n * T, T)
            ys[h, n] = (
                acc[h, pl.ds(n * SIDE + T, T), :] + rz[h, 0, rows, :].astype(F32) + rz[h, 1, rows, :].astype(F32)
            ).astype(BF)
        send_total(START, h)

    blocks = (j, j1, j2, j3)
    rows = [pl.ds(pl.multiple_of(block * FULL, FULL), FULL) for block in blocks]

    def attn_grad(weights_ref):
        total = nn(gall[0], weights_ref[rows[0], :])
        for n in range(1, 4):
            total = total + nn(gall[n], weights_ref[rows[n], :])
        return total.astype(BF)

    blocks = (j, j1, j2, j3)
    rows = [pl.ds(pl.multiple_of(block * FULL, FULL), FULL) for block in blocks]

    def send_gathered(act, n):
        source, target, device, k = ((0, 2, across, 1), (0, 1, sibling, 0), (2, 3, sibling, 2))[n]
        remote(act, gall.at[source], gall.at[target], gs.at[k], gr.at[k], device)

    def send_queries(act):
        remote(act, qo, qb.at[1], qs.at[0], qr.at[0], partner)

    def attn_grad(weights_ref):
        total = nn(gall[0], weights_ref[rows[0], :])
        for k in range(1, 4):
            total = total + nn(gall[k], weights_ref[rows[k], :])
        return total.astype(BF)

    def send_attn_grad(act):
        remote(act, dop, dob.at[1], qs.at[1], qr.at[1], partner)

    def project(n):
        return nt(att[0], wm[rows[n], :]) + nt(attr[...], wo[rows[n], :])

    for copy in staged[0]:
        copy.wait()
    send_swap(START, 0)
    for copy in kept_tiles[0]:
        copy.wait()
    send_z(START, 0, 4)
    for copy in staged[1]:
        copy.wait()
    send_swap(START, 1)
    arrived(slot(0, 7), fr.at[0, 7])
    send_z(START, 0, 7)
    g_copy.wait()
    send_gathered(START, 0)
    send_own_x(START, 0)
    for copy in kept_tiles[1]:
        copy.wait()
    send_z(START, 1, 4)
    for copy in staged[2]:
        copy.wait()
    send_swap(START, 2)
    arrived(slot(1, 7), fr.at[1, 7])
    send_z(START, 1, 7)
    forward(START, 0, 0, 0)
    send_other_x(START, 0)
    forward(START, 0, 0, 1)
    forward(START, 0, 1, 0)
    qo_copy.wait()
    send_queries(START)
    send_other_x(START, 1)
    send_own_x(START, 1)
    arrived(gall.at[2], gr.at[1])
    send_gathered(START, 2)
    send_gathered(START, 1)
    forward(START, 0, 1, 1)
    pass_on(START, 0)
    arrived(slot(2, 7), fr.at[2, 7])
    send_z(START, 2, 7)
    forward(START, 1, 0, 0)
    for copy in w_copies:
        copy.wait()
    arrived(gall.at[1], gr.at[0])
    arrived(gall.at[3], gr.at[2])
    dop[...] = attn_grad(wo)
    send_attn_grad(START)
    dob[0] = attn_grad(wm)
    for copy in kept_tiles[2]:
        copy.wait()
    send_z(START, 2, 4)
    forward(START, 1, 1, 1)
    send_other_x(START, 2)
    send_own_x(START, 2)
    pass_on(START, 1)
    forward(START, 1, 0, 1)
    q_copy.wait()
    arrived(qb.at[1], qr.at[0])
    attend(0)
    forward(START, 1, 1, 0)
    arrived(dob.at[1], qr.at[1])
    differentiate(0)
    forward(START, 2, 1, 1)
    forward(START, 2, 1, 0)
    forward(START, 2, 0, 0)
    attend(1)
    forward(START, 2, 0, 1)
    pass_back(START, 0)
    pass_on(START, 2)
    differentiate(1)
    reduce_x(0)
    attend(2)
    pass_back(START, 1)
    differentiate(2)
    reduce_x(1)
    for h in range(NH):
        arrived(attr.at[:, cols(h)], atr.at[h])
    ms[0] = project(3).astype(BF)
    ms[1] = project(1).astype(BF)
    remote(START, ms, mr, mss.at[0], msr.at[0], sibling)
    pass_back(START, 2)
    crossing_sum = project(2)
    arrived(mr, msr.at[0])
    ms2[...] = (crossing_sum + mr[0].astype(F32)).astype(BF)
    remote(START, ms2, mr2, mss.at[1], msr.at[1], across)
    kept = project(0) + mr[1].astype(F32)
    reduce_x(2)
    reduce_z(0)
    reduce_z(1)
    reduce_z(2)
    arrived(mr2, msr.at[1])
    mo[...] = (kept + mr2[...].astype(F32)).astype(BF)
    mixed_copy = local(mo, mixed, lsem.at[5])
    send_z(WAIT, 0, 4)
    send_z(WAIT, 0, 7)
    send_z(WAIT, 1, 4)
    send_z(WAIT, 1, 7)
    send_z(WAIT, 2, 4)
    send_z(WAIT, 2, 7)

    for n in range(3):
        send_gathered(WAIT, n)
    send_queries(WAIT)
    send_attn_grad(WAIT)
    remote(WAIT, ms, mr, mss.at[0], msr.at[0], sibling)
    remote(WAIT, ms2, mr2, mss.at[1], msr.at[1], across)
    for h in range(NH):
        for send in (
            send_swap, send_own_x, send_other_x, pass_on, pass_back, send_attended, send_query_grad, send_reduced,
            send_total,
        ):
            send(WAIT, h)
        for n in range(2):
            forward(WAIT, h, n, 0)
            forward(WAIT, h, n, 1)
            send_back(WAIT, h, n)
        arrived(dq_out.at[:, their_cols(h)], dqr.at[h])
        arrived(dk_out.at[:, their_cols(h)], byr.at[h, 0])
        arrived(dv_out.at[:, their_cols(h)], byr.at[h, 1])
    mixed_copy.wait()

def hand_over(*refs):
    sources, results, held, ins, outs = refs[:4], refs[4:8], refs[8], refs[9], refs[10]
    arriving = [pltpu.make_async_copy(sources[n], held.at[n], ins.at[n]) for n in range(4)]
    leaving = [pltpu.make_async_copy(held.at[n], results[n], outs.at[n]) for n in range(4)]
    for copy in arriving:
        copy.start()
    for n in range(4):
        arriving[n].wait()
        leaving[n].start()
    for copy in leaving:
        copy.wait()


def on_device(queries, keys, values, w_out, out_grad, tile_valid):
    dma = pltpu.SemaphoreType.DMA
    any_space = pl.BlockSpec(memory_space=pl.ANY)
    block = jax.ShapeDtypeStruct(queries.shape, BF)
    results = pl.pallas_call(
        kernel,
        out_shape=(block, block, block, block),
        in_specs=[any_space] * 5 + [pl.BlockSpec(memory_space=pltpu.SMEM)],
        out_specs=(any_space, any_space, any_space, any_space),
        scratch_shapes=[
            pltpu.VMEM((NH, 12 * T, 2 * HD), BF),
            pltpu.VMEM((NH, T, 2 * HD), BF),
            pltpu.VMEM((T, HALF), BF),
            pltpu.VMEM((2, T, HALF), BF),
            pltpu.VMEM((2, T, HALF), BF),
            pltpu.VMEM((T, HALF), BF),
            pltpu.VMEM((4, T, FULL), BF),
            pltpu.VMEM((4 * FULL, HALF), BF),
            pltpu.VMEM((4 * FULL, HALF), BF),
            pltpu.VMEM((2, T, HALF), BF),
            pltpu.VMEM((T, HALF), BF),
            pltpu.VMEM((2, T, HALF), BF),
            pltpu.VMEM((2, T, WIN), BF),
            pltpu.VMEM((2, T, HD), F32),
            pltpu.VMEM((2, 1, WIN), F32),
            pltpu.VMEM((NH, 2, SIDE, 2 * HD), BF),
            pltpu.VMEM((NH, 2, SIDE, 2 * HD), BF),
            pltpu.VMEM((NH, 2 * SIDE, 2 * HD), F32),
            pltpu.VMEM((NH, 2, 2 * T, 2 * HD), BF),
            pltpu.VMEM((NH, 2, 2 * T, 2 * HD), BF),
            pltpu.VMEM((NH, 2, T, 2 * HD), BF),
            pltpu.VMEM((2, T, FULL), BF),
            pltpu.VMEM((2, T, FULL), BF),
            pltpu.VMEM((T, FULL), BF),
            pltpu.VMEM((T, FULL), BF),
            pltpu.VMEM((T, FULL), BF),
            pltpu.VMEM((NH, T, 2 * HD), BF),
            pltpu.VMEM((NH, T, 2 * HD), BF),
            pltpu.VMEM((NH, T, 2 * HD), BF),
            dma((6,)),
            dma((NH, 4)),
            dma((NH, 14)),
            dma((NH, 12)),
            dma((NH, 2, 3)),
            dma((NH, 2, 3)),
            dma((NH, 2)),
            dma((NH, 2)),
            dma((NH, 2)),
            dma((NH, 2)),
            dma((3,)),
            dma((3,)),
            dma((2,)),
            dma((2,)),
            dma((NH,)),
            dma((NH,)),
            dma((NH,)),
            dma((NH,)),
            dma((2,)),
            dma((2,)),
            dma((NH, 4)),
            dma((NH, 2)),
            dma((NH, 2)),
            dma((NH,)),
        ],
        compiler_params=pltpu.CompilerParams(
            collective_id=0, has_side_effects=True, vmem_limit_bytes=56 * 1024 * 1024
        ),
    )(queries, keys, values, w_out, out_grad, tile_valid)
    return pl.pallas_call(
        hand_over,
        out_shape=(block, block, block, block),
        in_specs=[any_space] * 4,
        out_specs=(any_space, any_space, any_space, any_space),
        scratch_shapes=[pltpu.VMEM((4, *queries.shape), BF), dma((4,)), dma((4,))],
        compiler_params=pltpu.CompilerParams(vmem_limit_bytes=56 * 1024 * 1024),
    )(*results)


def solution(mesh):
    return jax.shard_map(
        on_device,
        mesh=mesh,
        in_specs=(
            P("tile", "head"),
            P("tile", "head"),
            P("tile", "head"),
            P(None, "head"),
            P("tile", "head"),
            P(),
        ),
        out_specs=(P("tile", "head"), P("tile", "head"), P("tile", "head"), P("tile", "head")),
        check_vma=False,
    )
```

```python
import jax
import jax.numpy as jnp
from jax import lax
from jax.experimental import pallas as pl
from jax.experimental.pallas import tpu as pltpu
from jax.sharding import PartitionSpec as P

HD = 128
GT = 4
GH = 16
T = 160
NH = 3
HALF = NH * HD
FULL = 2 * HALF
WIN = 9 * T
SIDE = 3 * T
LOG2E = 1.4426950408889634
DIRECT_OUT = (0,)
DIRECT_BACK = (2,)
MESH = pl.DeviceIdType.MESH
BF = jnp.bfloat16
F32 = jnp.float32


def nt(a, b):
    return lax.dot_general(a, b, (((1,), (1,)), ((), ())), preferred_element_type=F32)


def nn(a, b):
    return lax.dot_general(a, b, (((1,), (0,)), ((), ())), preferred_element_type=F32)


def tn(a, b):
    return lax.dot_general(a, b, (((0,), (0,)), ((), ())), preferred_element_type=F32)


def kernel(
    q_in, k_in, v_in, w_in, g_in, valid,
    mixed, dq_out, dk_out, dv_out,
    kv, kvo, qo, qb, dob, dop, gall, wm, wo, att, attr, dqb, pb, rb_sum, bias,
    xs, rx, acc, zs, rz, ys, ms, mr, ms2, mr2, mo, rb, rb2, rc,
    lsem, hsem, fs, fr, bxs, bxr, bzs, bzr, bys, byr, gs, gr, qs, qr, dqs, dqr, ats, atr, mss, msr, rls, rlr, bcs, bcr,
):
    i = lax.axis_index("tile")
    j = lax.axis_index("head")
    t = i // GH
    g = i % GH
    p = g % 2
    u = g // 2
    d = 2 * p - 1
    e = (u == 3).astype(jnp.int32) - (u == 4).astype(jnp.int32)
    partner = (i + 1 - 2 * p, j)
    near = (t * GH + (g + 2 * d + GH) % GH, j)
    far = (t * GH + (g - 2 * d + GH) % GH, j)
    up = (((t + 1) % GT) * GH + g, j)
    down = (((t + GT - 1) % GT) * GH + g, j)
    eight_off = (t * GH + (g + GH // 2) % GH, j)
    six_off = (t * GH + (g + 6 + 4 * (u == 7).astype(jnp.int32)) % GH, j)
    relay = (t * GH + (g + GH - 6 * e) % GH, j)
    relay_to = eight_off
    back = (((t - e + GT) % GT) * GH + (g + 2 * e), j)
    j1 = j + 1 - 2 * (j % 2)
    j2 = (j + 2) % 4
    j3 = (j1 + 2) % 4
    sibling = (i, j1)
    across = (i, j2)
    has_up = t < GT - 1
    has_down = t > 0
    has_near = (u + d >= 0) & (u + d < GH // 2)
    has_far = (u - d >= 0) & (u - d < GH // 2)
    near_cross = e == d
    far_cross = e == -d
    is_cross = e != 0
    is_relay = (u == 0) | (u == 7)
    has_back = (t - e >= 0) & (t - e < GT)
    has_ahead = (t + e >= 0) & (t + e < GT)
    mine = pl.multiple_of(p * HALF, 128)
    theirs = pl.multiple_of((1 - p) * HALF, 128)
    scale = HD ** (-0.5)

    spans = (
        (pl.ds(0, SIDE), has_up & has_down),
        (pl.ds(T, 2 * T), jnp.logical_not(has_down)),
        (pl.ds(0, 2 * T), jnp.logical_not(has_up)),
    )

    @pl.when(jnp.logical_not(has_down))
    def _():
        for s in (0, 3, 6, 9):
            kv[:, pl.ds(s * T, T), :] = jnp.zeros((NH, T, 2 * HD), BF)
        rz[:, 1] = jnp.zeros((NH, 2 * T, 2 * HD), BF)
        rx[:, :, pl.ds(0, T), :] = jnp.zeros((NH, 2, T, 2 * HD), BF)

    @pl.when(jnp.logical_not(has_up))
    def _():
        for s in (2, 5, 8, 11):
            kv[:, pl.ds(s * T, T), :] = jnp.zeros((NH, T, 2 * HD), BF)
        rz[:, 0] = jnp.zeros((NH, 2 * T, 2 * HD), BF)
        rx[:, :, pl.ds(2 * T, T), :] = jnp.zeros((NH, 2, T, 2 * HD), BF)

    for n, side, there, crossing in ((0, 0, has_near, near_cross), (1, 3, has_far, far_cross)):
        @pl.when(jnp.logical_not(there))
        def _():
            kv[:, pl.ds(side * SIDE, SIDE), :] = jnp.zeros((NH, SIDE, 2 * HD), BF)

        @pl.when(jnp.logical_not(there) | crossing)
        def _():
            rx[:, n] = jnp.zeros((NH, SIDE, 2 * HD), BF)

    barrier = pltpu.get_barrier_semaphore()
    greeted = 0
    for peer, cond in (
        (partner, None), (sibling, None), (across, None), (near, has_near), (far, has_far), (up, has_up),
        (down, has_down), (eight_off, is_cross | is_relay), (six_off, is_relay),
        (relay, is_cross), (back, is_cross & has_back),
    ):
        if cond is None:
            pl.semaphore_signal(barrier, inc=1, device_id=peer, device_id_type=MESH)
            greeted += 1
        else:
            @pl.when(cond)
            def _():
                pl.semaphore_signal(barrier, inc=1, device_id=peer, device_id_type=MESH)
            greeted += cond.astype(jnp.int32)

    START, WAIT = 0, 1

    def when(cond, action):
        if cond is None:
            action()
        else:
            @pl.when(cond)
            def _():
                action()

    def remote(act, src, dst, send, recv, device, cond=None):
        copy = pltpu.make_async_remote_copy(
            src_ref=src, dst_ref=dst, send_sem=send, recv_sem=recv, device_id=device, device_id_type=MESH
        )
        when(cond, copy.start if act == START else copy.wait_send)

    def arrived(dst, recv, cond=None):
        copy = pltpu.make_async_remote_copy(
            src_ref=dst, dst_ref=dst, send_sem=lsem.at[0], recv_sem=recv, device_id=partner, device_id_type=MESH
        )
        when(cond, copy.wait_recv)

    def slot(h, s):
        return kv.at[h, pl.ds(s * T, T), :]

    def cols(h):
        return pl.ds(pl.multiple_of(h * HD, HD), HD)

    def mine_cols(h):
        return pl.ds(pl.multiple_of(mine + h * HD, HD), HD)

    def their_cols(h):
        return pl.ds(pl.multiple_of(theirs + h * HD, HD), HD)

    def local(src, dst, sem):
        copy = pltpu.make_async_copy(src, dst, sem)
        copy.start()
        return copy

    staged = [
        [
            local(k_in.at[:, their_cols(h)], kvo.at[h, :, pl.ds(0, HD)], hsem.at[h, 0]),
            local(v_in.at[:, their_cols(h)], kvo.at[h, :, pl.ds(HD, HD)], hsem.at[h, 1]),
        ]
        for h in range(NH)
    ]
    kept_tiles = [
        [
            local(k_in.at[:, mine_cols(h)], slot(h, 4).at[:, pl.ds(0, HD)], hsem.at[h, 2]),
            local(v_in.at[:, mine_cols(h)], slot(h, 4).at[:, pl.ds(HD, HD)], hsem.at[h, 3]),
        ]
        for h in range(NH)
    ]
    g_copy = local(g_in, gall.at[0], lsem.at[0])
    q_copy = local(q_in.at[:, pl.ds(mine, HALF)], qb.at[0], lsem.at[1])
    qo_copy = local(q_in.at[:, pl.ds(theirs, HALF)], qo, lsem.at[2])
    w_copies = [
        local(w_in.at[:, pl.ds(theirs, HALF)], wo, lsem.at[3]),
        local(w_in.at[:, pl.ds(mine, HALF)], wm, lsem.at[4]),
    ]

    lanes = lax.broadcasted_iota(jnp.int32, (1, WIN), 1)
    ones = jnp.ones((WIN, HD), BF)
    for a in range(2):
        row = jnp.zeros((1, WIN), F32)
        for n in range(9):
            g_slot, t_slot = a + n // 3, n % 3
            t_abs = t + t_slot - 1
            g_abs = g + (g_slot - 1) * (1 - 2 * p)
            if t_slot == 1 and g_slot == a + 1:
                value = jnp.float32(0.0)
            else:
                flag = valid[((t_abs + GT) % GT) * GH + (g_abs + GH) % GH]
                inside = (t_abs >= 0) & (t_abs < GT) & (g_abs >= 0) & (g_abs < GH)
                value = jnp.where(inside & (flag > 0), 0.0, -jnp.inf).astype(F32)
            row = jnp.where((lanes >= n * T) & (lanes < (n + 1) * T), value, row)
        bias[a] = row

    pl.semaphore_wait(barrier, greeted)

    def send_side(act, h, s, target, n, device, there, crossing):
        tile = slot(h, s)
        direct = there if h in DIRECT_OUT else there & jnp.logical_not(crossing)
        remote(act, tile, slot(h, target), fs.at[h, n], fr.at[h, target], device, direct)
        if h not in DIRECT_OUT:
            remote(act, tile, rb.at[h], rls.at[h, 0], rlr.at[h, 0], relay, crossing)
        remote(
            act, tile, slot(h, target + e), fs.at[h, n + 1], fr.at[h, target + e], back, crossing & has_back
        )

    def send_swap(act, h):
        remote(act, kvo.at[h], slot(h, 7), fs.at[h, 12], fr.at[h, 7], partner)

    def send_z(act, h, s):
        remote(act, slot(h, s), slot(h, s - 1), fs.at[h, 0 if s == 4 else 2], fr.at[h, s - 1], up, has_up)
        remote(act, slot(h, s), slot(h, s + 1), fs.at[h, 1 if s == 4 else 3], fr.at[h, s + 1], down, has_down)

    def send_own_x(act, h):
        send_side(act, h, 4, 10, 4, near, has_near, near_cross)

    def send_other_x(act, h):
        send_side(act, h, 7, 1, 6, far, has_far, far_cross)

    def pass_on(act, h):
        if h in DIRECT_OUT:
            return
        if act == START:
            arrived(rb.at[h], rlr.at[h, 0], is_relay)
        target = jnp.where((u == 0) == (p == 1), 10, 1)
        remote(act, rb.at[h], slot(h, target), rls.at[h, 1], fr.at[h, target], relay_to, is_relay)

    def forward(act, h, n, k):
        target, device, there, crossing = ((9, near, has_near, near_cross), (0, far, has_far, far_cross))[n]
        exists, way = ((has_down, 1), (has_up, -1))[k]
        source = slot(h, 3 + 3 * n + 2 * k)
        if act == START:
            arrived(source, fr.at[h, 3 + 3 * n + 2 * k], exists)
        remote(
            act, source, slot(h, target + 2 * k), fs.at[h, 8 + 2 * n + k], fr.at[h, target + 2 * k], device,
            exists & there & (jnp.logical_not(crossing) | (e == way)),
        )

    def send_back(act, h, n):
        device, there, crossing = ((far, has_far, far_cross), (near, has_near, near_cross))[n]
        for rows, cond in spans:
            remote(
                act, xs.at[h, n, rows], rx.at[h, n, rows], bxs.at[h, n, 0], bxr.at[h, n, 0], device,
                there & jnp.logical_not(crossing) & cond,
            )
        middle = xs.at[h, n, pl.ds(T, T)]
        if h in DIRECT_BACK:
            remote(act, middle, rx.at[h, n, pl.ds(T, T)], bxs.at[h, n, 2], bxr.at[h, n, 1], device, crossing)
        else:
            remote(act, middle, rb2.at[h], rls.at[h, 2], rlr.at[h, 1], relay, crossing)
        rows = pl.ds((1 + e) * T, T)
        remote(
            act, xs.at[h, n, rows], rx.at[h, n, rows], bxs.at[h, n, 1], bxr.at[h, n, 2], device, crossing & has_ahead
        )
        remote(
            act, xs.at[h, n, pl.ds((1 - e) * T, T)], rc.at[h], bcs.at[h, n], bcr.at[h], back, crossing & has_back
        )

    def pass_back(act, h):
        if h in DIRECT_BACK:
            return
        if act == START:
            arrived(rb2.at[h], rlr.at[h, 1], is_relay)
        n = jnp.where(u == 0, p, 1 - p)
        remote(act, rb2.at[h], rx.at[h, n, pl.ds(T, T)], rls.at[h, 3], bxr.at[h, n, 1], relay_to, is_relay)

    def send_attended(act, h):
        remote(act, att.at[1, :, cols(h)], attr.at[:, cols(h)], ats.at[h], atr.at[h], partner)

    def send_query_grad(act, h):
        remote(act, dqb.at[1, :, cols(h)], dq_out.at[:, mine_cols(h)], dqs.at[h], dqr.at[h], partner)
        copy = pltpu.make_async_copy(dqb.at[0, :, cols(h)], dq_out.at[:, mine_cols(h)], hsem.at[h, 2])
        if act == START:
            copy.start()
        else:
            copy.wait()

    def send_reduced(act, h):
        remote(act, zs.at[h, 0], rz.at[h, 0], bzs.at[h, 0], bzr.at[h, 0], down, has_down)
        remote(act, zs.at[h, 1], rz.at[h, 1], bzs.at[h, 1], bzr.at[h, 1], up, has_up)

    def send_total(act, h):
        for part, out in enumerate((dk_out, dv_out)):
            lane = pl.ds(part * HD, HD)
            remote(act, ys.at[h, 1, :, lane], out.at[:, mine_cols(h)], bys.at[h, part], byr.at[h, part], partner)
            copy = pltpu.make_async_copy(ys.at[h, 0, :, lane], out.at[:, mine_cols(h)], hsem.at[h, part])
            if act == START:
                copy.start()
            else:
                copy.wait()

    def attend(h):
        for s, there in ((9, has_far & has_down), (10, has_far), (11, has_far & has_up),
                         (0, has_near & has_down), (1, has_near), (2, has_near & has_up)):
            arrived(slot(h, s), fr.at[h, s], there)
        for a in range(2):
            window = pl.ds(a * SIDE, WIN)
            s = nt(qb[a, :, cols(h)], kv[h, window, pl.ds(0, HD)]) * (scale * LOG2E) + bias[a]
            x = jnp.exp2(s - jnp.max(s, axis=1, keepdims=True)).astype(BF)
            pb[a] = x
            total = nn(x, jnp.concatenate([kv[h, window, pl.ds(HD, HD)], ones], axis=1))
            inverse = 1.0 / total[:, HD:]
            rb_sum[a] = inverse
            att[a, :, cols(h)] = (total[:, :HD] * inverse).astype(BF)
        send_attended(START, h)

    def differentiate(h, a):
        q = qb[a, :, cols(h)]
        do = dob[a, :, cols(h)].astype(F32)
        window = pl.ds(a * SIDE, WIN)
        k = kv[h, window, pl.ds(0, HD)]
        weights = pb[a]
        inverse = rb_sum[a]
        row_dot = jnp.sum(do * att[a, :, cols(h)].astype(F32) * (inverse * scale), axis=1, keepdims=True)
        do_sum = (do * inverse).astype(BF)
        weight_grad = nt((do * (inverse * scale)).astype(BF), kv[h, window, pl.ds(HD, HD)])
        score_grad = weights * (weight_grad - row_dot).astype(BF)
        dqb[a, :, cols(h)] = nn(score_grad, k).astype(BF)
        for part, lhs, rhs in ((0, score_grad, q), (1, weights, do_sum)):
            grad = tn(lhs, rhs)
            lane = pl.ds(part * HD, HD)
            if a == 0:
                xs[h, 1, :, lane] = grad[:SIDE].astype(BF)
                acc[h, :, lane] = grad[SIDE:]
            else:
                acc[h, :, lane] += grad[:2 * SIDE]
                xs[h, 0, :, lane] = grad[2 * SIDE:].astype(BF)
        send_back(START, h, 1 - a)
        if a == 1:
            send_query_grad(START, h)

    def reduce_x(h):
        for n, there, crossing in ((0, has_near, near_cross), (1, has_far, far_cross)):
            for rows, cond in spans:
                arrived(rx.at[h, n, rows], bxr.at[h, n, 0], there & jnp.logical_not(crossing) & cond)
            arrived(rx.at[h, n, pl.ds(T, T)], bxr.at[h, n, 1], crossing)
            arrived(rx.at[h, n, pl.ds((1 - e) * T, T)], bxr.at[h, n, 2], crossing & has_back)
        for n in range(2):
            for part, row in ((0, 0), (1, 2 * T)):
                zs[h, part, pl.ds(n * T, T), :] = (
                    acc[h, pl.ds(n * SIDE + row, T), :] + rx[h, n, pl.ds(row, T), :].astype(F32)
                ).astype(BF)
            acc[h, pl.ds(n * SIDE + T, T), :] += rx[h, n, pl.ds(T, T), :].astype(F32)
        send_reduced(START, h)

    def reduce_z(h):
        arrived(rz.at[h, 0], bzr.at[h, 0], has_up)
        arrived(rz.at[h, 1], bzr.at[h, 1], has_down)
        arrived(rc.at[h], bcr.at[h], is_cross & has_back)
        for n, crossing in ((0, near_cross), (1, far_cross)):
            @pl.when(crossing & has_back)
            def _():
                acc[h, pl.ds(n * SIDE + T, T), :] += rc[h].astype(F32)

        for n in range(2):
            rows = pl.ds(n * T, T)
            ys[h, n] = (
                acc[h, pl.ds(n * SIDE + T, T), :] + rz[h, 0, rows, :].astype(F32) + rz[h, 1, rows, :].astype(F32)
            ).astype(BF)
        send_total(START, h)

    blocks = (j, j1, j2, j3)
    rows = [pl.ds(pl.multiple_of(block * FULL, FULL), FULL) for block in blocks]

    def attn_grad(weights_ref):
        total = nn(gall[0], weights_ref[rows[0], :])
        for n in range(1, 4):
            total = total + nn(gall[n], weights_ref[rows[n], :])
        return total.astype(BF)

    blocks = (j, j1, j2, j3)
    rows = [pl.ds(pl.multiple_of(block * FULL, FULL), FULL) for block in blocks]

    def send_gathered(act, n):
        source, target, device, k = ((0, 2, across, 1), (0, 1, sibling, 0), (2, 3, sibling, 2))[n]
        remote(act, gall.at[source], gall.at[target], gs.at[k], gr.at[k], device)

    def send_queries(act):
        remote(act, qo, qb.at[1], qs.at[0], qr.at[0], partner)

    def attn_grad(weights_ref):
        total = nn(gall[0], weights_ref[rows[0], :])
        for k in range(1, 4):
            total = total + nn(gall[k], weights_ref[rows[k], :])
        return total.astype(BF)

    def send_attn_grad(act):
        remote(act, dop, dob.at[1], qs.at[1], qr.at[1], partner)

    def project(n):
        return nt(att[0], wm[rows[n], :]) + nt(attr[...], wo[rows[n], :])

    for copy in staged[0]:
        copy.wait()
    send_swap(START, 0)
    for copy in kept_tiles[0]:
        copy.wait()
    send_z(START, 0, 4)
    for copy in staged[1]:
        copy.wait()
    send_swap(START, 1)
    arrived(slot(0, 7), fr.at[0, 7])
    send_z(START, 0, 7)
    g_copy.wait()
    send_gathered(START, 0)
    send_own_x(START, 0)
    for copy in kept_tiles[1]:
        copy.wait()
    send_z(START, 1, 4)
    for copy in staged[2]:
        copy.wait()
    send_swap(START, 2)
    arrived(slot(1, 7), fr.at[1, 7])
    send_z(START, 1, 7)
    forward(START, 0, 0, 0)
    send_other_x(START, 0)
    forward(START, 0, 0, 1)
    forward(START, 0, 1, 0)
    qo_copy.wait()
    send_queries(START)
    send_other_x(START, 1)
    send_own_x(START, 1)
    arrived(gall.at[2], gr.at[1])
    send_gathered(START, 2)
    send_gathered(START, 1)
    forward(START, 0, 1, 1)
    pass_on(START, 0)
    arrived(slot(2, 7), fr.at[2, 7])
    send_z(START, 2, 7)
    forward(START, 1, 0, 0)
    for copy in w_copies:
        copy.wait()
    arrived(gall.at[1], gr.at[0])
    arrived(gall.at[3], gr.at[2])
    dop[...] = attn_grad(wo)
    send_attn_grad(START)
    dob[0] = attn_grad(wm)
    for copy in kept_tiles[2]:
        copy.wait()
    send_z(START, 2, 4)
    forward(START, 1, 1, 1)
    send_other_x(START, 2)
    send_own_x(START, 2)
    pass_on(START, 1)
    forward(START, 1, 0, 1)
    q_copy.wait()
    arrived(qb.at[1], qr.at[0])
    attend(0)
    forward(START, 1, 1, 0)
    arrived(dob.at[1], qr.at[1])
    differentiate(0, 0)
    differentiate(0, 1)
    forward(START, 2, 1, 1)
    forward(START, 2, 1, 0)
    forward(START, 2, 0, 0)
    attend(1)
    forward(START, 2, 0, 1)
    pass_back(START, 0)
    pass_on(START, 2)
    differentiate(1, 0)
    differentiate(1, 1)
    reduce_x(0)
    attend(2)
    pass_back(START, 1)
    differentiate(2, 0)
    differentiate(2, 1)
    reduce_x(1)
    for h in range(NH):
        arrived(attr.at[:, cols(h)], atr.at[h])
    ms[0] = project(3).astype(BF)
    ms[1] = project(1).astype(BF)
    remote(START, ms, mr, mss.at[0], msr.at[0], sibling)
    pass_back(START, 2)
    crossing_sum = project(2)
    arrived(mr, msr.at[0])
    ms2[...] = (crossing_sum + mr[0].astype(F32)).astype(BF)
    remote(START, ms2, mr2, mss.at[1], msr.at[1], across)
    kept = project(0) + mr[1].astype(F32)
    reduce_x(2)
    reduce_z(0)
    reduce_z(1)
    reduce_z(2)
    arrived(mr2, msr.at[1])
    mo[...] = (kept + mr2[...].astype(F32)).astype(BF)
    mixed_copy = local(mo, mixed, lsem.at[5])
    send_z(WAIT, 0, 4)
    send_z(WAIT, 0, 7)
    send_z(WAIT, 1, 4)
    send_z(WAIT, 1, 7)
    send_z(WAIT, 2, 4)
    send_z(WAIT, 2, 7)

    for n in range(3):
        send_gathered(WAIT, n)
    send_queries(WAIT)
    send_attn_grad(WAIT)
    remote(WAIT, ms, mr, mss.at[0], msr.at[0], sibling)
    remote(WAIT, ms2, mr2, mss.at[1], msr.at[1], across)
    for h in range(NH):
        for send in (
            send_swap, send_own_x, send_other_x, pass_on, pass_back, send_attended, send_query_grad, send_reduced,
            send_total,
        ):
            send(WAIT, h)
        for n in range(2):
            forward(WAIT, h, n, 0)
            forward(WAIT, h, n, 1)
            send_back(WAIT, h, n)
        arrived(dq_out.at[:, their_cols(h)], dqr.at[h])
        arrived(dk_out.at[:, their_cols(h)], byr.at[h, 0])
        arrived(dv_out.at[:, their_cols(h)], byr.at[h, 1])
    mixed_copy.wait()

def hand_over(*refs):
    sources, results, held, ins, outs = refs[:4], refs[4:8], refs[8], refs[9], refs[10]
    arriving = [pltpu.make_async_copy(sources[n], held.at[n], ins.at[n]) for n in range(4)]
    leaving = [pltpu.make_async_copy(held.at[n], results[n], outs.at[n]) for n in range(4)]
    for copy in arriving:
        copy.start()
    for n in range(4):
        arriving[n].wait()
        leaving[n].start()
    for copy in leaving:
        copy.wait()


def on_device(queries, keys, values, w_out, out_grad, tile_valid):
    dma = pltpu.SemaphoreType.DMA
    any_space = pl.BlockSpec(memory_space=pl.ANY)
    block = jax.ShapeDtypeStruct(queries.shape, BF)
    results = pl.pallas_call(
        kernel,
        out_shape=(block, block, block, block),
        in_specs=[any_space] * 5 + [pl.BlockSpec(memory_space=pltpu.SMEM)],
        out_specs=(any_space, any_space, any_space, any_space),
        scratch_shapes=[
            pltpu.VMEM((NH, 12 * T, 2 * HD), BF),
            pltpu.VMEM((NH, T, 2 * HD), BF),
            pltpu.VMEM((T, HALF), BF),
            pltpu.VMEM((2, T, HALF), BF),
            pltpu.VMEM((2, T, HALF), BF),
            pltpu.VMEM((T, HALF), BF),
            pltpu.VMEM((4, T, FULL), BF),
            pltpu.VMEM((4 * FULL, HALF), BF),
            pltpu.VMEM((4 * FULL, HALF), BF),
            pltpu.VMEM((2, T, HALF), BF),
            pltpu.VMEM((T, HALF), BF),
            pltpu.VMEM((2, T, HALF), BF),
            pltpu.VMEM((2, T, WIN), BF),
            pltpu.VMEM((2, T, HD), F32),
            pltpu.VMEM((2, 1, WIN), F32),
            pltpu.VMEM((NH, 2, SIDE, 2 * HD), BF),
            pltpu.VMEM((NH, 2, SIDE, 2 * HD), BF),
            pltpu.VMEM((NH, 2 * SIDE, 2 * HD), F32),
            pltpu.VMEM((NH, 2, 2 * T, 2 * HD), BF),
            pltpu.VMEM((NH, 2, 2 * T, 2 * HD), BF),
            pltpu.VMEM((NH, 2, T, 2 * HD), BF),
            pltpu.VMEM((2, T, FULL), BF),
            pltpu.VMEM((2, T, FULL), BF),
            pltpu.VMEM((T, FULL), BF),
            pltpu.VMEM((T, FULL), BF),
            pltpu.VMEM((T, FULL), BF),
            pltpu.VMEM((NH, T, 2 * HD), BF),
            pltpu.VMEM((NH, T, 2 * HD), BF),
            pltpu.VMEM((NH, T, 2 * HD), BF),
            dma((6,)),
            dma((NH, 4)),
            dma((NH, 14)),
            dma((NH, 12)),
            dma((NH, 2, 3)),
            dma((NH, 2, 3)),
            dma((NH, 2)),
            dma((NH, 2)),
            dma((NH, 2)),
            dma((NH, 2)),
            dma((3,)),
            dma((3,)),
            dma((2,)),
            dma((2,)),
            dma((NH,)),
            dma((NH,)),
            dma((NH,)),
            dma((NH,)),
            dma((2,)),
            dma((2,)),
            dma((NH, 4)),
            dma((NH, 2)),
            dma((NH, 2)),
            dma((NH,)),
        ],
        compiler_params=pltpu.CompilerParams(
            collective_id=0, has_side_effects=True, vmem_limit_bytes=56 * 1024 * 1024
        ),
    )(queries, keys, values, w_out, out_grad, tile_valid)
    return pl.pallas_call(
        hand_over,
        out_shape=(block, block, block, block),
        in_specs=[any_space] * 4,
        out_specs=(any_space, any_space, any_space, any_space),
        scratch_shapes=[pltpu.VMEM((4, *queries.shape), BF), dma((4,)), dma((4,))],
        compiler_params=pltpu.CompilerParams(vmem_limit_bytes=56 * 1024 * 1024),
    )(*results)


def solution(mesh):
    return jax.shard_map(
        on_device,
        mesh=mesh,
        in_specs=(
            P("tile", "head"),
            P("tile", "head"),
            P("tile", "head"),
            P(None, "head"),
            P("tile", "head"),
            P(),
        ),
        out_specs=(P("tile", "head"), P("tile", "head"), P("tile", "head"), P("tile", "head")),
        check_vma=False,
    )
```
